32 devices in a mesh: dp: 4 (over y, x), tile: 8 (over z, core).
Axes of the slice: x: 2, y: 2, z: 4, core: 2. Of those that a mesh axis runs over, the one named last changes fastest.
Arguments:
- features: bfloat16 [4, 128, 64, 256], P('dp', 'tile'), may hold values from -6 to 6
- fpn_weight: bfloat16 [9, 256, 256], replicated, may hold values from -0.125 to 0.125
- mask_w1: bfloat16 [9, 256, 256], replicated, may hold values from -0.125 to 0.125
- mask_w2: bfloat16 [9, 256, 256], replicated, may hold values from -0.125 to 0.125
- owner: int32 [4, 32, 1], P('dp', 'tile'), may hold values from 0 to 7; in each aligned block of 4 rows (0 to 3, 4 to 7, ..., all dimensions but the last counted through in order) at most 2 rows name the same one
- row_off: int32 [4, 32], P('dp', 'tile'), may hold values from 0 to 2
- col_off: int32 [4, 32], P('dp', 'tile'), may hold values from 0 to 50
- cotangent: bfloat16 [4, 32, 14, 14, 256], P('dp', 'tile'), may hold values from -6 to 6
Outputs:
- grad_w1: float32 [2304, 256], P('dp')
- grad_w2: float32 [2304, 256], P('dp')
- grad_pyramid: bfloat16 [4, 128, 64, 256], P('dp', 'tile')
The draws below stay inside these ranges and needn't reach their ends.
Inputs may be any that keep to these rules, and one draw needn't show every extreme that they name: `owner`: among the 4 regions of one device no tile is named more than 2 times.
All inputs are finite; a program needn't handle non-finite values.
Results may differ from the reference program's by a relative error of at most 0.017.
Values may be sent and summed in bfloat16 or wider, within the bound.
No kernel may reach another device: no remote copies, remote signals or barrier semaphores. Data moves between devices by JAX's collectives and lax.ppermute only.
A program may use at most 128 MiB of HBM per device.

```python
import math
import jax
import jax.numpy as jnp
import numpy as np
from jax import lax

C = 256
TH = 16
TW = 64
CROP = 14
REG = 4
CAP = 2
SCENES = 4
ROWS = 128
REGIONS = 32
N_TILE = 8


def set_ends(result, own_key, low, largest):
    longest = result.shape.index(max(result.shape))
    spots = []
    for shift in (0, 1):
        where = [jax.random.randint(jax.random.fold_in(own_key, axis), (), 0, length) for axis, length in enumerate(result.shape)]
        where[longest] = (where[longest] + shift) % result.shape[longest]
        spots.append(tuple(where))
    return result.at[spots[0]].set(low).at[spots[1]].set(largest)


def level_of(rng, shape, cuts, low, high):
    level = 1.0
    for axis_at, blocks in cuts:
        steps = jax.random.uniform(jax.random.fold_in(jax.random.fold_in(rng, 6), axis_at), (blocks,), jnp.float32, low / len(cuts), high / len(cuts))
        level = level * jnp.repeat(jnp.exp(steps), shape[axis_at] // blocks).reshape((-1,) + (1,) * (len(shape) - 1 - axis_at))
    return level


def routed_block(own_key, own, number, rows, count, top, bound, lean):
    order = jax.random.permutation(own_key, count)
    heavy_load, ordinary = load_shares(count, rows * top, bound, lean, True), load_shares(count, rows * top, bound, lean, False)
    places = jnp.arange(count)

    def named(tallies, rotation):
        used = int((tallies > 0).sum())
        fixed = max(1, used // 4)
        passed = fixed + (places - fixed + rotation * (used - fixed)) % max(1, count - fixed)
        return jnp.zeros((count,), jnp.int32).at[order[jnp.where(places < fixed, places, passed)]].set(jnp.asarray(tallies, jnp.int32))

    tallies = jnp.where(number % 4 == 0, named(heavy_load, number // 4), named(ordinary, number - number // 4 - 1))
    mixed = jax.random.permutation(jax.random.fold_in(own, 3), count)
    donor, receiver = mixed[0:count // 2 * 2:2], mixed[1:count // 2 * 2:2]
    slack = jnp.minimum(tallies[donor] - 1, bound - tallies[receiver]) // 2
    slack = jnp.where((donor == order[0]) | (receiver == order[0]) | (tallies[receiver] == 0), 0, jnp.maximum(slack, 0))
    passed = jax.random.randint(jax.random.fold_in(own, 4), (count // 2,), 0, 1 << 20) % (slack + 1)
    tallies = tallies.at[donor].add(-passed).at[receiver].add(passed)
    labels = jnp.searchsorted(jnp.cumsum(tallies), jnp.arange(rows * top), side="right").astype(jnp.int32)
    table = labels.reshape(top, rows).T
    table = table[jax.random.permutation(jax.random.fold_in(own, 1), rows)]
    rotation = jax.random.randint(jax.random.fold_in(own, 2), (rows, 1), 0, top)
    return jnp.take_along_axis(table, (jnp.arange(top)[None, :] + rotation) % top, axis=1)


def load_shares(count, total, most, lean, full):
    weights = [(1 << 20) // math.isqrt(standing ** lean) + 1 for standing in range(1, count + 1)]
    largest = most if full else min(most, max(-(-total // count), total * weights[0] // sum(weights)))
    least = 1 if total - largest >= count - 1 else 0
    holding, rest = [largest] + [least] * (count - 1), total - largest - least * (count - 1)
    while rest > 0:
        movable = [i for i in range(1, count) if holding[i] < largest] or [i for i in range(1, count) if holding[i] < most]
        pool, budget = sum([weights[i] for i in movable]), rest
        for i in movable:
            addition = min(most - holding[i], max(1, budget * weights[i] // pool), rest)
            holding[i] = holding[i] + addition
            rest = rest - addition
    return np.array(holding)


def scatter_about(own_key, dims, spread, bound, cuts=(), held_as=jnp.bfloat16):
    gain = level_of(own_key, dims, cuts, -0.22, 0.18) if cuts else 1.0
    values = jax.random.normal(own_key, dims, jnp.float32) * spread * gain
    return jnp.minimum(jnp.maximum(values, -bound), bound).astype(held_as)


def setup_inputs(seed: int = 0) -> dict:
    arg_keys = jax.random.split(jax.random.key(seed), 9)
    features = scatter_about(arg_keys[0], (SCENES, ROWS, TW, C), 1.0, 6.0, ((0, 4), (1, 8)))
    fpn_weight = scatter_about(arg_keys[1], (9, C, C), (9 * C) ** -0.5, 0.125)
    mask_w1 = scatter_about(arg_keys[2], (9, C, C), (9 * C) ** -0.5, 0.125)
    mask_w2 = scatter_about(arg_keys[3], (9, C, C), (9 * C) ** -0.5, 0.125)
    owner_keys = jax.random.split(jax.random.fold_in(arg_keys[4], 1), SCENES * REGIONS // REG)
    owner_turns = jax.random.permutation(jax.random.fold_in(arg_keys[4], 3), SCENES * REGIONS // REG)
    owner = jax.vmap(lambda own, number: routed_block(jax.random.fold_in(arg_keys[4], 2), own, number, REG, N_TILE, 1, CAP, 3))(owner_keys, owner_turns).reshape((SCENES, REGIONS, 1))
    row_off = set_ends(jax.random.randint(arg_keys[5], (SCENES, REGIONS), 0, TH - CROP + 1), jax.random.fold_in(arg_keys[5], 1), 0, TH - CROP).astype(jnp.int32)
    col_off = set_ends(jax.random.randint(arg_keys[6], (SCENES, REGIONS), 0, TW - CROP + 1), jax.random.fold_in(arg_keys[6], 1), 0, TW - CROP).astype(jnp.int32)
    cotangent = scatter_about(arg_keys[7], (SCENES, REGIONS, CROP, CROP, C), 1.0, 6.0, ((0, 4), (1, 8)))
    return {"features": features, "fpn_weight": fpn_weight, "mask_w1": mask_w1, "mask_w2": mask_w2, "owner": owner, "row_off": row_off, "col_off": col_off, "cotangent": cotangent}


def smooth(values):
    return jax.nn.gelu(values, approximate=True)

def conv_padded(padded, kernel):
    batch, rows, cols, channels = padded.shape
    height, width = (rows - 2, cols - 2)
    running = jnp.zeros((batch * height * width, kernel.shape[2]), jnp.float32)
    for row_tap in range(3):
        for col_tap in range(3):
            window = padded[:, row_tap:row_tap + height, col_tap:col_tap + width, :]
            running = running + jnp.dot(window.reshape(-1, channels), kernel[3 * row_tap + col_tap], preferred_element_type=jnp.float32)
    return running.reshape(batch, height, width, kernel.shape[2])

def conv_same(source, kernel):
    return conv_padded(jnp.pad(source, ((0, 0), (1, 1), (1, 1), (0, 0))), kernel)

def tap_grads(source, grads):
    batch, height, width, channels = source.shape
    padded = jnp.pad(source, ((0, 0), (1, 1), (1, 1), (0, 0)))
    flat_grads = grads.reshape(-1, grads.shape[3])
    pieces = []
    for row_tap in range(3):
        for col_tap in range(3):
            window = padded[:, row_tap:row_tap + height, col_tap:col_tap + width, :]
            pieces.append(jnp.dot(window.reshape(-1, channels).T, flat_grads, preferred_element_type=jnp.float32))
    return jnp.stack(pieces)

def conv_back(grads, kernel):
    batch, height, width, channels = grads.shape
    padded = jnp.pad(grads, ((0, 0), (1, 1), (1, 1), (0, 0)))
    running = jnp.zeros((batch * height * width, kernel.shape[1]), jnp.float32)
    for row_tap in range(3):
        for col_tap in range(3):
            window = padded[:, 2 - row_tap:2 - row_tap + height, 2 - col_tap:2 - col_tap + width, :]
            running = running + jnp.dot(window.reshape(-1, channels), kernel[3 * row_tap + col_tap].T, preferred_element_type=jnp.float32)
    return running.reshape(batch, height, width, kernel.shape[1])

def mask_head(crops, mask_w1, mask_w2, cotangent):
    pre1 = conv_same(crops, mask_w1)
    act1 = smooth(pre1).astype(jnp.bfloat16)
    pre2 = conv_same(act1, mask_w2)
    _, pull_two = jax.vjp(smooth, pre2)
    g2 = pull_two(cotangent.astype(jnp.float32))[0].astype(jnp.bfloat16)
    grad_two = tap_grads(act1, g2)
    gact1 = conv_back(g2, mask_w2)
    _, pull_one = jax.vjp(smooth, pre1)
    g1 = pull_one(gact1)[0].astype(jnp.bfloat16)
    grad_one = tap_grads(crops, g1)
    gcrop = conv_back(g1, mask_w1).astype(jnp.bfloat16)
    return (grad_one, grad_two, gcrop)

def reference(features, fpn_weight, mask_w1, mask_w2, owner, row_off, col_off, cotangent):

    def one_scene(carry, inputs):
        scene, owners, rows, cols, scene_cot = inputs
        padded = jnp.pad(scene[None], ((0, 0), (1, 1), (1, 1), (0, 0)))
        pyramid = conv_padded(padded, fpn_weight)[0].astype(jnp.bfloat16)
        starts = (owners[:, 0] * TH + rows).astype(jnp.int32)
        cols = cols.astype(jnp.int32)

        def cut(start, column):
            return lax.dynamic_slice(pyramid, (start, column, jnp.int32(0)), (CROP, CROP, C))
        crops = jax.vmap(cut)(starts, cols)
        grad_one, grad_two, gcrop = mask_head(crops, mask_w1, mask_w2, scene_cot)

        def place(running, item):
            start, column, grad_piece = item
            current = lax.dynamic_slice(running, (start, column, jnp.int32(0)), (CROP, CROP, C))
            updated = current + grad_piece.astype(jnp.float32)
            return (lax.dynamic_update_slice(running, updated, (start, column, jnp.int32(0))), None)
        placed, _ = lax.scan(place, jnp.zeros((ROWS, TW, C), jnp.float32), (starts, cols, gcrop))
        return ((carry[0] + grad_one, carry[1] + grad_two), placed.astype(jnp.bfloat16))
    start_grads = (jnp.zeros((9, C, C), jnp.float32), jnp.zeros((9, C, C), jnp.float32))
    sums, grad_pyramid = lax.scan(one_scene, start_grads, (features, owner, row_off, col_off, cotangent))
    return (sums[0].reshape(9 * C, C), sums[1].reshape(9 * C, C), grad_pyramid)
```

```python
import functools
import math

import jax
import jax.numpy as jnp
from jax import lax
from jax.experimental import pallas as pl
from jax.experimental.pallas import tpu as pltpu
from jax.sharding import PartitionSpec as P

BF = jnp.bfloat16
F32 = jnp.float32
VMEM_LIMIT = 56 * 1024 * 1024
PITCH = 16
SLOT = 208


def roundup(n, m):
    return (n + m - 1) // m * m


def call(kernel, outs, scratch=(), aliases=None):
    return pl.pallas_call(
        kernel,
        out_shape=outs,
        in_specs=None,
        scratch_shapes=list(scratch),
        input_output_aliases=aliases or {},
        compiler_params=pltpu.CompilerParams(vmem_limit_bytes=VMEM_LIMIT),
    )


def sds(shape, dtype):
    return jax.ShapeDtypeStruct(shape, dtype)


def pack_kernel(side, cot_ref, place_ref, out_ref, wide):
    regions = cot_ref.shape[0]
    lanes = lax.broadcasted_iota(jnp.int32, (16, 256), 1)
    rows = lax.broadcasted_iota(jnp.int32, (16, 256), 0)
    for r in range(regions):
        for i in range(side):
            wide[side * i : side * i + side, :] = cot_ref[r, i].astype(F32)
        tail = wide[192:208, :]
        spot = place_ref[r, 0].astype(F32)
        column = place_ref[r, 1].astype(F32)
        note = jnp.where(lanes == 0, spot, jnp.where(lanes == 1, column, 0.0))
        wide[192:208, :] = jnp.where(rows < 4, tail, note)
        out_ref[r] = wide[...].astype(BF)


def pack(cotangent, place):
    regions, side = cotangent.shape[0], cotangent.shape[1]
    return pl.pallas_call(
        functools.partial(pack_kernel, side),
        out_shape=sds((regions, SLOT, 256), BF),
        in_specs=[
            pl.BlockSpec(memory_space=pltpu.VMEM),
            pl.BlockSpec(memory_space=pltpu.SMEM),
        ],
        scratch_shapes=[pltpu.VMEM((SLOT, 256), F32)],
        compiler_params=pltpu.CompilerParams(vmem_limit_bytes=VMEM_LIMIT),
    )(cotangent, place)


def pyramid_part(height, width, own, other, rim_a, rim_b, wf, pyr, xp):
    core = lax.rem(lax.axis_index("tile"), 2)
    cells = height * width
    col = lax.broadcasted_iota(jnp.int32, (width, 256), 0)

    def fill(src, count, where):
        def step(t, carry):
            v = src[pl.ds(pl.multiple_of(t * width, width), width), :].astype(F32)
            to = pl.ds(pl.multiple_of(where + t * width, width), width)
            xp[to, 0:256] = jnp.where(col == 0, 0.0, pltpu.roll(v, 1, 0)).astype(BF)
            xp[to, 256:512] = v.astype(BF)
            xp[to, 512:768] = jnp.where(
                col == width - 1, 0.0, pltpu.roll(v, width - 1, 0)
            ).astype(BF)
            return carry

        lax.fori_loop(0, count, step, 0)

    bottom = width + 2 * cells
    fill(own, height, width + core * cells)
    fill(other, height, width + (1 - core) * cells)
    fill(rim_a, 1, core * bottom)
    fill(rim_b, 1, (1 - core) * bottom)

    def conv(t, carry):
        at = t * 256
        total = jnp.zeros((256, 256), F32)
        for a in range(3):
            piece = xp[pl.ds(pl.multiple_of(at + a * width, 64), 256), :]
            total += jnp.dot(piece, wf[a * 768 : a * 768 + 768, :], preferred_element_type=F32)
        pyr[pl.ds(pl.multiple_of(at, 256), 256), :] = total.astype(BF).astype(F32)
        return carry

    lax.fori_loop(0, 2 * cells // 256, conv, 0)
    pyr[2 * cells : 2 * cells + 16, :] = jnp.zeros((16, 256), F32)


def flip_part(w, wb):
    for k in range(9):
        block = w[(8 - k) * 256 : (9 - k) * 256, :].astype(F32)
        wb[k * 256 : k * 256 + 256, :] = block.T.astype(BF)


def gelu_pair(v):
    c = math.sqrt(2.0 / math.pi)
    sq = v * v
    t = jnp.tanh(c * (v + 0.044715 * (sq * v)))
    half = 0.5 * (1.0 + t)
    slope = half + 0.5 * v * (1.0 - t * t) * (c * (1.0 + 3 * 0.044715 * sq))
    return v * half, slope


def regions_part(side, height, width, blocks, pyr, w1, w2, wb1, wb2, acc1, acc2, gp, scratch):
    xs, hs, gs, wide, vs, slope1, todo = scratch
    cells = side * PITCH
    chip = lax.axis_index("tile") // 2
    lanes = lax.broadcasted_iota(jnp.int32, (16, 256), 1)
    rows16 = lax.broadcasted_iota(jnp.int32, (16, 256), 0)
    in_row = rows16 < side
    inside = lax.rem(lax.broadcasted_iota(jnp.int32, (cells, 256), 0), PITCH) < side
    per = blocks[0].shape[0]

    count = jnp.int32(0)
    for s, block in enumerate(blocks):
        for r in range(per):
            note = block[r, 192:208, :].astype(F32)
            note = jnp.where(rows16 == 15, note, 0.0)
            spot = jnp.sum(jnp.where(lanes == 0, note, 0.0)).astype(jnp.int32) - 1
            column = jnp.sum(jnp.where(lanes == 1, note, 0.0)).astype(jnp.int32)
            local = spot - chip * 2 * height
            here = (spot >= 0) & (local >= 0) & (local < 2 * height)
            todo[0, count] = jnp.int32(s * per + r)
            todo[1, count] = jnp.where(here, local * width + column // 8 * 8, 0)
            todo[2, count] = jnp.where(here, lax.rem(column, 8), 0)
            count = count + here.astype(jnp.int32)

    for buf in (xs, hs, gs):
        buf[0:16, :] = jnp.zeros((16, 768), BF)
        buf[cells + 16 : cells + 32, :] = jnp.zeros((16, 768), BF)

    def put(buf, v):
        buf[16 : 16 + cells, 0:256] = pltpu.roll(v, 1, 0).astype(BF)
        buf[16 : 16 + cells, 256:512] = v.astype(BF)
        buf[16 : 16 + cells, 512:768] = pltpu.roll(v, cells - 1, 0).astype(BF)

    def conv(buf, w):
        total = jnp.zeros((cells, 256), F32)
        for a in range(3):
            total += jnp.dot(
                buf[a * 16 : a * 16 + cells, :],
                w[a * 768 : a * 768 + 768, :],
                preferred_element_type=F32,
            )
        return total

    def taps(acc, buf, grad):
        turned = grad.T.astype(BF)
        for a in range(3):
            acc[:, a * 768 : a * 768 + 768] += jnp.dot(
                turned, buf[a * 16 : a * 16 + cells, :], preferred_element_type=F32
            )

    def region(n, carry):
        which = todo[0, n]
        base = pl.multiple_of(todo[1, n], 8)
        lead = todo[2, n]
        for s, block in enumerate(blocks):

            @pl.when(which // per == s)
            def _():
                wide[...] = block[lax.rem(which, per)].astype(F32)

        for i in range(side):
            got = pyr[pl.ds(pl.multiple_of(base + i * width, 8), 24), :]
            got = pltpu.roll(got, lax.rem(24 - lead, 24), 0)[0:16]
            vs[i * 16 : i * 16 + 16, :] = jnp.where(in_row, got, 0.0)
        put(xs, vs[...])
        pre1 = conv(xs, w1)
        act1, slope = gelu_pair(pre1)
        slope1[...] = slope
        put(hs, jnp.where(inside, act1, 0.0))
        pre2 = conv(hs, w2)
        _, slope = gelu_pair(pre2)
        for i in range(side):
            got = wide[i * side : i * side + 16, :]
            vs[i * 16 : i * 16 + 16, :] = jnp.where(in_row, got, 0.0)
        g2 = vs[...] * slope
        put(gs, g2)
        taps(acc2, hs, g2)
        gact1 = conv(gs, wb2)
        g1 = jnp.where(inside, gact1 * slope1[...], 0.0)
        put(gs, g1)
        taps(acc1, xs, g1)
        gcrop = jnp.where(inside, conv(gs, wb1), 0.0).astype(BF).astype(F32)
        vs[...] = gcrop
        for i in range(side):
            at = pl.ds(pl.multiple_of(base + i * width, 8), 24)
            piece = jnp.concatenate([vs[i * 16 : i * 16 + 16, :], jnp.zeros((8, 256), F32)])
            gp[at, :] = gp[at, :] + pltpu.roll(piece, lead, 0)
        return carry

    lax.fori_loop(0, count, region, 0)


def finish_part(height, width, acc1, acc2, gp, keep, send, gp_own, gp_other):
    core = lax.rem(lax.axis_index("tile"), 2)
    cells = height * width

    def write(acc, to):
        for k in range(9):
            to[k * 256 : k * 256 + 256, :] = acc[:, k * 256 : k * 256 + 256].T.astype(BF)

    @pl.when(core == 0)
    def _():
        write(acc1, keep)
        write(acc2, send)

    @pl.when(core == 1)
    def _():
        write(acc2, keep)
        write(acc1, send)

    gp_own[...] = gp[pl.ds(pl.multiple_of(core * cells, cells), cells), :]
    gp_other[...] = gp[pl.ds(pl.multiple_of((1 - core) * cells, cells), cells), :].astype(BF)


def main_call(side, height, width, first, last, state, weights, blocks):
    n = len(blocks)
    big = 2 * height * width + 16
    cells = side * PITCH
    kept = (
        sds((big, 256), F32),
        sds((2304, 256), BF),
        sds((2304, 256), BF),
    )
    sums = (sds((256, 2304), F32), sds((256, 2304), F32), sds((big, 256), F32))
    ends = (
        sds((2304, 256), BF),
        sds((2304, 256), BF),
        sds((height * width, 256), F32),
        sds((height * width, 256), BF),
    )
    outs = (kept if first and not last else ()) + (ends if last else sums)
    scratch = [
        pltpu.VMEM((cells + 32, 768), BF),
        pltpu.VMEM((cells + 32, 768), BF),
        pltpu.VMEM((cells + 32, 768), BF),
        pltpu.VMEM((SLOT, 256), F32),
        pltpu.VMEM((cells, 256), F32),
        pltpu.VMEM((cells, 256), F32),
        pltpu.SMEM((3, 128), jnp.int32),
    ]
    extra = []
    if first:
        extra.append(pltpu.VMEM(((2 * height + 2) * width, 768), BF))
    if first and last:
        extra += [pltpu.VMEM(s.shape, s.dtype) for s in kept]
    if last:
        extra += [pltpu.VMEM(s.shape, s.dtype) for s in sums]

    def kernel(*refs):
        refs = list(refs)

        def take(k):
            got = refs[:k]
            del refs[:k]
            return got

        state_refs = take(len(state))
        weight_refs = take(len(weights))
        block_refs = take(n)
        out_refs = take(len(outs))
        scratch_refs = take(len(scratch))
        if first:
            xp = take(1)[0]
            pyr, wb1, wb2 = take(3) if last else out_refs[:3]
            acc1, acc2, gp = take(3) if last else out_refs[3:]
            wf, w1, w2 = weight_refs
            pyramid_part(height, width, *state_refs, wf, pyr, xp)
            flip_part(w1, wb1)
            flip_part(w2, wb2)
            for total in (acc1, acc2, gp):
                total[...] = jnp.zeros(total.shape, F32)
        else:
            pyr, wb1, wb2 = state_refs[:3]
            acc1, acc2, gp = take(3) if last else out_refs
            w1, w2 = weight_refs
            for to, source in zip((acc1, acc2, gp), state_refs[3:]):
                to[...] = source[...]
        regions_part(
            side, height, width, block_refs, pyr, w1, w2, wb1, wb2, acc1, acc2, gp, scratch_refs
        )
        if last:
            finish_part(height, width, acc1, acc2, gp, *out_refs)

    aliases = {} if first or last else {3: 0, 4: 1, 5: 2}
    return pl.pallas_call(
        kernel,
        out_shape=outs,
        scratch_shapes=scratch + extra,
        input_output_aliases=aliases,
        compiler_params=pltpu.CompilerParams(vmem_limit_bytes=VMEM_LIMIT),
    )(*state, *weights, *blocks)


def local_kernel(fn, outs, *arrays):
    return pl.pallas_call(
        fn,
        out_shape=outs,
        compiler_params=pltpu.CompilerParams(vmem_limit_bytes=VMEM_LIMIT),
    )(*arrays)


def add(a, b):
    return (a.astype(F32) + b.astype(F32)).astype(BF)


def reduce_weights(keep, send, core_swap, dp, chips):
    rows = keep.shape[0] // dp
    bits = dp.bit_length() - 1
    low = roundup(rows // 2, 16)
    spans = ((0, low), (low, rows))
    orders = (list(range(bits)), list(reversed(range(bits))))
    got = lax.ppermute(send, "tile", core_swap)

    def split(members, order):
        bit = 1 << order[0]
        return [m for m in members if not m & bit], [m for m in members if m & bit]

    members = [list(range(dp)), list(range(dp))]
    shapes = []
    for half in range(2):
        size = spans[half][1] - spans[half][0]
        stay, go = split(members[half], orders[half])
        shapes += [sds((len(stay), size, 256), BF), sds((len(go), size, 256), BF)]

    def first(keep_ref, got_ref, *outs):
        me = lax.axis_index("dp")
        for half in range(2):
            lo, hi = spans[half]
            for out, group in zip(outs[2 * half : 2 * half + 2], split(members[half], orders[half])):
                for n, m in enumerate(group):
                    at = pl.ds(pl.multiple_of((me ^ m) * rows + lo, 16), hi - lo)
                    out[n] = add(keep_ref[at, :], got_ref[at, :])

    parts = local_kernel(first, tuple(shapes), keep, got)
    for stage in range(bits):
        received = []
        for half in range(2):
            bit = 1 << orders[half][stage]
            received.append(lax.ppermute(parts[2 * half + 1], "dp", [(i, i ^ bit) for i in range(dp)]))
        for half in range(2):
            members[half] = split(members[half], orders[half][stage:])[0]
        if stage == bits - 1:
            break
        shapes = []
        for half in range(2):
            size = spans[half][1] - spans[half][0]
            stay, go = split(members[half], orders[half][stage + 1 :])
            shapes += [sds((len(stay), size, 256), BF), sds((len(go), size, 256), BF)]

        def middle(p, pr, q, qr, *outs, stage=stage):
            for half, (mine, theirs) in enumerate(((p, pr), (q, qr))):
                groups = split(members[half], orders[half][stage + 1 :])
                for out, group in zip(outs[2 * half : 2 * half + 2], groups):
                    for n, m in enumerate(group):
                        k = members[half].index(m)
                        out[n] = add(mine[k], theirs[k])

        parts = local_kernel(middle, tuple(shapes), parts[0], received[0], parts[2], received[1])

    share = roundup(-(-rows // chips), 16)
    shifts = [
        [(2 * z + c, 2 * ((z + k) % chips) + c) for z in range(chips) for c in range(2)]
        for k in range(chips)
    ]

    def deal(p, pr, q, qr, *refs):
        outs, total = refs[:chips], refs[chips]
        chip = lax.axis_index("tile") // 2
        total[0:low, :] = add(p[0], pr[0])
        total[low:rows, :] = add(q[0], qr[0])
        if share * chips > rows:
            total[rows:, :] = jnp.zeros((share * chips - rows, 256), BF)
        for k in range(chips):
            to = lax.rem(chip + k, chips)
            outs[k][...] = total[pl.ds(pl.multiple_of(to * share, 16), share), :]

    dealt = pl.pallas_call(
        deal,
        out_shape=tuple(sds((share, 256), BF) for _ in range(chips)),
        scratch_shapes=[pltpu.VMEM((share * chips, 256), BF)],
        compiler_params=pltpu.CompilerParams(vmem_limit_bytes=VMEM_LIMIT),
    )(parts[0], received[0], parts[2], received[1])
    arrived = [lax.ppermute(dealt[k], "tile", shifts[k]) for k in range(1, chips)]

    def gather(*refs):
        total = refs[0][...].astype(F32)
        for ref in refs[1:-1]:
            total += ref[...].astype(F32)
        refs[-1][...] = total.astype(BF)

    mine = local_kernel(gather, sds((share, 256), BF), dealt[0], *arrived)
    pieces = [mine] + [lax.ppermute(mine, "tile", shifts[k]) for k in range(1, chips)]

    def lay(*refs):
        chip = lax.axis_index("tile") // 2
        for k in range(chips):
            source = lax.rem(chip - k + chips, chips)
            refs[-1][pl.ds(pl.multiple_of(source * share, 16), share), :] = refs[k][...]

    whole = local_kernel(lay, sds((share * chips, 256), BF), *pieces)
    theirs = lax.ppermute(whole, "tile", core_swap)

    def out(mine_ref, theirs_ref, one, two):
        core = lax.rem(lax.axis_index("tile"), 2)

        @pl.when(core == 0)
        def _():
            one[...] = mine_ref[0:rows, :].astype(F32)
            two[...] = theirs_ref[0:rows, :].astype(F32)

        @pl.when(core == 1)
        def _():
            one[...] = theirs_ref[0:rows, :].astype(F32)
            two[...] = mine_ref[0:rows, :].astype(F32)

    return local_kernel(out, (sds((rows, 256), F32), sds((rows, 256), F32)), whole, theirs)


def body(features, fpn_weight, mask_w1, mask_w2, owner, row_off, col_off, cotangent):
    tiles = lax.axis_size("tile")
    dp = lax.axis_size("dp")
    chips = tiles // 2
    core = lax.rem(lax.axis_index("tile"), 2)
    height, width, channels = features.shape[1:]
    side = cotangent.shape[2]
    swap = [(i, i ^ 1) for i in range(tiles)]

    place = jnp.stack([owner[0, :, 0] * height + row_off[0] + 1, col_off[0]], axis=1)
    packed = pack(cotangent[0], place)

    tile = features.reshape(height * width, channels)
    edge = jnp.where(core == 1, tile[(height - 1) * width :], tile[:width])
    rim_a = lax.ppermute(
        edge, "tile", [(i, i + 1 if i % 2 else i - 1) for i in range(1, tiles - 1)]
    )
    rim_b = lax.ppermute(
        edge,
        "tile",
        [(i, i + 2 if i % 2 else i - 2) for i in range(tiles) if 0 <= (i + 2 if i % 2 else i - 2) < tiles],
    )
    other = lax.ppermute(tile, "tile", swap)

    up = [(i, i + 2) for i in range(tiles - 2)]
    down = [(i + 2, i) for i in range(tiles - 2)]
    blocks = [packed]
    rising, falling = packed, packed
    for _ in range(chips - 1):
        rising = lax.ppermute(rising, "tile", up)
        falling = lax.ppermute(falling, "tile", down)
        blocks += [rising, falling]

    flat = lambda w: w.reshape(9 * channels, channels)
    weights = [flat(fpn_weight), flat(mask_w1), flat(mask_w2)]
    keep, send, gp_own, gp_other = main_call(
        side, height, width, True, True, [tile, other, rim_a, rim_b], weights, blocks
    )
    gp_got = lax.ppermute(gp_other, "tile", swap)
    grad_one, grad_two = reduce_weights(keep, send, swap, dp, chips)

    def join(a, b, out):
        out[...] = (a[...] + b[...].astype(F32)).astype(BF)

    grad_pyramid = local_kernel(join, sds((height * width, channels), BF), gp_own, gp_got)
    return grad_one, grad_two, grad_pyramid.reshape(1, height, width, channels)


def solution(mesh):
    placed = (
        P("dp", "tile", None, None),
        P(),
        P(),
        P(),
        P("dp", "tile", None),
        P("dp", "tile"),
        P("dp", "tile"),
        P("dp", "tile", None, None, None),
    )
    return jax.shard_map(
        body,
        mesh=mesh,
        in_specs=placed,
        out_specs=(P("dp", None), P("dp", None), P("dp", "tile", None, None)),
        check_vma=False,
    )
```

```python
import functools
import math

import jax
import jax.numpy as jnp
from jax import lax
from jax.experimental import pallas as pl
from jax.experimental.pallas import tpu as pltpu
from jax.sharding import PartitionSpec as P

BF = jnp.bfloat16
F32 = jnp.float32
VMEM_LIMIT = 24 * 1024 * 1024
PITCH = 16
SLOT = 208


def roundup(n, m):
    return (n + m - 1) // m * m


def run(kernel, outs, args, scratch=(), aliases=None, smem=(), hbm_out=()):
    args = [
        x if i in smem else pltpu.with_memory_space_constraint(x, pltpu.VMEM)
        for i, x in enumerate(args)
    ]
    return pl.pallas_call(
        kernel,
        out_shape=tuple(
            s if i in hbm_out else pltpu.VMEM(s.shape, s.dtype) for i, s in enumerate(outs)
        ),
        in_specs=[
            pl.BlockSpec(memory_space=pltpu.SMEM if i in smem else pltpu.VMEM)
            for i in range(len(args))
        ],
        out_specs=tuple(pl.BlockSpec(memory_space=pltpu.VMEM) for _ in outs),
        scratch_shapes=list(scratch),
        input_output_aliases=aliases or {},
        compiler_params=pltpu.CompilerParams(vmem_limit_bytes=VMEM_LIMIT),
    )(*args)


def sds(shape, dtype):
    return jax.ShapeDtypeStruct(shape, dtype)


def pack_kernel(side, height, cot_ref, owner_ref, row_ref, col_ref, out_ref, wide):
    regions = cot_ref.shape[0]
    lanes = lax.broadcasted_iota(jnp.int32, (16, 256), 1)
    rows = lax.broadcasted_iota(jnp.int32, (16, 256), 0)
    for r in range(regions):
        for i in range(side):
            wide[side * i : side * i + side, :] = cot_ref[r, i].astype(F32)
        tail = wide[192:208, :]
        spot = (owner_ref[0, r, 0] * height + row_ref[0, r] + 1).astype(F32)
        column = col_ref[0, r].astype(F32)
        note = jnp.where(lanes == 0, spot, jnp.where(lanes == 1, column, 0.0))
        wide[192:208, :] = jnp.where(rows < 4, tail, note)
        out_ref[r] = wide[...].astype(BF)


def pack(cotangent, height, place):
    regions, side = cotangent.shape[0], cotangent.shape[1]
    return run(
        functools.partial(pack_kernel, side, height),
        (sds((regions, SLOT, 256), BF),),
        (cotangent, *place),
        scratch=[pltpu.VMEM((SLOT, 256), F32)],
        smem=(1, 2, 3),
    )[0]


def pyramid_part(height, width, own, other, rim_a, rim_b, wf, pyr, xp):
    core = lax.rem(lax.axis_index("tile"), 2)
    cells = height * width
    col = lax.broadcasted_iota(jnp.int32, (width, 256), 0)

    def fill(src, count, where):
        def step(t, carry):
            v = src[pl.ds(pl.multiple_of(t * width, width), width), :].astype(F32)
            to = pl.ds(pl.multiple_of(where + t * width, width), width)
            xp[to, 0:256] = jnp.where(col == 0, 0.0, pltpu.roll(v, 1, 0)).astype(BF)
            xp[to, 256:512] = v.astype(BF)
            xp[to, 512:768] = jnp.where(
                col == width - 1, 0.0, pltpu.roll(v, width - 1, 0)
            ).astype(BF)
            return carry

        lax.fori_loop(0, count, step, 0)

    bottom = width + 2 * cells
    fill(own, height, width + core * cells)
    fill(other, height, width + (1 - core) * cells)
    fill(rim_a, 1, core * bottom)
    fill(rim_b, 1, (1 - core) * bottom)

    def conv(t, carry):
        at = t * 256
        total = jnp.zeros((256, 256), F32)
        for a in range(3):
            piece = xp[pl.ds(pl.multiple_of(at + a * width, 64), 256), :]
            total += jnp.dot(piece, wf[a * 768 : a * 768 + 768, :], preferred_element_type=F32)
        pyr[pl.ds(pl.multiple_of(at, 256), 256), :] = total.astype(BF).astype(F32)
        return carry

    lax.fori_loop(0, 2 * cells // 256, conv, 0)
    pyr[2 * cells : 2 * cells + 16, :] = jnp.zeros((16, 256), F32)


def flip_part(w, wb):
    for k in range(9):
        block = w[(8 - k) * 256 : (9 - k) * 256, :].astype(F32)
        wb[k * 256 : k * 256 + 256, :] = block.T.astype(BF)


def gelu_pair(v):
    c = math.sqrt(2.0 / math.pi)
    sq = v * v
    t = jnp.tanh(c * (v + 0.044715 * (sq * v)))
    half = 0.5 * (1.0 + t)
    slope = half + 0.5 * v * (1.0 - t * t) * (c * (1.0 + 3 * 0.044715 * sq))
    return v * half, slope


def regions_part(side, height, width, blocks, pyr, w1, w2, wb1, wb2, acc1, acc2, gp, scratch):
    xs, hs, gs, wide, vs, slope1, todo = scratch
    chip = lax.axis_index("tile") // 2
    lanes = lax.broadcasted_iota(jnp.int32, (16, 256), 1)
    rows16 = lax.broadcasted_iota(jnp.int32, (16, 256), 0)
    in_row = rows16 < side
    per = blocks[0].shape[0]

    count = jnp.int32(0)
    for s, block in enumerate(blocks):
        for r in range(per):
            note = block[r, 192:208, :].astype(F32)
            note = jnp.where(rows16 == 15, note, 0.0)
            spot = jnp.sum(jnp.where(lanes == 0, note, 0.0)).astype(jnp.int32) - 1
            column = jnp.sum(jnp.where(lanes == 1, note, 0.0)).astype(jnp.int32)
            local = spot - chip * 2 * height
            here = (spot >= 0) & (local >= 0) & (local < 2 * height)
            todo[0, count] = jnp.int32(s * per + r)
            todo[1, count] = jnp.where(here, local * width + column // 8 * 8, 0)
            todo[2, count] = jnp.where(here, lax.rem(column, 8), 0)
            count = count + here.astype(jnp.int32)

    def batch(size, start):
        cells = (size * (side + 1) - 1) * PITCH
        spot = lax.broadcasted_iota(jnp.int32, (cells, 256), 0)
        inside = (lax.rem(spot, PITCH) < side) & (lax.rem(spot // PITCH, side + 1) < side)
        used = pl.ds(16, cells)

        def put(buf, v):
            buf[used, 0:256] = pltpu.roll(v, 1, 0).astype(BF)
            buf[used, 256:512] = v.astype(BF)
            buf[used, 512:768] = pltpu.roll(v, cells - 1, 0).astype(BF)

        def conv(buf, w):
            total = jnp.zeros((cells, 256), F32)
            for a in range(3):
                total += jnp.dot(
                    buf[a * 16 : a * 16 + cells, :],
                    w[a * 768 : a * 768 + 768, :],
                    preferred_element_type=F32,
                )
            return total

        def taps(acc, buf, grad):
            turned = grad.T.astype(BF)
            for a in range(3):
                acc[:, a * 768 : a * 768 + 768] += jnp.dot(
                    turned, buf[a * 16 : a * 16 + cells, :], preferred_element_type=F32
                )

        for buf in (xs, hs, gs):
            buf[0:16, :] = jnp.zeros((16, 768), BF)
            buf[cells + 16 : cells + 32, :] = jnp.zeros((16, 768), BF)
        for n in range(size - 1):
            gap = ((n + 1) * (side + 1) - 1) * PITCH
            vs[gap : gap + PITCH, :] = jnp.zeros((PITCH, 256), F32)
        bases, leads = [], []
        for n in range(size):
            which = todo[0, start + n]
            bases.append(pl.multiple_of(todo[1, start + n], 8))
            leads.append(todo[2, start + n])
            for s, block in enumerate(blocks):

                @pl.when(which // per == s)
                def _(block=block, n=n, which=which):
                    wide[n] = block[lax.rem(which, per)].astype(F32)

        for n in range(size):
            for i in range(side):
                got = pyr[pl.ds(pl.multiple_of(bases[n] + i * width, 8), 24), :]
                got = pltpu.roll(got, lax.rem(24 - leads[n], 24), 0)[0:16]
                at = (n * (side + 1) + i) * PITCH
                vs[at : at + 16, :] = jnp.where(in_row, got, 0.0)
        put(xs, vs[0:cells, :])
        act1, slope = gelu_pair(conv(xs, w1))
        slope1[0:cells, :] = slope
        put(hs, jnp.where(inside, act1, 0.0))
        _, slope = gelu_pair(conv(hs, w2))
        for n in range(size):
            for i in range(side):
                got = wide[n, i * side : i * side + 16, :]
                at = (n * (side + 1) + i) * PITCH
                vs[at : at + 16, :] = jnp.where(in_row, got, 0.0)
        g2 = vs[0:cells, :] * slope
        put(gs, g2)
        taps(acc2, hs, g2)
        gact1 = conv(gs, wb2)
        g1 = jnp.where(inside, gact1 * slope1[0:cells, :], 0.0)
        put(gs, g1)
        taps(acc1, xs, g1)
        vs[0:cells, :] = jnp.where(inside, conv(gs, wb1), 0.0).astype(BF).astype(F32)
        for n in range(size):
            for i in range(side):
                at = pl.ds(pl.multiple_of(bases[n] + i * width, 8), 24)
                row = (n * (side + 1) + i) * PITCH
                piece = jnp.concatenate([vs[row : row + 16, :], jnp.zeros((8, 256), F32)])
                gp[at, :] = gp[at, :] + pltpu.roll(piece, leads[n], 0)

    def pair(n, carry):
        batch(2, 2 * n)
        return carry

    lax.fori_loop(0, count // 2, pair, 0)

    @pl.when(lax.rem(count, 2) == 1)
    def _():
        batch(1, count - 1)


def finish_part(height, width, acc1, acc2, gp, keep, send, gp_own, gp_other):
    core = lax.rem(lax.axis_index("tile"), 2)
    cells = height * width

    def write(acc, to):
        for k in range(9):
            to[k * 256 : k * 256 + 256, :] = acc[:, k * 256 : k * 256 + 256].T.astype(BF)

    @pl.when(core == 0)
    def _():
        write(acc1, keep)
        write(acc2, send)

    @pl.when(core == 1)
    def _():
        write(acc2, keep)
        write(acc1, send)

    gp_own[...] = gp[pl.ds(pl.multiple_of(core * cells, cells), cells), :]
    gp_other[...] = gp[pl.ds(pl.multiple_of((1 - core) * cells, cells), cells), :].astype(BF)


def main_call(side, height, width, first, last, state, weights, blocks):
    n = len(blocks)
    big = 2 * height * width + 16
    cells = (2 * side + 1) * PITCH
    kept = (
        sds((big, 256), F32),
        sds((2304, 256), BF),
        sds((2304, 256), BF),
    )
    sums = (sds((256, 2304), F32), sds((256, 2304), F32), sds((big, 256), F32))
    ends = (
        sds((2304, 256), BF),
        sds((2304, 256), BF),
        sds((height * width, 256), F32),
        sds((height * width, 256), BF),
    )
    outs = (kept if first else ()) + sums + (ends if last else ())
    scratch = [
        pltpu.VMEM((cells + 32, 768), BF),
        pltpu.VMEM((cells + 32, 768), BF),
        pltpu.VMEM((cells + 32, 768), BF),
        pltpu.VMEM((2, SLOT, 256), F32),
        pltpu.VMEM((cells, 256), F32),
        pltpu.VMEM((cells, 256), F32),
        pltpu.SMEM((3, 128), jnp.int32),
    ]
    extra = [pltpu.VMEM(((2 * height + 2) * width, 768), BF)] if first else []

    def kernel(*refs):
        refs = list(refs)

        def take(k):
            got = refs[:k]
            del refs[:k]
            return got

        state_refs = take(len(state))
        weight_refs = take(len(weights))
        block_refs = take(n)
        out_refs = take(len(outs))
        scratch_refs = take(len(scratch))
        if first:
            pyr, wb1, wb2 = out_refs[:3]
            acc1, acc2, gp = out_refs[3:6]
            wf, w1, w2 = weight_refs
            pyramid_part(height, width, *state_refs, wf, pyr, refs[0])
            flip_part(w1, wb1)
            flip_part(w2, wb2)
            for total in (acc1, acc2, gp):
                total[...] = jnp.zeros(total.shape, F32)
        else:
            pyr, wb1, wb2 = state_refs[:3]
            acc1, acc2, gp = out_refs[:3]
            w1, w2 = weight_refs
        if n:
            regions_part(
                side, height, width, block_refs, pyr, w1, w2, wb1, wb2, acc1, acc2, gp, scratch_refs
            )
        if last:
            finish_part(height, width, acc1, acc2, gp, *out_refs[-4:])

    aliases = {} if first else {3: 0, 4: 1, 5: 2}
    return run(kernel, outs, [*state, *weights, *blocks], scratch=scratch + extra, aliases=aliases)


def local_kernel(fn, outs, *arrays, **more):
    if isinstance(outs, tuple):
        return run(fn, outs, arrays, **more)
    return run(fn, (outs,), arrays, **more)[0]


def add(a, b):
    return (a.astype(F32) + b.astype(F32)).astype(BF)


def reduce_weights(keep, send, core_swap, dp, chips, beside):
    rows = keep.shape[0] // dp
    bits = dp.bit_length() - 1
    low = roundup(rows // 2, 16)
    spans = ((0, low), (low, rows))
    orders = (list(range(bits)), list(reversed(range(bits))))
    got = lax.ppermute(send, "tile", core_swap)

    def split(members, order):
        bit = 1 << order[0]
        return [m for m in members if not m & bit], [m for m in members if m & bit]

    members = [list(range(dp)), list(range(dp))]
    shapes = []
    for half in range(2):
        size = spans[half][1] - spans[half][0]
        stay, go = split(members[half], orders[half])
        shapes += [sds((len(stay), size, 256), BF), sds((len(go), size, 256), BF)]

    def first(keep_ref, got_ref, *outs):
        me = lax.axis_index("dp")
        for half in range(2):
            lo, hi = spans[half]
            for out, group in zip(outs[2 * half : 2 * half + 2], split(members[half], orders[half])):
                for n, m in enumerate(group):
                    at = pl.ds(pl.multiple_of((me ^ m) * rows + lo, 16), hi - lo)
                    out[n] = add(keep_ref[at, :], got_ref[at, :])

    parts = local_kernel(first, tuple(shapes), keep, got)
    for stage in range(bits):
        received = []
        for half in range(2):
            bit = 1 << orders[half][stage]
            received.append(lax.ppermute(parts[2 * half + 1], "dp", [(i, i ^ bit) for i in range(dp)]))
        if stage == 0:
            received[0], beside = lax.optimization_barrier((received[0], beside))
        for half in range(2):
            members[half] = split(members[half], orders[half][stage:])[0]
        if stage == bits - 1:
            break
        shapes = []
        for half in range(2):
            size = spans[half][1] - spans[half][0]
            stay, go = split(members[half], orders[half][stage + 1 :])
            shapes += [sds((len(stay), size, 256), BF), sds((len(go), size, 256), BF)]

        def middle(p, pr, q, qr, *outs, stage=stage):
            for half, (mine, theirs) in enumerate(((p, pr), (q, qr))):
                groups = split(members[half], orders[half][stage + 1 :])
                for out, group in zip(outs[2 * half : 2 * half + 2], groups):
                    for n, m in enumerate(group):
                        k = members[half].index(m)
                        out[n] = add(mine[k], theirs[k])

        parts = local_kernel(middle, tuple(shapes), parts[0], received[0], parts[2], received[1])

    share = roundup(-(-rows // chips), 16)
    shifts = [
        [(2 * z + c, 2 * ((z + k) % chips) + c) for z in range(chips) for c in range(2)]
        for k in range(chips)
    ]

    def deal(p, pr, q, qr, *refs):
        outs, total = refs[:chips], refs[chips]
        chip = lax.axis_index("tile") // 2
        total[0:low, :] = add(p[0], pr[0])
        total[low:rows, :] = add(q[0], qr[0])
        if share * chips > rows:
            total[rows:, :] = jnp.zeros((share * chips - rows, 256), BF)
        for k in range(chips):
            to = lax.rem(chip + k, chips)
            outs[k][...] = total[pl.ds(pl.multiple_of(to * share, 16), share), :]

    dealt = local_kernel(
        deal,
        tuple(sds((share, 256), BF) for _ in range(chips)),
        *(parts[0], received[0], parts[2], received[1]),
        scratch=[pltpu.VMEM((share * chips, 256), BF)],
    )
    arrived = [lax.ppermute(dealt[k], "tile", shifts[k]) for k in range(1, chips)]

    def gather(*refs):
        total = refs[0][...].astype(F32)
        for ref in refs[1:-1]:
            total += ref[...].astype(F32)
        refs[-1][...] = total.astype(BF)

    mine = local_kernel(gather, sds((share, 256), BF), dealt[0], *arrived)
    pieces = [mine] + [lax.ppermute(mine, "tile", shifts[k]) for k in range(1, chips)]

    def lay(*refs):
        chip = lax.axis_index("tile") // 2
        for k in range(chips):
            source = lax.rem(chip - k + chips, chips)
            refs[-1][pl.ds(pl.multiple_of(source * share, 16), share), :] = refs[k][...]

    whole = local_kernel(lay, sds((share * chips, 256), BF), *pieces)
    theirs = lax.ppermute(whole, "tile", core_swap)

    def out(mine_ref, theirs_ref, one, two):
        core = lax.rem(lax.axis_index("tile"), 2)

        @pl.when(core == 0)
        def _():
            one[...] = mine_ref[0:rows, :].astype(F32)
            two[...] = theirs_ref[0:rows, :].astype(F32)

        @pl.when(core == 1)
        def _():
            one[...] = theirs_ref[0:rows, :].astype(F32)
            two[...] = mine_ref[0:rows, :].astype(F32)

    one, two = local_kernel(
        out, (sds((rows, 256), F32), sds((rows, 256), F32)), whole, theirs, hbm_out=(0, 1)
    )
    return one, two, beside


def body(features, fpn_weight, mask_w1, mask_w2, owner, row_off, col_off, cotangent):
    tiles = lax.axis_size("tile")
    dp = lax.axis_size("dp")
    chips = tiles // 2
    core = lax.rem(lax.axis_index("tile"), 2)
    height, width, channels = features.shape[1:]
    side = cotangent.shape[2]
    swap = [(i, i ^ 1) for i in range(tiles)]

    packed = pack(cotangent[0], height, (owner, row_off, col_off))

    tile = features.reshape(height * width, channels)
    edge = jnp.where(core == 1, tile[(height - 1) * width :], tile[:width])
    rim_a = lax.ppermute(
        edge, "tile", [(i, i + 1 if i % 2 else i - 1) for i in range(1, tiles - 1)]
    )
    rim_b = lax.ppermute(
        edge,
        "tile",
        [(i, i + 2 if i % 2 else i - 2) for i in range(tiles) if 0 <= (i + 2 if i % 2 else i - 2) < tiles],
    )
    other = lax.ppermute(tile, "tile", swap)

    up = [(i, i + 2) for i in range(tiles - 2)]
    down = [(i + 2, i) for i in range(tiles - 2)]
    flat = lambda w: w.reshape(9 * channels, channels)
    wf, w1, w2 = flat(fpn_weight), flat(mask_w1), flat(mask_w2)
    blocks = [lax.ppermute(packed, "tile", up), lax.ppermute(packed, "tile", down)]
    start = main_call(
        side, height, width, True, False, [tile, other, rim_a, rim_b], [wf, w1, w2], []
    )
    kept, sums = list(start[:3]), list(start[3:])
    for step in range(1, chips):
        last = step == chips - 1
        held = blocks
        if not last:
            held[0], held[1], kept[0] = lax.optimization_barrier((held[0], held[1], kept[0]))
            blocks = [lax.ppermute(held[0], "tile", up), lax.ppermute(held[1], "tile", down)]
        got = main_call(
            side,
            height,
            width,
            False,
            last,
            [*kept, *sums],
            [w1, w2],
            ([packed] if step == 1 else []) + held,
        )
        sums, ends = list(got[:3]), got[3:]
        if not last:
            kept[0], sums[0] = lax.optimization_barrier((kept[0], sums[0]))
    keep, send, gp_own, gp_other = ends
    gp_got = lax.ppermute(gp_other, "tile", swap)

    def join(a, b, out):
        out[...] = (a[...] + b[...].astype(F32)).astype(BF)

    joined = local_kernel(
        join, sds((height * width, channels), BF), gp_own, gp_got, hbm_out=(0,)
    )
    grad_one, grad_two, grad_pyramid = reduce_weights(keep, send, swap, dp, chips, joined)
    return grad_one, grad_two, grad_pyramid.reshape(1, height, width, channels)


def solution(mesh):
    placed = (
        P("dp", "tile", None, None),
        P(),
        P(),
        P(),
        P("dp", "tile", None),
        P("dp", "tile"),
        P("dp", "tile"),
        P("dp", "tile", None, None, None),
    )
    return jax.shard_map(
        body,
        mesh=mesh,
        in_specs=placed,
        out_specs=(P("dp", None), P("dp", None), P("dp", "tile", None, None)),
        check_vma=False,
    )
```

```python
import functools
import math

import jax
import jax.numpy as jnp
from jax import lax
from jax.experimental import pallas as pl
from jax.experimental.pallas import tpu as pltpu
from jax.sharding import PartitionSpec as P

BF = jnp.bfloat16
F32 = jnp.float32
VMEM_LIMIT = 24 * 1024 * 1024
PITCH = 16
SLOT = 208


def roundup(n, m):
    return (n + m - 1) // m * m


def run(kernel, outs, args, scratch=(), aliases=None, hbm=(), hbm_out=()):
    args = [
        pltpu.with_memory_space_constraint(x, pltpu.HBM if i in hbm else pltpu.VMEM)
        for i, x in enumerate(args)
    ]
    return pl.pallas_call(
        kernel,
        out_shape=tuple(
            s if i in hbm_out else pltpu.VMEM(s.shape, s.dtype) for i, s in enumerate(outs)
        ),
        in_specs=[
            pl.BlockSpec(memory_space=pltpu.HBM if i in hbm else pltpu.VMEM)
            for i in range(len(args))
        ],
        out_specs=tuple(pl.BlockSpec(memory_space=pltpu.VMEM) for _ in outs),
        scratch_shapes=list(scratch),
        input_output_aliases=aliases or {},
        compiler_params=pltpu.CompilerParams(vmem_limit_bytes=VMEM_LIMIT),
    )(*args)


def sds(shape, dtype):
    return jax.ShapeDtypeStruct(shape, dtype)


def edge_of(tile, height, width):
    def kernel(tile, edge, sem):
        core = lax.rem(lax.axis_index("tile"), 2)
        line = pl.ds(pl.multiple_of(core * (height - 1) * width, width), width)
        copy = pltpu.make_async_copy(tile.at[line, :], edge, sem)
        copy.start()
        copy.wait()

    return local_kernel(
        kernel, sds((width, 256), BF), tile, scratch=[pltpu.SemaphoreType.DMA], hbm=(0,)
    )


def pack_kernel(side, height, cot, owner, row, col, packed, low, high, wide, places, sems):
    regions = cot.shape[2]
    copies = [
        pltpu.make_async_copy(source, places.at[n], sems.at[n])
        for n, source in enumerate((owner, row, col))
    ]
    for copy in copies:
        copy.start()
    for i in range(side):
        for j in range(side):
            at = (i * side + j) * regions
            cell = cot[i, j].astype(F32)
            low[at : at + regions, :] = cell[:, 0:128]
            high[at : at + regions, :] = cell[:, 128:256]
    for copy in copies:
        copy.wait()
    lanes = lax.broadcasted_iota(jnp.int32, (16, 256), 1)
    rows = lax.broadcasted_iota(jnp.int32, (16, 256), 0)
    cells = side * side
    for r in range(regions):
        wide[0:cells, 0:128] = low[pl.ds(r, cells, stride=regions), :]
        wide[0:cells, 128:256] = high[pl.ds(r, cells, stride=regions), :]
        spot = (places[0, 0, r] * height + places[1, 0, r] + 1).astype(F32)
        column = places[2, 0, r].astype(F32)
        note = jnp.where(lanes == 0, spot, jnp.where(lanes == 1, column, 0.0))
        wide[192:208, :] = jnp.where(rows < cells - 192, wide[192:208, :], note)
        packed[r] = wide[...].astype(BF)


def pack(cotangent, height, place):
    side, regions = cotangent.shape[0], cotangent.shape[2]
    return local_kernel(
        functools.partial(pack_kernel, side, height),
        sds((regions, SLOT, 256), BF),
        cotangent,
        *place,
        scratch=[
            pltpu.VMEM((side * side * regions, 128), F32),
            pltpu.VMEM((side * side * regions, 128), F32),
            pltpu.VMEM((SLOT, 256), F32),
            pltpu.SMEM((3, 1, regions), jnp.int32),
            pltpu.SemaphoreType.DMA((3,)),
        ],
        hbm=(1, 2, 3),
    )


def pyramid_part(height, width, own, other, rim_a, rim_b, wf, pyr, xp, fetched):
    core = lax.rem(lax.axis_index("tile"), 2)
    cells = height * width
    col = lax.broadcasted_iota(jnp.int32, (width, 256), 0)

    def fill(src, count, where):
        def step(t, carry):
            v = src[pl.ds(pl.multiple_of(t * width, width), width), :].astype(F32)
            to = pl.ds(pl.multiple_of(where + t * width, width), width)
            xp[to, 0:256] = jnp.where(col == 0, 0.0, pltpu.roll(v, 1, 0)).astype(BF)
            xp[to, 256:512] = v.astype(BF)
            xp[to, 512:768] = jnp.where(
                col == width - 1, 0.0, pltpu.roll(v, width - 1, 0)
            ).astype(BF)
            return carry

        lax.fori_loop(0, count, step, 0)

    bottom = width + 2 * cells
    fill(own, height, width + core * cells)
    fill(other, height, width + (1 - core) * cells)
    fill(rim_a, 1, core * bottom)
    fill(rim_b, 1, (1 - core) * bottom)

    fetched.wait()

    def conv(t, carry):
        at = t * 256
        total = jnp.zeros((256, 256), F32)
        for a in range(3):
            piece = xp[pl.ds(pl.multiple_of(at + a * width, 64), 256), :]
            total += jnp.dot(piece, wf[a * 768 : a * 768 + 768, :], preferred_element_type=F32)
        pyr[pl.ds(pl.multiple_of(at, 256), 256), :] = total.astype(BF).astype(F32)
        return carry

    lax.fori_loop(0, 2 * cells // 256, conv, 0)
    pyr[2 * cells : 2 * cells + 16, :] = jnp.zeros((16, 256), F32)


def flip_part(w, wb):
    for k in range(9):
        block = w[(8 - k) * 256 : (9 - k) * 256, :].astype(F32)
        wb[k * 256 : k * 256 + 256, :] = block.T.astype(BF)


def gelu_pair(v):
    c = math.sqrt(2.0 / math.pi)
    sq = v * v
    t = jnp.tanh(c * (v + 0.044715 * (sq * v)))
    half = 0.5 * (1.0 + t)
    slope = half + 0.5 * v * (1.0 - t * t) * (c * (1.0 + 3 * 0.044715 * sq))
    return v * half, slope


def regions_part(side, height, width, blocks, pyr, w1, w2, wb1, wb2, acc1, acc2, gp, scratch):
    xs, hs, gs, wide, vs, slope1, todo = scratch
    chip = lax.axis_index("tile") // 2
    lanes = lax.broadcasted_iota(jnp.int32, (16, 256), 1)
    rows16 = lax.broadcasted_iota(jnp.int32, (16, 256), 0)
    in_row = rows16 < side
    per = blocks[0].shape[0]

    count = jnp.int32(0)
    for s, block in enumerate(blocks):
        for r in range(per):
            note = block[r, 192:208, :].astype(F32)
            note = jnp.where(rows16 == 15, note, 0.0)
            spot = jnp.sum(jnp.where(lanes == 0, note, 0.0)).astype(jnp.int32) - 1
            column = jnp.sum(jnp.where(lanes == 1, note, 0.0)).astype(jnp.int32)
            local = spot - chip * 2 * height
            here = (spot >= 0) & (local >= 0) & (local < 2 * height)
            todo[0, count] = jnp.int32(s * per + r)
            todo[1, count] = jnp.where(here, local * width + column // 8 * 8, 0)
            todo[2, count] = jnp.where(here, lax.rem(column, 8), 0)
            count = count + here.astype(jnp.int32)

    def batch(size, start):
        cells = (size * (side + 1) - 1) * PITCH
        spot = lax.broadcasted_iota(jnp.int32, (cells, 256), 0)
        inside = (lax.rem(spot, PITCH) < side) & (lax.rem(spot // PITCH, side + 1) < side)
        used = pl.ds(16, cells)

        def put(buf, v):
            buf[used, 0:256] = pltpu.roll(v, 1, 0).astype(BF)
            buf[used, 256:512] = v.astype(BF)
            buf[used, 512:768] = pltpu.roll(v, cells - 1, 0).astype(BF)

        def conv(buf, w):
            total = jnp.zeros((cells, 256), F32)
            for a in range(3):
                total += jnp.dot(
                    buf[a * 16 : a * 16 + cells, :],
                    w[a * 768 : a * 768 + 768, :],
                    preferred_element_type=F32,
                )
            return total

        def taps(acc, buf, grad):
            turned = grad.T.astype(BF)
            for a in range(3):
                acc[:, a * 768 : a * 768 + 768] += jnp.dot(
                    turned, buf[a * 16 : a * 16 + cells, :], preferred_element_type=F32
                )

        for buf in (xs, hs, gs):
            buf[0:16, :] = jnp.zeros((16, 768), BF)
            buf[cells + 16 : cells + 32, :] = jnp.zeros((16, 768), BF)
        for n in range(size - 1):
            gap = ((n + 1) * (side + 1) - 1) * PITCH
            vs[gap : gap + PITCH, :] = jnp.zeros((PITCH, 256), F32)
        bases, leads = [], []
        for n in range(size):
            which = todo[0, start + n]
            bases.append(pl.multiple_of(todo[1, start + n], 8))
            leads.append(todo[2, start + n])
            for s, block in enumerate(blocks):

                @pl.when(which // per == s)
                def _(block=block, n=n, which=which):
                    wide[n] = block[lax.rem(which, per)].astype(F32)

        for n in range(size):
            for i in range(side):
                got = pyr[pl.ds(pl.multiple_of(bases[n] + i * width, 8), 24), :]
                got = pltpu.roll(got, lax.rem(24 - leads[n], 24), 0)[0:16]
                at = (n * (side + 1) + i) * PITCH
                vs[at : at + 16, :] = jnp.where(in_row, got, 0.0)
        put(xs, vs[0:cells, :])
        act1, slope = gelu_pair(conv(xs, w1))
        slope1[0:cells, :] = slope
        put(hs, jnp.where(inside, act1, 0.0))
        _, slope = gelu_pair(conv(hs, w2))
        for n in range(size):
            for i in range(side):
                got = wide[n, i * side : i * side + 16, :]
                at = (n * (side + 1) + i) * PITCH
                vs[at : at + 16, :] = jnp.where(in_row, got, 0.0)
        g2 = vs[0:cells, :] * slope
        put(gs, g2)
        taps(acc2, hs, g2)
        gact1 = conv(gs, wb2)
        g1 = jnp.where(inside, gact1 * slope1[0:cells, :], 0.0)
        put(gs, g1)
        taps(acc1, xs, g1)
        vs[0:cells, :] = jnp.where(inside, conv(gs, wb1), 0.0).astype(BF).astype(F32)
        for n in range(size):
            for i in range(side):
                at = pl.ds(pl.multiple_of(bases[n] + i * width, 8), 24)
                row = (n * (side + 1) + i) * PITCH
                piece = jnp.concatenate([vs[row : row + 16, :], jnp.zeros((8, 256), F32)])
                gp[at, :] = gp[at, :] + pltpu.roll(piece, leads[n], 0)

    def pair(n, carry):
        batch(2, 2 * n)
        return carry

    lax.fori_loop(0, count // 2, pair, 0)

    @pl.when(lax.rem(count, 2) == 1)
    def _():
        batch(1, count - 1)


def finish_part(height, width, acc1, acc2, gp, keep, send, gp_own, gp_other):
    core = lax.rem(lax.axis_index("tile"), 2)
    cells = height * width

    def write(acc, to):
        for k in range(9):
            to[k * 256 : k * 256 + 256, :] = acc[:, k * 256 : k * 256 + 256].T.astype(BF)

    @pl.when(core == 0)
    def _():
        write(acc1, keep)
        write(acc2, send)

    @pl.when(core == 1)
    def _():
        write(acc2, keep)
        write(acc1, send)

    gp_own[...] = gp[pl.ds(pl.multiple_of(core * cells, cells), cells), :]
    gp_other[...] = gp[pl.ds(pl.multiple_of((1 - core) * cells, cells), cells), :].astype(BF)


def main_call(side, height, width, first, last, state, weights, blocks):
    n = len(blocks)
    big = 2 * height * width + 16
    cells = (2 * side + 1) * PITCH
    kept = (sds((big, 256), F32),) + (sds((2304, 256), BF),) * 4
    sums = (sds((256, 2304), F32), sds((256, 2304), F32), sds((big, 256), F32))
    ends = (
        sds((2304, 256), BF),
        sds((2304, 256), BF),
        sds((height * width, 256), F32),
        sds((height * width, 256), BF),
    )
    outs = (kept if first else ()) + sums + (ends if last else ())
    scratch = [
        pltpu.VMEM((cells + 32, 768), BF),
        pltpu.VMEM((cells + 32, 768), BF),
        pltpu.VMEM((cells + 32, 768), BF),
        pltpu.VMEM((2, SLOT, 256), F32),
        pltpu.VMEM((cells, 256), F32),
        pltpu.VMEM((cells, 256), F32),
        pltpu.SMEM((3, 128), jnp.int32),
    ]
    extra = []
    if first:
        extra = [
            pltpu.VMEM(((2 * height + 2) * width, 768), BF),
            pltpu.VMEM((2304, 256), BF),
            pltpu.VMEM((height * width, 256), BF),
            pltpu.SemaphoreType.DMA((4,)),
        ]

    def kernel(*refs):
        refs = list(refs)

        def take(k):
            got = refs[:k]
            del refs[:k]
            return got

        state_refs = take(len(state))
        weight_refs = take(len(weights))
        block_refs = take(n)
        out_refs = take(len(outs))
        scratch_refs = take(len(scratch))
        if first:
            pyr, wb1, wb2, w1, w2 = out_refs[:5]
            acc1, acc2, gp = out_refs[5:8]
            xp, wf, own, sems = refs
            copies = [
                pltpu.make_async_copy(source, to, sems.at[k])
                for k, (source, to) in enumerate(zip((state_refs[0], *weight_refs), (own, wf, w1, w2)))
            ]
            for copy in copies:
                copy.start()
            for total in (acc1, acc2, gp):
                total[...] = jnp.zeros(total.shape, F32)
            copies[0].wait()
            pyramid_part(height, width, own, *state_refs[1:], wf, pyr, xp, copies[1])
            copies[2].wait()
            flip_part(w1, wb1)
            copies[3].wait()
            flip_part(w2, wb2)
        else:
            pyr, wb1, wb2, w1, w2 = state_refs[:5]
            acc1, acc2, gp = out_refs[:3]
        regions_part(
            side, height, width, block_refs, pyr, w1, w2, wb1, wb2, acc1, acc2, gp, scratch_refs
        )
        if last:
            finish_part(height, width, acc1, acc2, gp, *out_refs[-4:])

    aliases = {} if first else {5: 0, 6: 1, 7: 2}
    return run(
        kernel,
        outs,
        [*state, *weights, *blocks],
        scratch=scratch + extra,
        aliases=aliases,
        hbm=(0, *range(len(state), len(state) + len(weights))) if first else (),
    )


def local_kernel(fn, outs, *arrays, **more):
    if isinstance(outs, tuple):
        return run(fn, outs, arrays, **more)
    return run(fn, (outs,), arrays, **more)[0]


def add(a, b):
    return (a.astype(F32) + b.astype(F32)).astype(BF)


def reduce_weights(keep, send, core_swap, dp, chips, beside):
    rows = keep.shape[0] // dp
    bits = dp.bit_length() - 1
    low = roundup(rows // 2, 16)
    spans = ((0, low), (low, rows))
    orders = (list(range(bits)), list(reversed(range(bits))))
    got = lax.ppermute(send, "tile", core_swap)

    def split(members, order):
        bit = 1 << order[0]
        return [m for m in members if not m & bit], [m for m in members if m & bit]

    members = [list(range(dp)), list(range(dp))]
    shapes = []
    for half in range(2):
        size = spans[half][1] - spans[half][0]
        stay, go = split(members[half], orders[half])
        shapes += [sds((len(stay), size, 256), BF), sds((len(go), size, 256), BF)]

    def first(keep_ref, got_ref, *outs):
        me = lax.axis_index("dp")
        for half in range(2):
            lo, hi = spans[half]
            for out, group in zip(outs[2 * half : 2 * half + 2], split(members[half], orders[half])):
                for n, m in enumerate(group):
                    at = pl.ds(pl.multiple_of((me ^ m) * rows + lo, 16), hi - lo)
                    out[n] = add(keep_ref[at, :], got_ref[at, :])

    parts = local_kernel(first, tuple(shapes), keep, got)
    for stage in range(bits):
        received = []
        for half in range(2):
            bit = 1 << orders[half][stage]
            received.append(lax.ppermute(parts[2 * half + 1], "dp", [(i, i ^ bit) for i in range(dp)]))
        if stage == 0:
            received[0], beside = lax.optimization_barrier((received[0], beside))
        for half in range(2):
            members[half] = split(members[half], orders[half][stage:])[0]
        if stage == bits - 1:
            break
        shapes = []
        for half in range(2):
            size = spans[half][1] - spans[half][0]
            stay, go = split(members[half], orders[half][stage + 1 :])
            shapes += [sds((len(stay), size, 256), BF), sds((len(go), size, 256), BF)]

        def middle(p, pr, q, qr, *outs, stage=stage):
            for half, (mine, theirs) in enumerate(((p, pr), (q, qr))):
                groups = split(members[half], orders[half][stage + 1 :])
                for out, group in zip(outs[2 * half : 2 * half + 2], groups):
                    for n, m in enumerate(group):
                        k = members[half].index(m)
                        out[n] = add(mine[k], theirs[k])

        parts = local_kernel(middle, tuple(shapes), parts[0], received[0], parts[2], received[1])

    share = roundup(-(-rows // chips), 16)
    shifts = [
        [(2 * z + c, 2 * ((z + k) % chips) + c) for z in range(chips) for c in range(2)]
        for k in range(chips)
    ]

    def deal(p, pr, q, qr, *refs):
        outs, total = refs[:chips], refs[chips]
        chip = lax.axis_index("tile") // 2
        total[0:low, :] = add(p[0], pr[0])
        total[low:rows, :] = add(q[0], qr[0])
        if share * chips > rows:
            total[rows:, :] = jnp.zeros((share * chips - rows, 256), BF)
        for k in range(chips):
            to = lax.rem(chip + k, chips)
            outs[k][...] = total[pl.ds(pl.multiple_of(to * share, 16), share), :]

    dealt = local_kernel(
        deal,
        tuple(sds((share, 256), BF) for _ in range(chips)),
        *(parts[0], received[0], parts[2], received[1]),
        scratch=[pltpu.VMEM((share * chips, 256), BF)],
    )
    arrived = [lax.ppermute(dealt[k], "tile", shifts[k]) for k in range(1, chips)]

    def gather(*refs):
        total = refs[0][...].astype(F32)
        for ref in refs[1:-1]:
            total += ref[...].astype(F32)
        refs[-1][...] = total.astype(BF)

    mine = local_kernel(gather, sds((share, 256), BF), dealt[0], *arrived)
    pieces = [mine] + [lax.ppermute(mine, "tile", shifts[k]) for k in range(1, chips)]

    def lay(*refs):
        chip = lax.axis_index("tile") // 2
        for k in range(chips):
            source = lax.rem(chip - k + chips, chips)
            refs[-1][pl.ds(pl.multiple_of(source * share, 16), share), :] = refs[k][...]

    whole = local_kernel(lay, sds((share * chips, 256), BF), *pieces)
    theirs = lax.ppermute(whole, "tile", core_swap)

    def out(mine_ref, theirs_ref, one, two):
        core = lax.rem(lax.axis_index("tile"), 2)

        @pl.when(core == 0)
        def _():
            one[...] = mine_ref[0:rows, :].astype(F32)
            two[...] = theirs_ref[0:rows, :].astype(F32)

        @pl.when(core == 1)
        def _():
            one[...] = theirs_ref[0:rows, :].astype(F32)
            two[...] = mine_ref[0:rows, :].astype(F32)

    one, two = local_kernel(
        out, (sds((rows, 256), F32), sds((rows, 256), F32)), whole, theirs, hbm_out=(0, 1)
    )
    return one, two, beside


def body(features, fpn_weight, mask_w1, mask_w2, owner, row_off, col_off, cotangent):
    tiles = lax.axis_size("tile")
    dp = lax.axis_size("dp")
    chips = tiles // 2
    height, width, channels = features.shape[1:]
    side = cotangent.shape[2]
    swap = [(i, i ^ 1) for i in range(tiles)]

    tile = features.reshape(height * width, channels)
    regions = cotangent.shape[1]
    place = [x.reshape(1, regions) for x in (owner, row_off, col_off)]
    edge = edge_of(tile, height, width)
    rim_a = lax.ppermute(
        edge, "tile", [(i, i + 1 if i % 2 else i - 1) for i in range(1, tiles - 1)]
    )
    across = [(i, i + 2 if i % 2 else i - 2) for i in range(tiles)]
    rim_b = lax.ppermute(edge, "tile", [(i, j) for i, j in across if 0 <= j < tiles])
    other = lax.ppermute(tile, "tile", swap)
    packed = pack(cotangent[0].transpose(1, 2, 0, 3), height, place)
    packed, rim_a, rim_b = lax.optimization_barrier((packed, rim_a, rim_b))

    up = [(i, i + 2) for i in range(tiles - 2)]
    down = [(i + 2, i) for i in range(tiles - 2)]
    flat = lambda w: w.reshape(9 * channels, channels)
    wf, w1, w2 = flat(fpn_weight), flat(mask_w1), flat(mask_w2)
    blocks = [lax.ppermute(packed, "tile", up), lax.ppermute(packed, "tile", down)]
    start = main_call(
        side, height, width, True, False, [tile, other, rim_a, rim_b], [wf, w1, w2], [packed]
    )
    kept, sums = list(start[:5]), list(start[5:])
    for step in range(1, chips):
        last = step == chips - 1
        held = blocks
        if not last:
            held[0], held[1], kept[0] = lax.optimization_barrier((held[0], held[1], kept[0]))
            blocks = [lax.ppermute(held[0], "tile", up), lax.ppermute(held[1], "tile", down)]
        got = main_call(
            side,
            height,
            width,
            False,
            last,
            [*kept, *sums],
            [],
            held,
        )
        sums, ends = list(got[:3]), got[3:]
        if not last:
            kept[0], sums[0] = lax.optimization_barrier((kept[0], sums[0]))
    keep, send, gp_own, gp_other = ends
    gp_got = lax.ppermute(gp_other, "tile", swap)

    def join(a, b, out):
        out[...] = (a[...] + b[...].astype(F32)).astype(BF)

    joined = local_kernel(
        join, sds((height * width, channels), BF), gp_own, gp_got, hbm_out=(0,)
    )
    grad_one, grad_two, grad_pyramid = reduce_weights(keep, send, swap, dp, chips, joined)
    return grad_one, grad_two, grad_pyramid.reshape(1, height, width, channels)


def solution(mesh):
    placed = (
        P("dp", "tile", None, None),
        P(),
        P(),
        P(),
        P("dp", "tile", None),
        P("dp", "tile"),
        P("dp", "tile"),
        P("dp", "tile", None, None, None),
    )
    return jax.shard_map(
        body,
        mesh=mesh,
        in_specs=placed,
        out_specs=(P("dp", None), P("dp", None), P("dp", "tile", None, None)),
        check_vma=False,
    )
```

```python
import functools
import math

import jax
import jax.numpy as jnp
from jax import lax
from jax.experimental import pallas as pl
from jax.experimental.pallas import tpu as pltpu
from jax.sharding import PartitionSpec as P

BF = jnp.bfloat16
F32 = jnp.float32
VMEM_LIMIT = 24 * 1024 * 1024
PITCH = 16
SLOT = 208


def roundup(n, m):
    return (n + m - 1) // m * m


def run(kernel, outs, args, scratch=(), aliases=None, hbm=(), hbm_out=()):
    args = [
        pltpu.with_memory_space_constraint(x, pltpu.HBM if i in hbm else pltpu.VMEM)
        for i, x in enumerate(args)
    ]
    return pl.pallas_call(
        kernel,
        out_shape=tuple(
            s if i in hbm_out else pltpu.VMEM(s.shape, s.dtype) for i, s in enumerate(outs)
        ),
        in_specs=[
            pl.BlockSpec(memory_space=pltpu.HBM if i in hbm else pltpu.VMEM)
            for i in range(len(args))
        ],
        out_specs=tuple(pl.BlockSpec(memory_space=pltpu.VMEM) for _ in outs),
        scratch_shapes=list(scratch),
        input_output_aliases=aliases or {},
        compiler_params=pltpu.CompilerParams(vmem_limit_bytes=VMEM_LIMIT),
    )(*args)


def sds(shape, dtype):
    return jax.ShapeDtypeStruct(shape, dtype)


def edge_of(tile, height, width):
    def kernel(tile, edge, sem):
        core = lax.rem(lax.axis_index("tile"), 2)
        line = pl.ds(pl.multiple_of(core * (height - 1) * width, width), width)
        copy = pltpu.make_async_copy(tile.at[line, :], edge, sem)
        copy.start()
        copy.wait()

    return local_kernel(
        kernel, sds((width, 256), BF), tile, scratch=[pltpu.SemaphoreType.DMA], hbm=(0,)
    )


def pack_kernel(side, height, cot, owner, row, col, packed, low, high, wide, places, sems):
    regions = cot.shape[2]
    copies = [
        pltpu.make_async_copy(source, places.at[n], sems.at[n])
        for n, source in enumerate((owner, row, col))
    ]
    for copy in copies:
        copy.start()
    for i in range(side):
        for j in range(side):
            at = (i * side + j) * regions
            cell = cot[i, j].astype(F32)
            low[at : at + regions, :] = cell[:, 0:128]
            high[at : at + regions, :] = cell[:, 128:256]
    for copy in copies:
        copy.wait()
    lanes = lax.broadcasted_iota(jnp.int32, (16, 256), 1)
    rows = lax.broadcasted_iota(jnp.int32, (16, 256), 0)
    cells = side * side
    for r in range(regions):
        wide[0:cells, 0:128] = low[pl.ds(r, cells, stride=regions), :]
        wide[0:cells, 128:256] = high[pl.ds(r, cells, stride=regions), :]
        spot = (places[0, 0, r] * height + places[1, 0, r] + 1).astype(F32)
        column = places[2, 0, r].astype(F32)
        note = jnp.where(lanes == 0, spot, jnp.where(lanes == 1, column, 0.0))
        wide[192:208, :] = jnp.where(rows < cells - 192, wide[192:208, :], note)
        packed[r] = wide[...].astype(BF)


def pack(cotangent, height, place):
    side, regions = cotangent.shape[0], cotangent.shape[2]
    return local_kernel(
        functools.partial(pack_kernel, side, height),
        sds((regions, SLOT, 256), BF),
        cotangent,
        *place,
        scratch=[
            pltpu.VMEM((side * side * regions, 128), F32),
            pltpu.VMEM((side * side * regions, 128), F32),
            pltpu.VMEM((SLOT, 256), F32),
            pltpu.SMEM((3, 1, regions), jnp.int32),
            pltpu.SemaphoreType.DMA((3,)),
        ],
        hbm=(1, 2, 3),
    )


def pyramid_part(height, width, own, other, rim_a, rim_b, wf, pyr, xp, fetched):
    core = lax.rem(lax.axis_index("tile"), 2)
    cells = height * width
    col = lax.broadcasted_iota(jnp.int32, (width, 256), 0)

    def fill(src, count, where):
        def step(t, carry):
            v = src[pl.ds(pl.multiple_of(t * width, width), width), :].astype(F32)
            to = pl.ds(pl.multiple_of(where + t * width, width), width)
            xp[to, 0:256] = jnp.where(col == 0, 0.0, pltpu.roll(v, 1, 0)).astype(BF)
            xp[to, 256:512] = v.astype(BF)
            xp[to, 512:768] = jnp.where(
                col == width - 1, 0.0, pltpu.roll(v, width - 1, 0)
            ).astype(BF)
            return carry

        lax.fori_loop(0, count, step, 0)

    bottom = width + 2 * cells
    fill(own, height, width + core * cells)
    fill(other, height, width + (1 - core) * cells)
    fill(rim_a, 1, core * bottom)
    fill(rim_b, 1, (1 - core) * bottom)

    fetched.wait()

    def conv(t, carry):
        at = t * 256
        total = jnp.zeros((256, 256), F32)
        for a in range(3):
            piece = xp[pl.ds(pl.multiple_of(at + a * width, 64), 256), :]
            total += jnp.dot(piece, wf[a * 768 : a * 768 + 768, :], preferred_element_type=F32)
        pyr[pl.ds(pl.multiple_of(at, 256), 256), :] = total.astype(BF).astype(F32)
        return carry

    lax.fori_loop(0, 2 * cells // 256, conv, 0)
    pyr[2 * cells : 2 * cells + 16, :] = jnp.zeros((16, 256), F32)


def flip_part(w, wb):
    for k in range(9):
        block = w[(8 - k) * 256 : (9 - k) * 256, :].astype(F32)
        wb[k * 256 : k * 256 + 256, :] = block.T.astype(BF)


def gelu_pair(v):
    c = math.sqrt(2.0 / math.pi)
    sq = v * v
    t = jnp.tanh(c * (v + 0.044715 * (sq * v)))
    half = 0.5 * (1.0 + t)
    slope = half + 0.5 * v * (1.0 - t * t) * (c * (1.0 + 3 * 0.044715 * sq))
    return v * half, slope


def regions_part(side, height, width, blocks, pyr, w1, w2, wb1, wb2, acc1, acc2, gp, scratch):
    xs, hs, gs, wide, vs, slope1, todo = scratch
    chip = lax.axis_index("tile") // 2
    lanes = lax.broadcasted_iota(jnp.int32, (16, 256), 1)
    rows16 = lax.broadcasted_iota(jnp.int32, (16, 256), 0)
    in_row = rows16 < side
    per = blocks[0].shape[0]

    count = jnp.int32(0)
    for s, block in enumerate(blocks):
        for r in range(per):
            note = block[r, 192:208, :].astype(F32)
            note = jnp.where(rows16 == 15, note, 0.0)
            spot = jnp.sum(jnp.where(lanes == 0, note, 0.0)).astype(jnp.int32) - 1
            column = jnp.sum(jnp.where(lanes == 1, note, 0.0)).astype(jnp.int32)
            local = spot - chip * 2 * height
            here = (spot >= 0) & (local >= 0) & (local < 2 * height)
            todo[0, count] = jnp.int32(s * per + r)
            todo[1, count] = jnp.where(here, local * width + column // 8 * 8, 0)
            todo[2, count] = jnp.where(here, lax.rem(column, 8), 0)
            count = count + here.astype(jnp.int32)

    def batch(size, start):
        cells = (size * (side + 1) - 1) * PITCH
        spot = lax.broadcasted_iota(jnp.int32, (cells, 256), 0)
        gap = side * PITCH
        inside = ((spot & (PITCH - 1)) < side) & ((spot < gap) | (spot >= gap + PITCH))
        used = pl.ds(16, cells)

        def put(buf, v):
            buf[used, 0:256] = pltpu.roll(v, 1, 0).astype(BF)
            buf[used, 256:512] = v.astype(BF)
            buf[used, 512:768] = pltpu.roll(v, cells - 1, 0).astype(BF)

        def conv(buf, w):
            total = jnp.zeros((cells, 256), F32)
            for a in range(3):
                total += jnp.dot(
                    buf[a * 16 : a * 16 + cells, :],
                    w[a * 768 : a * 768 + 768, :],
                    preferred_element_type=F32,
                )
            return total

        def taps(acc, buf, grad):
            turned = grad.T.astype(BF)
            for a in range(3):
                acc[:, a * 768 : a * 768 + 768] += jnp.dot(
                    turned, buf[a * 16 : a * 16 + cells, :], preferred_element_type=F32
                )

        for buf in (xs, hs, gs):
            buf[0:16, :] = jnp.zeros((16, 768), BF)
            buf[cells + 16 : cells + 32, :] = jnp.zeros((16, 768), BF)
        for n in range(size - 1):
            vs[gap : gap + PITCH, :] = jnp.zeros((PITCH, 256), F32)
        bases, leads = [], []
        for n in range(size):
            which = todo[0, start + n]
            bases.append(pl.multiple_of(todo[1, start + n], 8))
            leads.append(todo[2, start + n])
            for s, block in enumerate(blocks):

                @pl.when(which // per == s)
                def _(block=block, n=n, which=which):
                    wide[n] = block[lax.rem(which, per)].astype(F32)

        for n in range(size):
            for i in range(side):
                got = pyr[pl.ds(pl.multiple_of(bases[n] + i * width, 8), 24), :]
                got = pltpu.roll(got, lax.rem(24 - leads[n], 24), 0)[0:16]
                at = (n * (side + 1) + i) * PITCH
                vs[at : at + 16, :] = jnp.where(in_row, got, 0.0)
        put(xs, vs[0:cells, :])
        act1, slope = gelu_pair(conv(xs, w1))
        slope1[0:cells, :] = slope
        put(hs, jnp.where(inside, act1, 0.0))
        _, slope = gelu_pair(conv(hs, w2))
        for n in range(size):
            for i in range(side):
                got = wide[n, i * side : i * side + 16, :]
                at = (n * (side + 1) + i) * PITCH
                vs[at : at + 16, :] = jnp.where(in_row, got, 0.0)
        g2 = vs[0:cells, :] * slope
        put(gs, g2)
        taps(acc2, hs, g2)
        gact1 = conv(gs, wb2)
        g1 = jnp.where(inside, gact1 * slope1[0:cells, :], 0.0)
        put(gs, g1)
        taps(acc1, xs, g1)
        vs[0:cells, :] = jnp.where(inside, conv(gs, wb1), 0.0).astype(BF).astype(F32)
        for n in range(size):
            for i in range(side):
                at = pl.ds(pl.multiple_of(bases[n] + i * width, 8), 24)
                row = (n * (side + 1) + i) * PITCH
                piece = jnp.concatenate([vs[row : row + 16, :], jnp.zeros((8, 256), F32)])
                gp[at, :] = gp[at, :] + pltpu.roll(piece, leads[n], 0)

    def pair(n, carry):
        batch(2, 2 * n)
        return carry

    lax.fori_loop(0, count // 2, pair, 0)

    @pl.when(lax.rem(count, 2) == 1)
    def _():
        batch(1, count - 1)


def finish_part(height, width, acc1, acc2, gp, keep, send, gp_own, gp_other):
    core = lax.rem(lax.axis_index("tile"), 2)
    cells = height * width

    def write(acc, to):
        for k in range(9):
            to[k * 256 : k * 256 + 256, :] = acc[:, k * 256 : k * 256 + 256].T.astype(BF)

    @pl.when(core == 0)
    def _():
        write(acc1, keep)
        write(acc2, send)

    @pl.when(core == 1)
    def _():
        write(acc2, keep)
        write(acc1, send)

    gp_own[...] = gp[pl.ds(pl.multiple_of(core * cells, cells), cells), :]
    gp_other[...] = gp[pl.ds(pl.multiple_of((1 - core) * cells, cells), cells), :].astype(BF)


def main_call(side, height, width, first, last, state, weights, blocks):
    n = len(blocks)
    big = 2 * height * width + 16
    cells = (2 * side + 1) * PITCH
    kept = (sds((big, 256), F32),) + (sds((2304, 256), BF),) * 4
    sums = (sds((256, 2304), F32), sds((256, 2304), F32), sds((big, 256), F32))
    ends = (
        sds((2304, 256), BF),
        sds((2304, 256), BF),
        sds((height * width, 256), F32),
        sds((height * width, 256), BF),
    )
    outs = (kept if first else ()) + sums + (ends if last else ())
    scratch = [
        pltpu.VMEM((cells + 32, 768), BF),
        pltpu.VMEM((cells + 32, 768), BF),
        pltpu.VMEM((cells + 32, 768), BF),
        pltpu.VMEM((2, SLOT, 256), F32),
        pltpu.VMEM((cells, 256), F32),
        pltpu.VMEM((cells, 256), F32),
        pltpu.SMEM((3, 128), jnp.int32),
    ]
    extra = []
    if first:
        extra = [
            pltpu.VMEM(((2 * height + 2) * width, 768), BF),
            pltpu.VMEM((2304, 256), BF),
            pltpu.VMEM((height * width, 256), BF),
            pltpu.SemaphoreType.DMA((4,)),
        ]

    def kernel(*refs):
        refs = list(refs)

        def take(k):
            got = refs[:k]
            del refs[:k]
            return got

        state_refs = take(len(state))
        weight_refs = take(len(weights))
        block_refs = take(n)
        out_refs = take(len(outs))
        scratch_refs = take(len(scratch))
        if first:
            pyr, wb1, wb2, w1, w2 = out_refs[:5]
            acc1, acc2, gp = out_refs[5:8]
            xp, wf, own, sems = refs
            copies = [
                pltpu.make_async_copy(source, to, sems.at[k])
                for k, (source, to) in enumerate(zip((state_refs[0], *weight_refs), (own, wf, w1, w2)))
            ]
            for copy in copies:
                copy.start()
            for total in (acc1, acc2, gp):
                total[...] = jnp.zeros(total.shape, F32)
            copies[0].wait()
            pyramid_part(height, width, own, *state_refs[1:], wf, pyr, xp, copies[1])
            copies[2].wait()
            flip_part(w1, wb1)
            copies[3].wait()
            flip_part(w2, wb2)
        else:
            pyr, wb1, wb2, w1, w2 = state_refs[:5]
            acc1, acc2, gp = out_refs[:3]
        regions_part(
            side, height, width, block_refs, pyr, w1, w2, wb1, wb2, acc1, acc2, gp, scratch_refs
        )
        if last:
            finish_part(height, width, acc1, acc2, gp, *out_refs[-4:])

    aliases = {} if first else {5: 0, 6: 1, 7: 2}
    return run(
        kernel,
        outs,
        [*state, *weights, *blocks],
        scratch=scratch + extra,
        aliases=aliases,
        hbm=(0, *range(len(state), len(state) + len(weights))) if first else (),
    )


def local_kernel(fn, outs, *arrays, **more):
    if isinstance(outs, tuple):
        return run(fn, outs, arrays, **more)
    return run(fn, (outs,), arrays, **more)[0]


def add(a, b):
    return (a.astype(F32) + b.astype(F32)).astype(BF)


def reduce_weights(keep, send, core_swap, dp, chips, beside):
    rows = keep.shape[0] // dp
    bits = dp.bit_length() - 1
    low = roundup(rows // 2, 16)
    spans = ((0, low), (low, rows))
    orders = (list(range(bits)), list(reversed(range(bits))))
    got = lax.ppermute(send, "tile", core_swap)

    def split(members, order):
        bit = 1 << order[0]
        return [m for m in members if not m & bit], [m for m in members if m & bit]

    members = [list(range(dp)), list(range(dp))]
    shapes = []
    for half in range(2):
        size = spans[half][1] - spans[half][0]
        stay, go = split(members[half], orders[half])
        shapes += [sds((len(stay), size, 256), BF), sds((len(go), size, 256), BF)]

    def first(keep_ref, got_ref, *outs):
        me = lax.axis_index("dp")
        for half in range(2):
            lo, hi = spans[half]
            for out, group in zip(outs[2 * half : 2 * half + 2], split(members[half], orders[half])):
                for n, m in enumerate(group):
                    at = pl.ds(pl.multiple_of((me ^ m) * rows + lo, 16), hi - lo)
                    out[n] = add(keep_ref[at, :], got_ref[at, :])

    parts = local_kernel(first, tuple(shapes), keep, got)
    for stage in range(bits):
        received = []
        for half in range(2):
            bit = 1 << orders[half][stage]
            received.append(lax.ppermute(parts[2 * half + 1], "dp", [(i, i ^ bit) for i in range(dp)]))
        if stage == 0:
            received[0], beside = lax.optimization_barrier((received[0], beside))
        for half in range(2):
            members[half] = split(members[half], orders[half][stage:])[0]
        if stage == bits - 1:
            break
        shapes = []
        for half in range(2):
            size = spans[half][1] - spans[half][0]
            stay, go = split(members[half], orders[half][stage + 1 :])
            shapes += [sds((len(stay), size, 256), BF), sds((len(go), size, 256), BF)]

        def middle(p, pr, q, qr, *outs, stage=stage):
            for half, (mine, theirs) in enumerate(((p, pr), (q, qr))):
                groups = split(members[half], orders[half][stage + 1 :])
                for out, group in zip(outs[2 * half : 2 * half + 2], groups):
                    for n, m in enumerate(group):
                        k = members[half].index(m)
                        out[n] = add(mine[k], theirs[k])

        parts = local_kernel(middle, tuple(shapes), parts[0], received[0], parts[2], received[1])

    share = roundup(-(-rows // chips), 16)
    shifts = [
        [(2 * z + c, 2 * ((z + k) % chips) + c) for z in range(chips) for c in range(2)]
        for k in range(chips)
    ]

    def deal(p, pr, q, qr, *refs):
        outs, total = refs[:chips], refs[chips]
        chip = lax.axis_index("tile") // 2
        total[0:low, :] = add(p[0], pr[0])
        total[low:rows, :] = add(q[0], qr[0])
        if share * chips > rows:
            total[rows:, :] = jnp.zeros((share * chips - rows, 256), BF)
        for k in range(chips):
            to = lax.rem(chip + k, chips)
            outs[k][...] = total[pl.ds(pl.multiple_of(to * share, 16), share), :]

    dealt = local_kernel(
        deal,
        tuple(sds((share, 256), BF) for _ in range(chips)),
        *(parts[0], received[0], parts[2], received[1]),
        scratch=[pltpu.VMEM((share * chips, 256), BF)],
    )
    arrived = [lax.ppermute(dealt[k], "tile", shifts[k]) for k in range(1, chips)]

    def gather(*refs):
        total = refs[0][...].astype(F32)
        for ref in refs[1:-1]:
            total += ref[...].astype(F32)
        refs[-1][...] = total.astype(BF)

    mine = local_kernel(gather, sds((share, 256), BF), dealt[0], *arrived)
    pieces = [mine] + [lax.ppermute(mine, "tile", shifts[k]) for k in range(1, chips)]

    def lay(*refs):
        chip = lax.axis_index("tile") // 2
        for k in range(chips):
            source = lax.rem(chip - k + chips, chips)
            refs[-1][pl.ds(pl.multiple_of(source * share, 16), share), :] = refs[k][...]

    whole = local_kernel(lay, sds((share * chips, 256), BF), *pieces)
    theirs = lax.ppermute(whole, "tile", core_swap)

    def out(mine_ref, theirs_ref, one, two):
        core = lax.rem(lax.axis_index("tile"), 2)

        @pl.when(core == 0)
        def _():
            one[...] = mine_ref[0:rows, :].astype(F32)
            two[...] = theirs_ref[0:rows, :].astype(F32)

        @pl.when(core == 1)
        def _():
            one[...] = theirs_ref[0:rows, :].astype(F32)
            two[...] = mine_ref[0:rows, :].astype(F32)

    one, two = local_kernel(
        out, (sds((rows, 256), F32), sds((rows, 256), F32)), whole, theirs, hbm_out=(0, 1)
    )
    return one, two, beside


def body(features, fpn_weight, mask_w1, mask_w2, owner, row_off, col_off, cotangent):
    tiles = lax.axis_size("tile")
    dp = lax.axis_size("dp")
    chips = tiles // 2
    height, width, channels = features.shape[1:]
    side = cotangent.shape[2]
    swap = [(i, i ^ 1) for i in range(tiles)]

    tile = features.reshape(height * width, channels)
    regions = cotangent.shape[1]
    place = [x.reshape(1, regions) for x in (owner, row_off, col_off)]
    edge = edge_of(tile, height, width)
    rim_a = lax.ppermute(
        edge, "tile", [(i, i + 1 if i % 2 else i - 1) for i in range(1, tiles - 1)]
    )
    across = [(i, i + 2 if i % 2 else i - 2) for i in range(tiles)]
    rim_b = lax.ppermute(edge, "tile", [(i, j) for i, j in across if 0 <= j < tiles])
    other = lax.ppermute(tile, "tile", swap)
    packed = pack(cotangent[0].transpose(1, 2, 0, 3), height, place)
    packed, rim_a, rim_b = lax.optimization_barrier((packed, rim_a, rim_b))

    ring = [(i, (i + 2) % tiles) for i in range(tiles)]

    flat = lambda w: w.reshape(9 * channels, channels)
    wf, w1, w2 = flat(fpn_weight), flat(mask_w1), flat(mask_w2)
    block = lax.ppermute(packed, "tile", ring)
    start = main_call(
        side, height, width, True, False, [tile, other, rim_a, rim_b], [wf, w1, w2], [packed]
    )
    kept, sums = list(start[:5]), list(start[5:])
    for step in range(1, chips):
        last = step == chips - 1
        held = block
        if not last:
            held, kept[0] = lax.optimization_barrier((held, kept[0]))
            block = lax.ppermute(held, "tile", ring)
        got = main_call(
            side,
            height,
            width,
            False,
            last,
            [*kept, *sums],
            [],
            [held],
        )
        sums, ends = list(got[:3]), got[3:]
        if not last:
            kept[0], sums[0] = lax.optimization_barrier((kept[0], sums[0]))
    keep, send, gp_own, gp_other = ends
    gp_got = lax.ppermute(gp_other, "tile", swap)

    def join(a, b, out):
        out[...] = (a[...] + b[...].astype(F32)).astype(BF)

    joined = local_kernel(
        join, sds((height * width, channels), BF), gp_own, gp_got, hbm_out=(0,)
    )
    grad_one, grad_two, grad_pyramid = reduce_weights(keep, send, swap, dp, chips, joined)
    return grad_one, grad_two, grad_pyramid.reshape(1, height, width, channels)


def solution(mesh):
    placed = (
        P("dp", "tile", None, None),
        P(),
        P(),
        P(),
        P("dp", "tile", None),
        P("dp", "tile"),
        P("dp", "tile"),
        P("dp", "tile", None, None, None),
    )
    return jax.shard_map(
        body,
        mesh=mesh,
        in_specs=placed,
        out_specs=(P("dp", None), P("dp", None), P("dp", "tile", None, None)),
        check_vma=False,
    )
```

```python
import functools
import math

import jax
import jax.numpy as jnp
from jax import lax
from jax.experimental import pallas as pl
from jax.experimental.pallas import tpu as pltpu
from jax.sharding import PartitionSpec as P

BF = jnp.bfloat16
F32 = jnp.float32
VMEM_LIMIT = 24 * 1024 * 1024
PITCH = 16
SLOT = 208


def roundup(n, m):
    return (n + m - 1) // m * m


def run(kernel, outs, args, scratch=(), aliases=None, hbm=(), hbm_out=()):
    args = [
        pltpu.with_memory_space_constraint(x, pltpu.HBM if i in hbm else pltpu.VMEM)
        for i, x in enumerate(args)
    ]
    return pl.pallas_call(
        kernel,
        out_shape=tuple(
            s if i in hbm_out else pltpu.VMEM(s.shape, s.dtype) for i, s in enumerate(outs)
        ),
        in_specs=[
            pl.BlockSpec(memory_space=pltpu.HBM if i in hbm else pltpu.VMEM)
            for i in range(len(args))
        ],
        out_specs=tuple(pl.BlockSpec(memory_space=pltpu.VMEM) for _ in outs),
        scratch_shapes=list(scratch),
        input_output_aliases=aliases or {},
        compiler_params=pltpu.CompilerParams(vmem_limit_bytes=VMEM_LIMIT),
    )(*args)


def sds(shape, dtype):
    return jax.ShapeDtypeStruct(shape, dtype)


def edge_of(tile, height, width):
    def kernel(tile, edge, sem):
        core = lax.rem(lax.axis_index("tile"), 2)
        line = pl.ds(pl.multiple_of(core * (height - 1) * width, width), width)
        copy = pltpu.make_async_copy(tile.at[line, :], edge, sem)
        copy.start()
        copy.wait()

    return local_kernel(
        kernel, sds((width, 256), BF), tile, scratch=[pltpu.SemaphoreType.DMA], hbm=(0,)
    )


def pack_kernel(side, height, cot, owner, row, col, packed, low, high, wide, places, sems):
    regions = cot.shape[2]
    copies = [
        pltpu.make_async_copy(source, places.at[n], sems.at[n])
        for n, source in enumerate((owner, row, col))
    ]
    for copy in copies:
        copy.start()
    for i in range(side):
        for j in range(side):
            at = (i * side + j) * regions
            cell = cot[i, j].astype(F32)
            low[at : at + regions, :] = cell[:, 0:128]
            high[at : at + regions, :] = cell[:, 128:256]
    for copy in copies:
        copy.wait()
    lanes = lax.broadcasted_iota(jnp.int32, (16, 256), 1)
    rows = lax.broadcasted_iota(jnp.int32, (16, 256), 0)
    cells = side * side
    for r in range(regions):
        wide[0:cells, 0:128] = low[pl.ds(r, cells, stride=regions), :]
        wide[0:cells, 128:256] = high[pl.ds(r, cells, stride=regions), :]
        spot = (places[0, 0, r] * height + places[1, 0, r] + 1).astype(F32)
        column = places[2, 0, r].astype(F32)
        note = jnp.where(lanes == 0, spot, jnp.where(lanes == 1, column, 0.0))
        wide[192:208, :] = jnp.where(rows < cells - 192, wide[192:208, :], note)
        packed[r] = wide[...].astype(BF)


def pack(cotangent, height, place):
    side, regions = cotangent.shape[0], cotangent.shape[2]
    return local_kernel(
        functools.partial(pack_kernel, side, height),
        sds((regions, SLOT, 256), BF),
        cotangent,
        *place,
        scratch=[
            pltpu.VMEM((side * side * regions, 128), F32),
            pltpu.VMEM((side * side * regions, 128), F32),
            pltpu.VMEM((SLOT, 256), F32),
            pltpu.SMEM((3, 1, regions), jnp.int32),
            pltpu.SemaphoreType.DMA((3,)),
        ],
        hbm=(1, 2, 3),
    )


def pyramid_part(height, width, own, other, rim_a, rim_b, wf, pyr, xp, fetched):
    core = lax.rem(lax.axis_index("tile"), 2)
    cells = height * width
    col = lax.broadcasted_iota(jnp.int32, (width, 256), 0)

    def fill(src, count, where):
        def step(t, carry):
            v = src[pl.ds(pl.multiple_of(t * width, width), width), :].astype(F32)
            to = pl.ds(pl.multiple_of(where + t * width, width), width)
            xp[to, 0:256] = jnp.where(col == 0, 0.0, pltpu.roll(v, 1, 0)).astype(BF)
            xp[to, 256:512] = v.astype(BF)
            xp[to, 512:768] = jnp.where(
                col == width - 1, 0.0, pltpu.roll(v, width - 1, 0)
            ).astype(BF)
            return carry

        lax.fori_loop(0, count, step, 0)

    bottom = width + 2 * cells
    fill(own, height, width + core * cells)
    fill(other, height, width + (1 - core) * cells)
    fill(rim_a, 1, core * bottom)
    fill(rim_b, 1, (1 - core) * bottom)

    fetched.wait()

    def conv(t, carry):
        at = t * 256
        total = jnp.zeros((256, 256), F32)
        for a in range(3):
            piece = xp[pl.ds(pl.multiple_of(at + a * width, 64), 256), :]
            total += jnp.dot(piece, wf[a * 768 : a * 768 + 768, :], preferred_element_type=F32)
        pyr[pl.ds(pl.multiple_of(at, 256), 256), :] = total.astype(BF).astype(F32)
        return carry

    lax.fori_loop(0, 2 * cells // 256, conv, 0)
    pyr[2 * cells : 2 * cells + 16, :] = jnp.zeros((16, 256), F32)


def flip_part(w, wb):
    for k in range(9):
        block = w[(8 - k) * 256 : (9 - k) * 256, :].astype(F32)
        wb[k * 256 : k * 256 + 256, :] = block.T.astype(BF)


def gelu_pair(v):
    c = math.sqrt(2.0 / math.pi)
    sq = v * v
    t = jnp.tanh(c * (v + 0.044715 * (sq * v)))
    half = 0.5 * (1.0 + t)
    slope = half + 0.5 * v * (1.0 - t * t) * (c * (1.0 + 3 * 0.044715 * sq))
    return v * half, slope


def regions_part(side, height, width, blocks, pyr, w1, w2, wb1, wb2, acc1, acc2, gp, scratch):
    xs, hs, gs, wide, vs, slope1, todo = scratch
    chip = lax.axis_index("tile") // 2
    lanes = lax.broadcasted_iota(jnp.int32, (16, 256), 1)
    rows16 = lax.broadcasted_iota(jnp.int32, (16, 256), 0)
    in_row = rows16 < side
    per = blocks[0].shape[0]

    count = jnp.int32(0)
    for s, block in enumerate(blocks):
        for r in range(per):
            note = block[r, 192:208, :].astype(F32)
            note = jnp.where(rows16 == 15, note, 0.0)
            spot = jnp.sum(jnp.where(lanes == 0, note, 0.0)).astype(jnp.int32) - 1
            column = jnp.sum(jnp.where(lanes == 1, note, 0.0)).astype(jnp.int32)
            local = spot - chip * 2 * height
            here = (spot >= 0) & (local >= 0) & (local < 2 * height)
            todo[0, count] = jnp.int32(s * per + r)
            todo[1, count] = jnp.where(here, local * width + column // 8 * 8, 0)
            todo[2, count] = jnp.where(here, lax.rem(column, 8), 0)
            count = count + here.astype(jnp.int32)

    def batch(size, start):
        cells = (size * (side + 1) - 1) * PITCH
        spot = lax.broadcasted_iota(jnp.int32, (cells, 256), 0)
        gap = side * PITCH
        inside = ((spot & (PITCH - 1)) < side) & ((spot < gap) | (spot >= gap + PITCH))
        used = pl.ds(16, cells)

        def put(buf, v):
            buf[used, 0:256] = pltpu.roll(v, 1, 0).astype(BF)
            buf[used, 256:512] = v.astype(BF)
            buf[used, 512:768] = pltpu.roll(v, cells - 1, 0).astype(BF)

        def conv(buf, w):
            total = jnp.zeros((cells, 256), F32)
            for a in range(3):
                total += jnp.dot(
                    buf[a * 16 : a * 16 + cells, :],
                    w[a * 768 : a * 768 + 768, :],
                    preferred_element_type=F32,
                )
            return total

        def taps(acc, buf, grad):
            turned = grad.T.astype(BF)
            for a in range(3):
                acc[:, a * 768 : a * 768 + 768] += jnp.dot(
                    turned, buf[a * 16 : a * 16 + cells, :], preferred_element_type=F32
                )

        for buf in (xs, hs, gs):
            buf[0:16, :] = jnp.zeros((16, 768), BF)
            buf[cells + 16 : cells + 32, :] = jnp.zeros((16, 768), BF)
        for n in range(size - 1):
            vs[gap : gap + PITCH, :] = jnp.zeros((PITCH, 256), F32)
        bases, leads = [], []
        for n in range(size):
            which = todo[0, start + n]
            bases.append(pl.multiple_of(todo[1, start + n], 8))
            leads.append(todo[2, start + n])
            for s, block in enumerate(blocks):

                @pl.when(which // per == s)
                def _(block=block, n=n, which=which):
                    wide[n] = block[lax.rem(which, per)].astype(F32)

        for n in range(size):
            for i in range(side):
                got = pyr[pl.ds(pl.multiple_of(bases[n] + i * width, 8), 24), :]
                got = pltpu.roll(got, lax.rem(24 - leads[n], 24), 0)[0:16]
                at = (n * (side + 1) + i) * PITCH
                vs[at : at + 16, :] = jnp.where(in_row, got, 0.0)
        put(xs, vs[0:cells, :])
        act1, slope = gelu_pair(conv(xs, w1))
        slope1[0:cells, :] = slope
        put(hs, jnp.where(inside, act1, 0.0))
        _, slope = gelu_pair(conv(hs, w2))
        for n in range(size):
            for i in range(side):
                got = wide[n, i * side : i * side + 16, :]
                at = (n * (side + 1) + i) * PITCH
                vs[at : at + 16, :] = jnp.where(in_row, got, 0.0)
        g2 = vs[0:cells, :] * slope
        put(gs, g2)
        taps(acc2, hs, g2)
        gact1 = conv(gs, wb2)
        g1 = jnp.where(inside, gact1 * slope1[0:cells, :], 0.0)
        put(gs, g1)
        taps(acc1, xs, g1)
        vs[0:cells, :] = jnp.where(inside, conv(gs, wb1), 0.0).astype(BF).astype(F32)
        for n in range(size):
            for i in range(side):
                at = pl.ds(pl.multiple_of(bases[n] + i * width, 8), 24)
                row = (n * (side + 1) + i) * PITCH
                piece = jnp.concatenate([vs[row : row + 16, :], jnp.zeros((8, 256), F32)])
                gp[at, :] = gp[at, :] + pltpu.roll(piece, leads[n], 0)

    def one(n, carry):
        batch(1, n)
        return carry

    lax.fori_loop(0, count, one, 0)


def chunks_of(rows, chips):
    unit = 16 * chips if rows >= 32 * chips else 16
    cut = roundup(rows // 2, unit)
    return ((0, cut), (cut, rows))


def finish_part(height, width, dp, chips, acc1, acc2, gp, keep, sends, gp_own, gp_other):
    core = lax.rem(lax.axis_index("tile"), 2)
    cells = height * width
    rows = 2304 // dp
    parts = chunks_of(rows, chips)

    def write_keep(acc):
        for k in range(9):
            keep[k * 256 : k * 256 + 256, :] = acc[:, k * 256 : k * 256 + 256].T.astype(BF)

    def write_sends(acc):
        for k in range(9):
            value = acc[:, k * 256 : k * 256 + 256].T.astype(BF)
            for d in range(dp):
                for to, (lo, hi) in zip(sends, parts):
                    first = max(d * rows + lo, k * 256)
                    end = min(d * rows + hi, k * 256 + 256)
                    if first < end:
                        at = d * (hi - lo) + first - d * rows - lo
                        to[at : at + end - first, :] = value[first - k * 256 : end - k * 256, :]

    @pl.when(core == 0)
    def _():
        write_sends(acc2)
        write_keep(acc1)

    @pl.when(core == 1)
    def _():
        write_sends(acc1)
        write_keep(acc2)

    gp_own[...] = gp[pl.ds(pl.multiple_of(core * cells, cells), cells), :]
    gp_other[...] = gp[pl.ds(pl.multiple_of((1 - core) * cells, cells), cells), :].astype(BF)


def main_call(side, height, width, dp, chips, first, last, state, weights, blocks):
    n = len(blocks)
    big = 2 * height * width + 16
    cells = side * PITCH
    kept = (sds((big, 256), F32),) + (sds((2304, 256), BF),) * 4
    sums = (sds((256, 2304), F32), sds((256, 2304), F32), sds((big, 256), F32))
    ends = (
        sds((2304, 256), BF),
        *(sds((dp * (hi - lo), 256), BF) for lo, hi in chunks_of(2304 // dp, chips)),
        sds((height * width, 256), F32),
        sds((height * width, 256), BF),
    )
    outs = (kept if first else ()) + sums + (ends if last else ())
    scratch = [
        pltpu.VMEM((cells + 32, 768), BF),
        pltpu.VMEM((cells + 32, 768), BF),
        pltpu.VMEM((cells + 32, 768), BF),
        pltpu.VMEM((1, SLOT, 256), F32),
        pltpu.VMEM((cells, 256), F32),
        pltpu.VMEM((cells, 256), F32),
        pltpu.SMEM((3, 128), jnp.int32),
    ]
    extra = []
    if first:
        extra = [
            pltpu.VMEM(((2 * height + 2) * width, 768), BF),
            pltpu.VMEM((2304, 256), BF),
            pltpu.VMEM((height * width, 256), BF),
            pltpu.SemaphoreType.DMA((4,)),
        ]

    def kernel(*refs):
        refs = list(refs)

        def take(k):
            got = refs[:k]
            del refs[:k]
            return got

        state_refs = take(len(state))
        weight_refs = take(len(weights))
        block_refs = take(n)
        out_refs = take(len(outs))
        scratch_refs = take(len(scratch))
        if first:
            pyr, wb1, wb2, w1, w2 = out_refs[:5]
            acc1, acc2, gp = out_refs[5:8]
            xp, wf, own, sems = refs
            copies = [
                pltpu.make_async_copy(source, to, sems.at[k])
                for k, (source, to) in enumerate(zip((state_refs[0], *weight_refs), (own, wf, w1, w2)))
            ]
            for copy in copies:
                copy.start()
            for total in (acc1, acc2, gp):
                total[...] = jnp.zeros(total.shape, F32)
            copies[0].wait()
            pyramid_part(height, width, own, *state_refs[1:], wf, pyr, xp, copies[1])
            copies[2].wait()
            flip_part(w1, wb1)
            copies[3].wait()
            flip_part(w2, wb2)
        else:
            pyr, wb1, wb2, w1, w2 = state_refs[:5]
            acc1, acc2, gp = out_refs[:3]
        regions_part(
            side, height, width, block_refs, pyr, w1, w2, wb1, wb2, acc1, acc2, gp, scratch_refs
        )
        if last:
            keep, *sends, gp_own, gp_other = out_refs[3:]
            finish_part(height, width, dp, chips, acc1, acc2, gp, keep, sends, gp_own, gp_other)

    aliases = {} if first else {5: 0, 6: 1, 7: 2}
    return run(
        kernel,
        outs,
        [*state, *weights, *blocks],
        scratch=scratch + extra,
        aliases=aliases,
        hbm=(0, *range(len(state), len(state) + len(weights))) if first else (),
    )


def local_kernel(fn, outs, *arrays, **more):
    if isinstance(outs, tuple):
        return run(fn, outs, arrays, **more)
    return run(fn, (outs,), arrays, **more)[0]


def add(a, b):
    return (a.astype(F32) + b.astype(F32)).astype(BF)


def reduce_weights(keep, sends, core_swap, dp, chips, beside):
    rows = keep.shape[0] // dp
    bits = dp.bit_length() - 1
    orders = (list(range(bits)), list(reversed(range(bits))))
    shifts = [
        [(2 * z + c, 2 * ((z + k) % chips) + c) for z in range(chips) for c in range(2)]
        for k in range(chips)
    ]
    arrived = [lax.ppermute(send, "tile", core_swap) for send in sends]

    def split(members, bit):
        return [m for m in members if not m & bit], [m for m in members if m & bit]

    class Chunk:
        pass

    def begin(lo, hi, got):
        c = Chunk()
        c.rows = hi - lo
        low = roundup(c.rows // 2, 16)
        c.spans = ((0, low), (low, c.rows))
        c.members = [list(range(dp)), list(range(dp))]

        def first(keep_ref, got_ref, *outs):
            me = lax.axis_index("dp")
            for half in range(2):
                start, size = c.spans[half][0], c.spans[half][1] - c.spans[half][0]
                groups = split(c.members[half], 1 << orders[half][0])
                for out, group in zip(outs[2 * half : 2 * half + 2], groups):
                    for n, m in enumerate(group):
                        a = pl.ds(pl.multiple_of((me ^ m) * rows + lo + start, 16), size)
                        b = pl.ds(pl.multiple_of((me ^ m) * c.rows + start, 16), size)
                        out[n] = add(keep_ref[a, :], got_ref[b, :])

        shapes = []
        for half in range(2):
            shapes += [sds((dp // 2, c.spans[half][1] - c.spans[half][0], 256), BF)] * 2
        c.parts = local_kernel(first, tuple(shapes), keep, got)
        return c

    def exchange(c, stage):
        c.received = []
        for half in range(2):
            bit = 1 << orders[half][stage]
            pairs = [(i, i ^ bit) for i in range(dp)]
            c.received.append(lax.ppermute(c.parts[2 * half + 1], "dp", pairs))
            c.members[half] = split(c.members[half], bit)[0]

    def halve(c, stage):
        shapes = []
        for half in range(2):
            size = c.spans[half][1] - c.spans[half][0]
            shapes += [sds((len(c.members[half]) // 2, size, 256), BF)] * 2
        members = [list(m) for m in c.members]

        def kernel(p, pr, q, qr, *outs):
            for half, (mine, theirs) in enumerate(((p, pr), (q, qr))):
                groups = split(members[half], 1 << orders[half][stage])
                for out, group in zip(outs[2 * half : 2 * half + 2], groups):
                    for n, m in enumerate(group):
                        k = members[half].index(m)
                        out[n] = add(mine[k], theirs[k])

        c.parts = local_kernel(
            kernel, tuple(shapes), c.parts[0], c.received[0], c.parts[2], c.received[1]
        )

    def deal(c):
        c.share = roundup(-(-c.rows // chips), 16)
        low = c.spans[0][1]

        def kernel(p, pr, q, qr, *refs):
            outs, total = refs[:chips], refs[chips]
            chip = lax.axis_index("tile") // 2
            total[0:low, :] = add(p[0], pr[0])
            total[low : c.rows, :] = add(q[0], qr[0])
            if c.share * chips > c.rows:
                total[c.rows :, :] = jnp.zeros((c.share * chips - c.rows, 256), BF)
            for k in range(chips):
                to = lax.rem(chip + k, chips)
                outs[k][...] = total[pl.ds(pl.multiple_of(to * c.share, 16), c.share), :]

        dealt = local_kernel(
            kernel,
            tuple(sds((c.share, 256), BF) for _ in range(chips)),
            *(c.parts[0], c.received[0], c.parts[2], c.received[1]),
            scratch=[pltpu.VMEM((c.share * chips, 256), BF)],
        )
        c.mine = dealt[0]
        c.others = [lax.ppermute(dealt[k], "tile", shifts[k]) for k in range(1, chips)]

    def gather(c):
        def kernel(*refs):
            total = refs[0][...].astype(F32)
            for ref in refs[1:-1]:
                total += ref[...].astype(F32)
            refs[-1][...] = total.astype(BF)

        c.mine = local_kernel(kernel, sds((c.share, 256), BF), c.mine, *c.others)
        c.others = [lax.ppermute(c.mine, "tile", shifts[k]) for k in range(1, chips)]

    def lay(c):
        def kernel(*refs):
            chip = lax.axis_index("tile") // 2
            for k in range(chips):
                source = lax.rem(chip - k + chips, chips)
                refs[-1][pl.ds(pl.multiple_of(source * c.share, 16), c.share), :] = refs[k][...]

        c.whole = local_kernel(kernel, sds((c.share * chips, 256), BF), c.mine, *c.others)
        c.theirs = lax.ppermute(c.whole, "tile", core_swap)

    spans = chunks_of(rows, chips)
    chunks = [begin(lo, hi, got) for (lo, hi), got in zip(spans, arrived)]
    for c in chunks:
        exchange(c, 0)
    chunks[0].received[0], beside = lax.optimization_barrier((chunks[0].received[0], beside))
    for stage in range(1, bits):
        for c in chunks:
            halve(c, stage)
            exchange(c, stage)
    for step in (deal, gather, lay):
        for c in chunks:
            step(c)

    def out(*refs):
        core = lax.rem(lax.axis_index("tile"), 2)
        one, two = refs[-2:]

        def write(to, sources):
            for (lo, hi), source in zip(spans, sources):
                to[lo:hi, :] = source[0 : hi - lo, :].astype(F32)

        @pl.when(core == 0)
        def _():
            write(one, refs[0:2])
            write(two, refs[2:4])

        @pl.when(core == 1)
        def _():
            write(one, refs[2:4])
            write(two, refs[0:2])

    one, two = local_kernel(
        out,
        (sds((rows, 256), F32), sds((rows, 256), F32)),
        *(c.whole for c in chunks),
        *(c.theirs for c in chunks),
        hbm_out=(0, 1),
    )
    return one, two, beside


def body(features, fpn_weight, mask_w1, mask_w2, owner, row_off, col_off, cotangent):
    tiles = lax.axis_size("tile")
    dp = lax.axis_size("dp")
    chips = tiles // 2
    height, width, channels = features.shape[1:]
    side = cotangent.shape[2]
    swap = [(i, i ^ 1) for i in range(tiles)]

    tile = features.reshape(height * width, channels)
    regions = cotangent.shape[1]
    place = [x.reshape(1, regions) for x in (owner, row_off, col_off)]
    edge = edge_of(tile, height, width)
    rim_a = lax.ppermute(
        edge, "tile", [(i, i + 1 if i % 2 else i - 1) for i in range(1, tiles - 1)]
    )
    other = lax.ppermute(tile, "tile", swap)
    packed = pack(cotangent[0].transpose(1, 2, 0, 3), height, place)
    packed, rim_a = lax.optimization_barrier((packed, rim_a))
    rim_b = lax.ppermute(rim_a, "tile", swap)

    order = [0] + list(range(1, chips, 2)) + list(range(2, chips, 2))[::-1]
    ring = [
        (2 * z + c, 2 * order[(k + 1) % chips] + c) for k, z in enumerate(order) for c in range(2)
    ]

    flat = lambda w: w.reshape(9 * channels, channels)
    wf, w1, w2 = flat(fpn_weight), flat(mask_w1), flat(mask_w2)
    block = lax.ppermute(packed, "tile", ring)
    start = main_call(
        side, height, width, dp, chips, True, False, [tile, other, rim_a, rim_b], [wf, w1, w2], [packed]
    )
    kept, sums = list(start[:5]), list(start[5:])
    for step in range(1, chips):
        last = step == chips - 1
        held = block
        if not last:
            held, kept[0] = lax.optimization_barrier((held, kept[0]))
            block = lax.ppermute(held, "tile", ring)
        got = main_call(
            *(side, height, width, dp, chips, False, last),
            [*kept, *sums],
            [],
            [held],
        )
        sums, ends = list(got[:3]), got[3:]
        if not last:
            kept[0], sums[0] = lax.optimization_barrier((kept[0], sums[0]))
    keep, *sends, gp_own, gp_other = ends
    gp_got = lax.ppermute(gp_other, "tile", swap)

    def join(a, b, out):
        out[...] = (a[...] + b[...].astype(F32)).astype(BF)

    joined = local_kernel(
        join, sds((height * width, channels), BF), gp_own, gp_got, hbm_out=(0,)
    )
    grad_one, grad_two, grad_pyramid = reduce_weights(keep, sends, swap, dp, chips, joined)
    return grad_one, grad_two, grad_pyramid.reshape(1, height, width, channels)


def solution(mesh):
    placed = (
        P("dp", "tile", None, None),
        P(),
        P(),
        P(),
        P("dp", "tile", None),
        P("dp", "tile"),
        P("dp", "tile"),
        P("dp", "tile", None, None, None),
    )
    return jax.shard_map(
        body,
        mesh=mesh,
        in_specs=placed,
        out_specs=(P("dp", None), P("dp", None), P("dp", "tile", None, None)),
        check_vma=False,
    )
```

```python
import functools
import math

import jax
import jax.numpy as jnp
from jax import lax
from jax.experimental import pallas as pl
from jax.experimental.pallas import tpu as pltpu
from jax.sharding import PartitionSpec as P

BF = jnp.bfloat16
F32 = jnp.float32
VMEM_LIMIT = 24 * 1024 * 1024
PITCH = 16
SLOT = 208


def roundup(n, m):
    return (n + m - 1) // m * m


def run(kernel, outs, args, scratch=(), aliases=None, hbm=(), hbm_out=()):
    args = [
        pltpu.with_memory_space_constraint(x, pltpu.HBM if i in hbm else pltpu.VMEM)
        for i, x in enumerate(args)
    ]
    return pl.pallas_call(
        kernel,
        out_shape=tuple(
            s if i in hbm_out else pltpu.VMEM(s.shape, s.dtype) for i, s in enumerate(outs)
        ),
        in_specs=[
            pl.BlockSpec(memory_space=pltpu.HBM if i in hbm else pltpu.VMEM)
            for i in range(len(args))
        ],
        out_specs=tuple(pl.BlockSpec(memory_space=pltpu.VMEM) for _ in outs),
        scratch_shapes=list(scratch),
        input_output_aliases=aliases or {},
        compiler_params=pltpu.CompilerParams(vmem_limit_bytes=VMEM_LIMIT),
    )(*args)


def sds(shape, dtype):
    return jax.ShapeDtypeStruct(shape, dtype)


def edge_of(tile, height, width):
    def kernel(tile, edge, sem):
        core = lax.rem(lax.axis_index("tile"), 2)
        line = pl.ds(pl.multiple_of(core * (height - 1) * width, width), width)
        copy = pltpu.make_async_copy(tile.at[line, :], edge, sem)
        copy.start()
        copy.wait()

    return local_kernel(
        kernel, sds((width, 256), BF), tile, scratch=[pltpu.SemaphoreType.DMA], hbm=(0,)
    )


def pack_kernel(side, height, cot, owner, row, col, packed, low, high, wide, places, sems):
    regions = cot.shape[2]
    copies = [
        pltpu.make_async_copy(source, places.at[n], sems.at[n])
        for n, source in enumerate((owner, row, col))
    ]
    for copy in copies:
        copy.start()
    for i in range(side):
        for j in range(side):
            at = (i * side + j) * regions
            cell = cot[i, j].astype(F32)
            low[at : at + regions, :] = cell[:, 0:128]
            high[at : at + regions, :] = cell[:, 128:256]
    for copy in copies:
        copy.wait()
    lanes = lax.broadcasted_iota(jnp.int32, (16, 256), 1)
    rows = lax.broadcasted_iota(jnp.int32, (16, 256), 0)
    cells = side * side
    for r in range(regions):
        wide[0:cells, 0:128] = low[pl.ds(r, cells, stride=regions), :]
        wide[0:cells, 128:256] = high[pl.ds(r, cells, stride=regions), :]
        spot = (places[0, 0, r] * height + places[1, 0, r] + 1).astype(F32)
        column = places[2, 0, r].astype(F32)
        note = jnp.where(lanes == 0, spot, jnp.where(lanes == 1, column, 0.0))
        wide[192:208, :] = jnp.where(rows < cells - 192, wide[192:208, :], note)
        packed[r] = wide[...].astype(BF)


def pack(cotangent, height, place):
    side, regions = cotangent.shape[0], cotangent.shape[2]
    return local_kernel(
        functools.partial(pack_kernel, side, height),
        sds((regions, SLOT, 256), BF),
        cotangent,
        *place,
        scratch=[
            pltpu.VMEM((side * side * regions, 128), F32),
            pltpu.VMEM((side * side * regions, 128), F32),
            pltpu.VMEM((SLOT, 256), F32),
            pltpu.SMEM((3, 1, regions), jnp.int32),
            pltpu.SemaphoreType.DMA((3,)),
        ],
        hbm=(1, 2, 3),
    )


def pyramid_part(height, width, own, other, rim_a, rim_b, wf, pyr, xp, fetched):
    core = lax.rem(lax.axis_index("tile"), 2)
    cells = height * width
    col = lax.broadcasted_iota(jnp.int32, (width, 256), 0)

    def fill(src, count, where):
        def step(t, carry):
            v = src[pl.ds(pl.multiple_of(t * width, width), width), :].astype(F32)
            to = pl.ds(pl.multiple_of(where + t * width, width), width)
            xp[to, 0:256] = jnp.where(col == 0, 0.0, pltpu.roll(v, 1, 0)).astype(BF)
            xp[to, 256:512] = v.astype(BF)
            xp[to, 512:768] = jnp.where(
                col == width - 1, 0.0, pltpu.roll(v, width - 1, 0)
            ).astype(BF)
            return carry

        lax.fori_loop(0, count, step, 0)

    bottom = width + 2 * cells
    fill(own, height, width + core * cells)
    fill(other, height, width + (1 - core) * cells)
    fill(rim_a, 1, core * bottom)
    fill(rim_b, 1, (1 - core) * bottom)

    fetched.wait()

    def conv(t, carry):
        at = t * 256
        total = jnp.zeros((256, 256), F32)
        for a in range(3):
            piece = xp[pl.ds(pl.multiple_of(at + a * width, 64), 256), :]
            total += jnp.dot(piece, wf[a * 768 : a * 768 + 768, :], preferred_element_type=F32)
        pyr[pl.ds(pl.multiple_of(at, 256), 256), :] = total.astype(BF).astype(F32)
        return carry

    lax.fori_loop(0, 2 * cells // 256, conv, 0)
    pyr[2 * cells : 2 * cells + 16, :] = jnp.zeros((16, 256), F32)


def flip_part(w, wb):
    for k in range(9):
        block = w[(8 - k) * 256 : (9 - k) * 256, :].astype(F32)
        wb[k * 256 : k * 256 + 256, :] = block.T.astype(BF)


def gelu_pair(v):
    c = math.sqrt(2.0 / math.pi)
    sq = v * v
    t = jnp.tanh(c * (v + 0.044715 * (sq * v)))
    half = 0.5 * (1.0 + t)
    slope = half + 0.5 * v * (1.0 - t * t) * (c * (1.0 + 3 * 0.044715 * sq))
    return v * half, slope


def regions_part(side, height, width, blocks, pyr, w1, w2, wb1, wb2, acc1, acc2, gp, scratch):
    xs, hs, gs, wide, vs, slope1, todo = scratch
    chip = lax.axis_index("tile") // 2
    lanes = lax.broadcasted_iota(jnp.int32, (16, 256), 1)
    rows16 = lax.broadcasted_iota(jnp.int32, (16, 256), 0)
    in_row = rows16 < side
    per = blocks[0].shape[0]

    count = jnp.int32(0)
    for s, block in enumerate(blocks):
        for r in range(per):
            note = block[r, 192:208, :].astype(F32)
            note = jnp.where(rows16 == 15, note, 0.0)
            spot = jnp.sum(jnp.where(lanes == 0, note, 0.0)).astype(jnp.int32) - 1
            column = jnp.sum(jnp.where(lanes == 1, note, 0.0)).astype(jnp.int32)
            local = spot - chip * 2 * height
            here = (spot >= 0) & (local >= 0) & (local < 2 * height)
            todo[0, count] = jnp.int32(s * per + r)
            todo[1, count] = jnp.where(here, local * width + column // 8 * 8, 0)
            todo[2, count] = jnp.where(here, lax.rem(column, 8), 0)
            count = count + here.astype(jnp.int32)

    def batch(size, start):
        cells = (size * (side + 1) - 1) * PITCH
        spot = lax.broadcasted_iota(jnp.int32, (cells, 256), 0)
        gap = side * PITCH
        inside = ((spot & (PITCH - 1)) < side) & ((spot < gap) | (spot >= gap + PITCH))
        used = pl.ds(16, cells)

        def put(buf, v):
            buf[used, 0:256] = pltpu.roll(v, 1, 0).astype(BF)
            buf[used, 256:512] = v.astype(BF)
            buf[used, 512:768] = pltpu.roll(v, cells - 1, 0).astype(BF)

        def conv(buf, w):
            total = jnp.zeros((cells, 256), F32)
            for a in range(3):
                total += jnp.dot(
                    buf[a * 16 : a * 16 + cells, :],
                    w[a * 768 : a * 768 + 768, :],
                    preferred_element_type=F32,
                )
            return total

        def taps(acc, buf, grad):
            turned = grad.T.astype(BF)
            for a in range(3):
                acc[:, a * 768 : a * 768 + 768] += jnp.dot(
                    turned, buf[a * 16 : a * 16 + cells, :], preferred_element_type=F32
                )

        for buf in (xs, hs, gs):
            buf[0:16, :] = jnp.zeros((16, 768), BF)
            buf[cells + 16 : cells + 32, :] = jnp.zeros((16, 768), BF)
        for n in range(size - 1):
            vs[gap : gap + PITCH, :] = jnp.zeros((PITCH, 256), F32)
        bases, leads = [], []
        for n in range(size):
            which = todo[0, start + n]
            bases.append(pl.multiple_of(todo[1, start + n], 8))
            leads.append(todo[2, start + n])
            for s, block in enumerate(blocks):

                @pl.when(which // per == s)
                def _(block=block, n=n, which=which):
                    wide[n] = block[lax.rem(which, per)].astype(F32)

        for n in range(size):
            for i in range(side):
                got = pyr[pl.ds(pl.multiple_of(bases[n] + i * width, 8), 24), :]
                got = pltpu.roll(got, lax.rem(24 - leads[n], 24), 0)[0:16]
                at = (n * (side + 1) + i) * PITCH
                vs[at : at + 16, :] = jnp.where(in_row, got, 0.0)
        put(xs, vs[0:cells, :])
        act1, slope = gelu_pair(conv(xs, w1))
        slope1[0:cells, :] = slope
        put(hs, jnp.where(inside, act1, 0.0))
        _, slope = gelu_pair(conv(hs, w2))
        for n in range(size):
            for i in range(side):
                got = wide[n, i * side : i * side + 16, :]
                at = (n * (side + 1) + i) * PITCH
                vs[at : at + 16, :] = jnp.where(in_row, got, 0.0)
        g2 = vs[0:cells, :] * slope
        put(gs, g2)
        taps(acc2, hs, g2)
        gact1 = conv(gs, wb2)
        g1 = jnp.where(inside, gact1 * slope1[0:cells, :], 0.0)
        put(gs, g1)
        taps(acc1, xs, g1)
        vs[0:cells, :] = jnp.where(inside, conv(gs, wb1), 0.0).astype(BF).astype(F32)
        for n in range(size):
            for i in range(side):
                at = pl.ds(pl.multiple_of(bases[n] + i * width, 8), 24)
                row = (n * (side + 1) + i) * PITCH
                piece = jnp.concatenate([vs[row : row + 16, :], jnp.zeros((8, 256), F32)])
                gp[at, :] = gp[at, :] + pltpu.roll(piece, leads[n], 0)

    def one(n, carry):
        batch(1, n)
        return carry

    lax.fori_loop(0, count, one, 0)


def chunks_of(rows):
    return ((0, rows),)


def finish_part(height, width, dp, chips, acc1, acc2, gp, keep, sends, gp_own, gp_other):
    core = lax.rem(lax.axis_index("tile"), 2)
    cells = height * width
    rows = 2304 // dp
    parts = chunks_of(rows)

    def write_keep(acc):
        for k in range(9):
            keep[k * 256 : k * 256 + 256, :] = acc[:, k * 256 : k * 256 + 256].T.astype(BF)

    def write_sends(acc):
        for k in range(9):
            value = acc[:, k * 256 : k * 256 + 256].T.astype(BF)
            for d in range(dp):
                for to, (lo, hi) in zip(sends, parts):
                    first = max(d * rows + lo, k * 256)
                    end = min(d * rows + hi, k * 256 + 256)
                    if first < end:
                        at = d * (hi - lo) + first - d * rows - lo
                        to[at : at + end - first, :] = value[first - k * 256 : end - k * 256, :]

    @pl.when(core == 0)
    def _():
        write_sends(acc2)
        write_keep(acc1)

    @pl.when(core == 1)
    def _():
        write_sends(acc1)
        write_keep(acc2)

    gp_own[...] = gp[pl.ds(pl.multiple_of(core * cells, cells), cells), :]
    gp_other[...] = gp[pl.ds(pl.multiple_of((1 - core) * cells, cells), cells), :].astype(BF)


def main_call(side, height, width, dp, chips, first, last, state, weights, blocks):
    n = len(blocks)
    big = 2 * height * width + 16
    cells = side * PITCH
    kept = (sds((big, 256), F32),) + (sds((2304, 256), BF),) * 4
    sums = (sds((256, 2304), F32), sds((256, 2304), F32), sds((big, 256), F32))
    ends = (
        sds((2304, 256), BF),
        *(sds((dp * (hi - lo), 256), BF) for lo, hi in chunks_of(2304 // dp)),
        sds((height * width, 256), F32),
        sds((height * width, 256), BF),
    )
    outs = (kept if first else ()) + sums + (ends if last else ())
    scratch = [
        pltpu.VMEM((cells + 32, 768), BF),
        pltpu.VMEM((cells + 32, 768), BF),
        pltpu.VMEM((cells + 32, 768), BF),
        pltpu.VMEM((1, SLOT, 256), F32),
        pltpu.VMEM((cells, 256), F32),
        pltpu.VMEM((cells, 256), F32),
        pltpu.SMEM((3, 128), jnp.int32),
    ]
    extra = []
    if first:
        extra = [
            pltpu.VMEM(((2 * height + 2) * width, 768), BF),
            pltpu.VMEM((2304, 256), BF),
            pltpu.VMEM((height * width, 256), BF),
            pltpu.SemaphoreType.DMA((4,)),
        ]

    def kernel(*refs):
        refs = list(refs)

        def take(k):
            got = refs[:k]
            del refs[:k]
            return got

        state_refs = take(len(state))
        weight_refs = take(len(weights))
        block_refs = take(n)
        out_refs = take(len(outs))
        scratch_refs = take(len(scratch))
        if first:
            pyr, wb1, wb2, w1, w2 = out_refs[:5]
            acc1, acc2, gp = out_refs[5:8]
            xp, wf, own, sems = refs
            copies = [
                pltpu.make_async_copy(source, to, sems.at[k])
                for k, (source, to) in enumerate(zip((state_refs[0], *weight_refs), (own, wf, w1, w2)))
            ]
            for copy in copies:
                copy.start()
            for total in (acc1, acc2, gp):
                total[...] = jnp.zeros(total.shape, F32)
            copies[0].wait()
            pyramid_part(height, width, own, *state_refs[1:], wf, pyr, xp, copies[1])
            copies[2].wait()
            flip_part(w1, wb1)
            copies[3].wait()
            flip_part(w2, wb2)
        else:
            pyr, wb1, wb2, w1, w2 = state_refs[:5]
            acc1, acc2, gp = out_refs[:3]
        regions_part(
            side, height, width, block_refs, pyr, w1, w2, wb1, wb2, acc1, acc2, gp, scratch_refs
        )
        if last:
            keep, *sends, gp_own, gp_other = out_refs[3:]
            finish_part(height, width, dp, chips, acc1, acc2, gp, keep, sends, gp_own, gp_other)

    aliases = {} if first else {5: 0, 6: 1, 7: 2}
    return run(
        kernel,
        outs,
        [*state, *weights, *blocks],
        scratch=scratch + extra,
        aliases=aliases,
        hbm=(0, *range(len(state), len(state) + len(weights))) if first else (),
    )


def local_kernel(fn, outs, *arrays, **more):
    if isinstance(outs, tuple):
        return run(fn, outs, arrays, **more)
    return run(fn, (outs,), arrays, **more)[0]


def add(a, b):
    return (a.astype(F32) + b.astype(F32)).astype(BF)


def reduce_weights(keep, sends, core_swap, dp, chips, beside):
    rows = keep.shape[0] // dp
    bits = dp.bit_length() - 1
    orders = (list(range(bits)), list(reversed(range(bits))))
    shifts = [
        [(2 * z + c, 2 * ((z + k) % chips) + c) for z in range(chips) for c in range(2)]
        for k in range(chips)
    ]
    arrived = [lax.ppermute(send, "tile", core_swap) for send in sends]

    def split(members, bit):
        return [m for m in members if not m & bit], [m for m in members if m & bit]

    class Chunk:
        pass

    def begin(lo, hi, got):
        c = Chunk()
        c.rows = hi - lo
        low = roundup(c.rows // 2, 16)
        c.spans = ((0, low), (low, c.rows))
        c.members = [list(range(dp)), list(range(dp))]

        def first(keep_ref, got_ref, *outs):
            me = lax.axis_index("dp")
            for half in range(2):
                start, size = c.spans[half][0], c.spans[half][1] - c.spans[half][0]
                groups = split(c.members[half], 1 << orders[half][0])
                for out, group in zip(outs[2 * half : 2 * half + 2], groups):
                    for n, m in enumerate(group):
                        a = pl.ds(pl.multiple_of((me ^ m) * rows + lo + start, 16), size)
                        b = pl.ds(pl.multiple_of((me ^ m) * c.rows + start, 16), size)
                        out[n] = add(keep_ref[a, :], got_ref[b, :])

        shapes = []
        for half in range(2):
            shapes += [sds((dp // 2, c.spans[half][1] - c.spans[half][0], 256), BF)] * 2
        c.parts = local_kernel(first, tuple(shapes), keep, got)
        return c

    def exchange(c, stage):
        c.received = []
        for half in range(2):
            bit = 1 << orders[half][stage]
            pairs = [(i, i ^ bit) for i in range(dp)]
            c.received.append(lax.ppermute(c.parts[2 * half + 1], "dp", pairs))
            c.members[half] = split(c.members[half], bit)[0]

    def halve(c, stage):
        shapes = []
        for half in range(2):
            size = c.spans[half][1] - c.spans[half][0]
            shapes += [sds((len(c.members[half]) // 2, size, 256), BF)] * 2
        members = [list(m) for m in c.members]

        def kernel(p, pr, q, qr, *outs):
            for half, (mine, theirs) in enumerate(((p, pr), (q, qr))):
                groups = split(members[half], 1 << orders[half][stage])
                for out, group in zip(outs[2 * half : 2 * half + 2], groups):
                    for n, m in enumerate(group):
                        k = members[half].index(m)
                        out[n] = add(mine[k], theirs[k])

        c.parts = local_kernel(
            kernel, tuple(shapes), c.parts[0], c.received[0], c.parts[2], c.received[1]
        )

    def deal(c):
        c.share = roundup(-(-c.rows // chips), 16)
        low = c.spans[0][1]

        def kernel(p, pr, q, qr, *refs):
            outs, total = refs[:chips], refs[chips]
            chip = lax.axis_index("tile") // 2
            total[0:low, :] = add(p[0], pr[0])
            total[low : c.rows, :] = add(q[0], qr[0])
            if c.share * chips > c.rows:
                total[c.rows :, :] = jnp.zeros((c.share * chips - c.rows, 256), BF)
            for k in range(chips):
                to = lax.rem(chip + k, chips)
                outs[k][...] = total[pl.ds(pl.multiple_of(to * c.share, 16), c.share), :]

        dealt = local_kernel(
            kernel,
            tuple(sds((c.share, 256), BF) for _ in range(chips)),
            *(c.parts[0], c.received[0], c.parts[2], c.received[1]),
            scratch=[pltpu.VMEM((c.share * chips, 256), BF)],
        )
        c.mine = dealt[0]
        c.others = [lax.ppermute(dealt[k], "tile", shifts[k]) for k in range(1, chips)]

    def gather(c):
        def kernel(*refs):
            total = refs[0][...].astype(F32)
            for ref in refs[1:-1]:
                total += ref[...].astype(F32)
            refs[-1][...] = total.astype(BF)

        c.mine = local_kernel(kernel, sds((c.share, 256), BF), c.mine, *c.others)
        c.others = [lax.ppermute(c.mine, "tile", shifts[k]) for k in range(1, chips)]

    def lay(c):
        def kernel(*refs):
            chip = lax.axis_index("tile") // 2
            for k in range(chips):
                source = lax.rem(chip - k + chips, chips)
                refs[-1][pl.ds(pl.multiple_of(source * c.share, 16), c.share), :] = refs[k][...]

        c.whole = local_kernel(kernel, sds((c.share * chips, 256), BF), c.mine, *c.others)
        c.theirs = lax.ppermute(c.whole, "tile", core_swap)

    spans = chunks_of(rows)
    chunks = [begin(lo, hi, got) for (lo, hi), got in zip(spans, arrived)]
    for c in chunks:
        exchange(c, 0)
    chunks[0].received[0], beside = lax.optimization_barrier((chunks[0].received[0], beside))
    for stage in range(1, bits):
        for c in chunks:
            halve(c, stage)
            exchange(c, stage)
    for step in (deal, gather, lay):
        for c in chunks:
            step(c)

    def out(*refs):
        core = lax.rem(lax.axis_index("tile"), 2)
        one, two = refs[-2:]

        def write(to, sources):
            for (lo, hi), source in zip(spans, sources):
                to[lo:hi, :] = source[0 : hi - lo, :].astype(F32)

        @pl.when(core == 0)
        def _():
            write(one, refs[0 : len(spans)])
            write(two, refs[len(spans) : -2])

        @pl.when(core == 1)
        def _():
            write(one, refs[len(spans) : -2])
            write(two, refs[0 : len(spans)])

    one, two = local_kernel(
        out,
        (sds((rows, 256), F32), sds((rows, 256), F32)),
        *(c.whole for c in chunks),
        *(c.theirs for c in chunks),
        hbm_out=(0, 1),
    )
    return one, two, beside


def body(features, fpn_weight, mask_w1, mask_w2, owner, row_off, col_off, cotangent):
    tiles = lax.axis_size("tile")
    dp = lax.axis_size("dp")
    chips = tiles // 2
    height, width, channels = features.shape[1:]
    side = cotangent.shape[2]
    swap = [(i, i ^ 1) for i in range(tiles)]

    tile = features.reshape(height * width, channels)
    regions = cotangent.shape[1]
    place = [x.reshape(1, regions) for x in (owner, row_off, col_off)]
    edge = edge_of(tile, height, width)
    rim_a = lax.ppermute(
        edge, "tile", [(i, i + 1 if i % 2 else i - 1) for i in range(1, tiles - 1)]
    )
    other = lax.ppermute(tile, "tile", swap)
    packed = pack(cotangent[0].transpose(1, 2, 0, 3), height, place)
    packed, rim_a = lax.optimization_barrier((packed, rim_a))
    rim_b = lax.ppermute(rim_a, "tile", swap)

    order = [0] + list(range(1, chips, 2)) + list(range(2, chips, 2))[::-1]
    ring = [
        (2 * z + c, 2 * order[(k + 1) % chips] + c) for k, z in enumerate(order) for c in range(2)
    ]

    flat = lambda w: w.reshape(9 * channels, channels)
    wf, w1, w2 = flat(fpn_weight), flat(mask_w1), flat(mask_w2)
    block = lax.ppermute(packed, "tile", ring)
    start = main_call(
        side, height, width, dp, chips, True, False, [tile, other, rim_a, rim_b], [wf, w1, w2], [packed]
    )
    kept, sums = list(start[:5]), list(start[5:])
    for step in range(1, chips):
        last = step == chips - 1
        held = block
        if not last:
            held, kept[0] = lax.optimization_barrier((held, kept[0]))
            block = lax.ppermute(held, "tile", ring)
        got = main_call(
            *(side, height, width, dp, chips, False, last),
            [*kept, *sums],
            [],
            [held],
        )
        sums, ends = list(got[:3]), got[3:]
        if not last:
            kept[0], sums[0] = lax.optimization_barrier((kept[0], sums[0]))
    keep, *sends, gp_own, gp_other = ends
    gp_got = lax.ppermute(gp_other, "tile", swap)

    def join(a, b, out):
        out[...] = (a[...] + b[...].astype(F32)).astype(BF)

    joined = local_kernel(
        join, sds((height * width, channels), BF), gp_own, gp_got, hbm_out=(0,)
    )
    grad_one, grad_two, grad_pyramid = reduce_weights(keep, sends, swap, dp, chips, joined)
    return grad_one, grad_two, grad_pyramid.reshape(1, height, width, channels)


def solution(mesh):
    placed = (
        P("dp", "tile", None, None),
        P(),
        P(),
        P(),
        P("dp", "tile", None),
        P("dp", "tile"),
        P("dp", "tile"),
        P("dp", "tile", None, None, None),
    )
    return jax.shard_map(
        body,
        mesh=mesh,
        in_specs=placed,
        out_specs=(P("dp", None), P("dp", None), P("dp", "tile", None, None)),
        check_vma=False,
    )
```

```python
import functools
import math

import jax
import jax.numpy as jnp
from jax import lax
from jax.experimental import pallas as pl
from jax.experimental.pallas import tpu as pltpu
from jax.sharding import PartitionSpec as P

BF = jnp.bfloat16
F32 = jnp.float32
VMEM_LIMIT = 24 * 1024 * 1024
PITCH = 16
SLOT = 208


def roundup(n, m):
    return (n + m - 1) // m * m


def run(kernel, outs, args, scratch=(), aliases=None, hbm=(), hbm_out=()):
    args = [
        pltpu.with_memory_space_constraint(x, pltpu.HBM if i in hbm else pltpu.VMEM)
        for i, x in enumerate(args)
    ]
    return pl.pallas_call(
        kernel,
        out_shape=tuple(
            s if i in hbm_out else pltpu.VMEM(s.shape, s.dtype) for i, s in enumerate(outs)
        ),
        in_specs=[
            pl.BlockSpec(memory_space=pltpu.HBM if i in hbm else pltpu.VMEM)
            for i in range(len(args))
        ],
        out_specs=tuple(pl.BlockSpec(memory_space=pltpu.VMEM) for _ in outs),
        scratch_shapes=list(scratch),
        input_output_aliases=aliases or {},
        compiler_params=pltpu.CompilerParams(vmem_limit_bytes=VMEM_LIMIT),
    )(*args)


def sds(shape, dtype):
    return jax.ShapeDtypeStruct(shape, dtype)


def edge_of(tile, height, width):
    def kernel(tile, edge, sem):
        core = lax.rem(lax.axis_index("tile"), 2)
        line = pl.ds(pl.multiple_of(core * (height - 1) * width, width), width)
        copy = pltpu.make_async_copy(tile.at[line, :], edge, sem)
        copy.start()
        copy.wait()

    return local_kernel(
        kernel, sds((width, 256), BF), tile, scratch=[pltpu.SemaphoreType.DMA], hbm=(0,)
    )


def pack_kernel(side, height, cot, owner, row, col, packed, notes, low, high, wide, places, sems):
    regions = cot.shape[2]
    copies = [
        pltpu.make_async_copy(source, places.at[n], sems.at[n])
        for n, source in enumerate((owner, row, col))
    ]
    for copy in copies:
        copy.start()
    for i in range(side):
        for j in range(side):
            at = (i * side + j) * regions
            cell = cot[i, j].astype(F32)
            low[at : at + regions, :] = cell[:, 0:128]
            high[at : at + regions, :] = cell[:, 128:256]
    for copy in copies:
        copy.wait()
    lanes = lax.broadcasted_iota(jnp.int32, (16, 256), 1)
    rows = lax.broadcasted_iota(jnp.int32, (16, 256), 0)
    cells = side * side
    for r in range(regions):
        wide[0:cells, 0:128] = low[pl.ds(r, cells, stride=regions), :]
        wide[0:cells, 128:256] = high[pl.ds(r, cells, stride=regions), :]
        spot = (places[0, 0, r] * height + places[1, 0, r] + 1).astype(F32)
        column = places[2, 0, r].astype(F32)
        note = jnp.where(lanes == 0, spot, jnp.where(lanes == 1, column, 0.0))
        wide[192:208, :] = jnp.where(rows < cells - 192, wide[192:208, :], note)
        packed[r] = wide[...].astype(BF)
        notes[r] = note.astype(BF)


def pack(cotangent, height, place):
    side, regions = cotangent.shape[0], cotangent.shape[2]
    return local_kernel(
        functools.partial(pack_kernel, side, height),
        (sds((regions, SLOT, 256), BF), sds((regions, 16, 256), BF)),
        cotangent,
        *place,
        scratch=[
            pltpu.VMEM((side * side * regions, 128), F32),
            pltpu.VMEM((side * side * regions, 128), F32),
            pltpu.VMEM((SLOT, 256), F32),
            pltpu.SMEM((3, 1, regions), jnp.int32),
            pltpu.SemaphoreType.DMA((3,)),
        ],
        hbm=(1, 2, 3),
    )


def pyramid_part(height, width, own, other, rim_a, rim_b, wf, pyr, xp, fetched):
    core = lax.rem(lax.axis_index("tile"), 2)
    cells = height * width
    col = lax.broadcasted_iota(jnp.int32, (width, 256), 0)

    def fill(src, count, where):
        def step(t, carry):
            v = src[pl.ds(pl.multiple_of(t * width, width), width), :].astype(F32)
            to = pl.ds(pl.multiple_of(where + t * width, width), width)
            xp[to, 0:256] = jnp.where(col == 0, 0.0, pltpu.roll(v, 1, 0)).astype(BF)
            xp[to, 256:512] = v.astype(BF)
            xp[to, 512:768] = jnp.where(
                col == width - 1, 0.0, pltpu.roll(v, width - 1, 0)
            ).astype(BF)
            return carry

        lax.fori_loop(0, count, step, 0)

    bottom = width + 2 * cells
    fill(own, height, width + core * cells)
    fill(other, height, width + (1 - core) * cells)
    fill(rim_a, 1, core * bottom)
    fill(rim_b, 1, (1 - core) * bottom)

    fetched.wait()

    def conv(t, carry):
        at = t * 256
        total = jnp.zeros((256, 256), F32)
        for a in range(3):
            piece = xp[pl.ds(pl.multiple_of(at + a * width, 64), 256), :]
            total += jnp.dot(piece, wf[a * 768 : a * 768 + 768, :], preferred_element_type=F32)
        pyr[pl.ds(pl.multiple_of(at, 256), 256), :] = total.astype(BF).astype(F32)
        return carry

    lax.fori_loop(0, 2 * cells // 256, conv, 0)
    pyr[2 * cells : 2 * cells + 16, :] = jnp.zeros((16, 256), F32)


def flip_part(w, wb):
    for k in range(9):
        block = w[(8 - k) * 256 : (9 - k) * 256, :].astype(F32)
        wb[k * 256 : k * 256 + 256, :] = block.T.astype(BF)


def gelu_pair(v):
    c = math.sqrt(2.0 / math.pi)
    sq = v * v
    t = jnp.tanh(c * (v + 0.044715 * (sq * v)))
    half = 0.5 * (1.0 + t)
    slope = half + 0.5 * v * (1.0 - t * t) * (c * (1.0 + 3 * 0.044715 * sq))
    return v * half, slope


def regions_part(side, height, width, plan, blocks, early, stash, tables, sums, scratch):
    pyr, wb1, wb2, w1, w2 = tables
    acc1, acc2, gp = sums
    xs, hs, gs, wide, vs, slope1, todo = scratch
    chip = lax.axis_index("tile") // 2
    lanes = lax.broadcasted_iota(jnp.int32, (16, 256), 1)
    rows16 = lax.broadcasted_iota(jnp.int32, (16, 256), 0)
    in_row = rows16 < side
    cells = side * PITCH
    inside = (lax.broadcasted_iota(jnp.int32, (cells, 256), 0) & (PITCH - 1)) < side
    used = pl.ds(16, cells)
    per = (blocks or early)[0].shape[0]
    tail = pl.ds(192, 16)

    count = jnp.int32(0)
    start, end = jnp.int32(0), jnp.int32(0)

    def enlist(s, r, note):
        note = jnp.where(rows16 == 15, note.astype(F32), 0.0)
        spot = jnp.sum(jnp.where(lanes == 0, note, 0.0)).astype(jnp.int32) - 1
        column = jnp.sum(jnp.where(lanes == 1, note, 0.0)).astype(jnp.int32)
        local = spot - chip * 2 * height
        here = (spot >= 0) & (local >= 0) & (local < 2 * height)
        todo[0, count] = jnp.int32(s * per + r)
        todo[1, count] = jnp.where(here, local * width + column // 8 * 8, 0)
        todo[2, count] = jnp.where(here, lax.rem(column, 8), 0)
        return count + here.astype(jnp.int32)

    for s, block in enumerate(blocks):
        for r in range(per):
            count = enlist(s, r, block[r, tail, :])
        most = plan[s]
        start, end = end, count if most is None else jnp.minimum(count, end + most)
    total = count
    for block in early:
        for r in range(per):
            count = enlist(len(blocks), r, block[r])

    for buf in (xs, hs, gs):
        buf[0:16, :] = jnp.zeros((16, 768), BF)
        buf[cells + 16 : cells + 32, :] = jnp.zeros((16, 768), BF)

    def put(buf, v):
        buf[used, 0:256] = pltpu.roll(v, 1, 0).astype(BF)
        buf[used, 256:512] = v.astype(BF)
        buf[used, 512:768] = pltpu.roll(v, cells - 1, 0).astype(BF)

    def conv(buf, w):
        total = jnp.zeros((cells, 256), F32)
        for a in range(3):
            total += jnp.dot(
                buf[a * 16 : a * 16 + cells, :],
                w[a * 768 : a * 768 + 768, :],
                preferred_element_type=F32,
            )
        return total

    def taps(acc, buf, grad):
        turned = grad.T.astype(BF)
        for a in range(3):
            acc[:, a * 768 : a * 768 + 768] += jnp.dot(
                turned, buf[a * 16 : a * 16 + cells, :], preferred_element_type=F32
            )

    def crop(n):
        base, lead = todo[1, n], todo[2, n]
        for i in range(side):
            got = pyr[pl.ds(pl.multiple_of(base + i * width, 8), 24), :]
            got = pltpu.roll(got, lax.rem(24 - lead, 24), 0)[0:16]
            vs[i * 16 : i * 16 + 16, :] = jnp.where(in_row, got, 0.0)
        put(xs, vs[...])

    def forward(n):
        crop(n)
        act1, slope = gelu_pair(conv(xs, w1))
        slope1[...] = slope
        act1 = jnp.where(inside, act1, 0.0)
        put(hs, act1)
        _, slope = gelu_pair(conv(hs, w2))
        return act1, slope

    def backward(n, slope2):
        which = todo[0, n]
        base, lead = todo[1, n], todo[2, n]
        for s, block in enumerate(blocks):

            @pl.when(which // per == s)
            def _(block=block):
                wide[...] = block[lax.rem(which, per)].astype(F32)

        for i in range(side):
            got = wide[i * side : i * side + 16, :]
            vs[i * 16 : i * 16 + 16, :] = jnp.where(in_row, got, 0.0)
        g2 = vs[...] * slope2
        put(gs, g2)
        taps(acc2, hs, g2)
        g1 = jnp.where(inside, conv(gs, wb2) * slope1[...], 0.0)
        put(gs, g1)
        taps(acc1, xs, g1)
        vs[...] = jnp.where(inside, conv(gs, wb1), 0.0).astype(BF).astype(F32)
        for i in range(side):
            at = pl.ds(pl.multiple_of(base + i * width, 8), 24)
            piece = jnp.concatenate([vs[i * 16 : i * 16 + 16, :], jnp.zeros((8, 256), F32)])
            gp[at, :] = gp[at, :] + pltpu.roll(piece, lead, 0)

    def whole(n, carry):
        _, slope2 = forward(n)
        backward(n, slope2)
        return carry

    def ahead(n, carry):
        r = lax.rem(todo[0, n], per)
        act1, slope2 = forward(n)
        stash[0][r] = act1.astype(BF)
        stash[1][r] = slope1[...]
        stash[2][r] = slope2
        return carry

    def behind(n, carry):
        r = lax.rem(todo[0, n], per)
        crop(n)
        put(hs, stash[0][r].astype(F32))
        slope1[...] = stash[1][r]
        backward(n, stash[2][r])
        return carry

    if early:
        lax.fori_loop(start, end, whole, 0)
        lax.fori_loop(total, count, ahead, 0)
    elif stash:
        lax.fori_loop(0, total, behind, 0)
    else:
        lax.fori_loop(start, end, whole, 0)


def chunks_of(rows):
    return ((0, rows),)


def finish_part(height, width, dp, chips, acc1, acc2, gp, keep, sends, gp_own, gp_other):
    core = lax.rem(lax.axis_index("tile"), 2)
    cells = height * width
    rows = 2304 // dp
    parts = chunks_of(rows)

    def write_keep(acc):
        for k in range(9):
            keep[k * 256 : k * 256 + 256, :] = acc[:, k * 256 : k * 256 + 256].T.astype(BF)

    def write_sends(acc):
        for k in range(9):
            value = acc[:, k * 256 : k * 256 + 256].T.astype(BF)
            for d in range(dp):
                for to, (lo, hi) in zip(sends, parts):
                    first = max(d * rows + lo, k * 256)
                    end = min(d * rows + hi, k * 256 + 256)
                    if first < end:
                        at = d * (hi - lo) + first - d * rows - lo
                        to[at : at + end - first, :] = value[first - k * 256 : end - k * 256, :]

    @pl.when(core == 0)
    def _():
        write_sends(acc2)
        write_keep(acc1)

    @pl.when(core == 1)
    def _():
        write_sends(acc1)
        write_keep(acc2)

    gp_own[...] = gp[pl.ds(pl.multiple_of(core * cells, cells), cells), :]
    gp_other[...] = gp[pl.ds(pl.multiple_of((1 - core) * cells, cells), cells), :].astype(BF)


def main_call(side, height, width, dp, chips, first, last, plan, state, weights, blocks, early, stash):
    n = len(blocks)
    big = 2 * height * width + 16
    cells = side * PITCH
    kept = (sds((big, 256), F32),) + (sds((2304, 256), BF),) * 4
    sums = (sds((256, 2304), F32), sds((256, 2304), F32), sds((big, 256), F32))
    ends = (
        sds((2304, 256), BF),
        *(sds((dp * (hi - lo), 256), BF) for lo, hi in chunks_of(2304 // dp)),
        sds((height * width, 256), F32),
        sds((height * width, 256), BF),
    )
    per = blocks[0].shape[0]
    stashed = (
        sds((per, cells, 256), BF),
        sds((per, cells, 256), F32),
        sds((per, cells, 256), F32),
    )
    outs = (kept if first else ()) + sums + (ends if last else ()) + (stashed if early else ())
    scratch = [
        pltpu.VMEM((cells + 32, 768), BF),
        pltpu.VMEM((cells + 32, 768), BF),
        pltpu.VMEM((cells + 32, 768), BF),
        pltpu.VMEM((SLOT, 256), F32),
        pltpu.VMEM((cells, 256), F32),
        pltpu.VMEM((cells, 256), F32),
        pltpu.SMEM((3, 256), jnp.int32),
    ]
    extra = []
    if first:
        extra = [
            pltpu.VMEM(((2 * height + 2) * width, 768), BF),
            pltpu.VMEM((2304, 256), BF),
            pltpu.VMEM((height * width, 256), BF),
            pltpu.SemaphoreType.DMA((4,)),
        ]

    def kernel(*refs):
        refs = list(refs)

        def take(k):
            got = refs[:k]
            del refs[:k]
            return got

        state_refs = take(len(state))
        weight_refs = take(len(weights))
        block_refs = take(n)
        early_refs = take(len(early))
        stash_refs = take(len(stash))
        out_refs = take(len(outs))
        if early:
            stash_refs = out_refs[-3:]
        scratch_refs = take(len(scratch))
        if first:
            pyr, wb1, wb2, w1, w2 = out_refs[:5]
            acc1, acc2, gp = out_refs[5:8]
            xp, wf, own, sems = refs
            copies = [
                pltpu.make_async_copy(source, to, sems.at[k])
                for k, (source, to) in enumerate(zip((state_refs[0], *weight_refs), (own, wf, w1, w2)))
            ]
            for copy in copies:
                copy.start()
            for total in (acc1, acc2, gp):
                total[...] = jnp.zeros(total.shape, F32)
            copies[0].wait()
            pyramid_part(height, width, own, *state_refs[1:], wf, pyr, xp, copies[1])
            copies[2].wait()
            flip_part(w1, wb1)
            copies[3].wait()
            flip_part(w2, wb2)
        else:
            pyr, wb1, wb2, w1, w2 = state_refs[:5]
            acc1, acc2, gp = out_refs[:3]
        regions_part(
            *(side, height, width, plan, block_refs, early_refs, stash_refs),
            *((pyr, wb1, wb2, w1, w2), (acc1, acc2, gp), scratch_refs),
        )
        if last:
            keep, *sends, gp_own, gp_other = out_refs[3:]
            finish_part(height, width, dp, chips, acc1, acc2, gp, keep, sends, gp_own, gp_other)

    aliases = {} if first else {5: 0, 6: 1, 7: 2}
    return run(
        kernel,
        outs,
        [*state, *weights, *blocks, *early, *stash],
        scratch=scratch + extra,
        aliases=aliases,
        hbm=(0, *range(len(state), len(state) + len(weights))) if first else (),
    )


def local_kernel(fn, outs, *arrays, **more):
    if isinstance(outs, tuple):
        return run(fn, outs, arrays, **more)
    return run(fn, (outs,), arrays, **more)[0]


def add(a, b):
    return (a.astype(F32) + b.astype(F32)).astype(BF)


def reduce_weights(keep, sends, core_swap, dp, chips, beside):
    rows = keep.shape[0] // dp
    bits = dp.bit_length() - 1
    orders = (list(range(bits)), list(reversed(range(bits))))
    shifts = [
        [(2 * z + c, 2 * ((z + k) % chips) + c) for z in range(chips) for c in range(2)]
        for k in range(chips)
    ]
    arrived = [lax.ppermute(send, "tile", core_swap) for send in sends]

    def split(members, bit):
        return [m for m in members if not m & bit], [m for m in members if m & bit]

    class Chunk:
        pass

    def begin(lo, hi, got):
        c = Chunk()
        c.rows = hi - lo
        low = roundup(c.rows // 2, 16)
        c.spans = ((0, low), (low, c.rows))
        c.members = [list(range(dp)), list(range(dp))]

        def first(keep_ref, got_ref, *outs):
            me = lax.axis_index("dp")
            for half in range(2):
                start, size = c.spans[half][0], c.spans[half][1] - c.spans[half][0]
                groups = split(c.members[half], 1 << orders[half][0])
                for out, group in zip(outs[2 * half : 2 * half + 2], groups):
                    for n, m in enumerate(group):
                        a = pl.ds(pl.multiple_of((me ^ m) * rows + lo + start, 16), size)
                        b = pl.ds(pl.multiple_of((me ^ m) * c.rows + start, 16), size)
                        out[n] = add(keep_ref[a, :], got_ref[b, :])

        shapes = []
        for half in range(2):
            shapes += [sds((dp // 2, c.spans[half][1] - c.spans[half][0], 256), BF)] * 2
        c.parts = local_kernel(first, tuple(shapes), keep, got)
        return c

    def exchange(c, stage):
        c.received = []
        for half in range(2):
            bit = 1 << orders[half][stage]
            pairs = [(i, i ^ bit) for i in range(dp)]
            c.received.append(lax.ppermute(c.parts[2 * half + 1], "dp", pairs))
            c.members[half] = split(c.members[half], bit)[0]

    def halve(c, stage):
        shapes = []
        for half in range(2):
            size = c.spans[half][1] - c.spans[half][0]
            shapes += [sds((len(c.members[half]) // 2, size, 256), BF)] * 2
        members = [list(m) for m in c.members]

        def kernel(p, pr, q, qr, *outs):
            for half, (mine, theirs) in enumerate(((p, pr), (q, qr))):
                groups = split(members[half], 1 << orders[half][stage])
                for out, group in zip(outs[2 * half : 2 * half + 2], groups):
                    for n, m in enumerate(group):
                        k = members[half].index(m)
                        out[n] = add(mine[k], theirs[k])

        c.parts = local_kernel(
            kernel, tuple(shapes), c.parts[0], c.received[0], c.parts[2], c.received[1]
        )

    def deal(c):
        c.share = roundup(-(-c.rows // chips), 16)
        low = c.spans[0][1]

        def kernel(p, pr, q, qr, *refs):
            outs, total = refs[:chips], refs[chips]
            chip = lax.axis_index("tile") // 2
            total[0:low, :] = add(p[0], pr[0])
            total[low : c.rows, :] = add(q[0], qr[0])
            if c.share * chips > c.rows:
                total[c.rows :, :] = jnp.zeros((c.share * chips - c.rows, 256), BF)
            for k in range(chips):
                to = lax.rem(chip + k, chips)
                outs[k][...] = total[pl.ds(pl.multiple_of(to * c.share, 16), c.share), :]

        dealt = local_kernel(
            kernel,
            tuple(sds((c.share, 256), BF) for _ in range(chips)),
            *(c.parts[0], c.received[0], c.parts[2], c.received[1]),
            scratch=[pltpu.VMEM((c.share * chips, 256), BF)],
        )
        c.mine = dealt[0]
        c.others = [lax.ppermute(dealt[k], "tile", shifts[k]) for k in range(1, chips)]

    def gather(c):
        def kernel(*refs):
            total = refs[0][...].astype(F32)
            for ref in refs[1:-1]:
                total += ref[...].astype(F32)
            refs[-1][...] = total.astype(BF)

        c.mine = local_kernel(kernel, sds((c.share, 256), BF), c.mine, *c.others)
        c.others = [lax.ppermute(c.mine, "tile", shifts[k]) for k in range(1, chips)]

    def lay(c):
        def kernel(*refs):
            chip = lax.axis_index("tile") // 2
            for k in range(chips):
                source = lax.rem(chip - k + chips, chips)
                refs[-1][pl.ds(pl.multiple_of(source * c.share, 16), c.share), :] = refs[k][...]

        c.whole = local_kernel(kernel, sds((c.share * chips, 256), BF), c.mine, *c.others)
        c.theirs = lax.ppermute(c.whole, "tile", core_swap)

    spans = chunks_of(rows)
    chunks = [begin(lo, hi, got) for (lo, hi), got in zip(spans, arrived)]
    for c in chunks:
        exchange(c, 0)
    chunks[0].received[0], beside = lax.optimization_barrier((chunks[0].received[0], beside))
    for stage in range(1, bits):
        for c in chunks:
            halve(c, stage)
            exchange(c, stage)
    for step in (deal, gather, lay):
        for c in chunks:
            step(c)

    def out(*refs):
        core = lax.rem(lax.axis_index("tile"), 2)
        one, two = refs[-2:]

        def write(to, sources):
            for (lo, hi), source in zip(spans, sources):
                to[lo:hi, :] = source[0 : hi - lo, :].astype(F32)

        @pl.when(core == 0)
        def _():
            write(one, refs[0 : len(spans)])
            write(two, refs[len(spans) : -2])

        @pl.when(core == 1)
        def _():
            write(one, refs[len(spans) : -2])
            write(two, refs[0 : len(spans)])

    one, two = local_kernel(
        out,
        (sds((rows, 256), F32), sds((rows, 256), F32)),
        *(c.whole for c in chunks),
        *(c.theirs for c in chunks),
        hbm_out=(0, 1),
    )
    return one, two, beside


def body(features, fpn_weight, mask_w1, mask_w2, owner, row_off, col_off, cotangent):
    tiles = lax.axis_size("tile")
    dp = lax.axis_size("dp")
    chips = tiles // 2
    height, width, channels = features.shape[1:]
    side = cotangent.shape[2]
    swap = [(i, i ^ 1) for i in range(tiles)]

    tile = features.reshape(height * width, channels)
    regions = cotangent.shape[1]
    place = [x.reshape(1, regions) for x in (owner, row_off, col_off)]
    edge = edge_of(tile, height, width)
    rim_a = lax.ppermute(
        edge, "tile", [(i, i + 1 if i % 2 else i - 1) for i in range(1, tiles - 1)]
    )
    other = lax.ppermute(tile, "tile", swap)
    packed, notes = pack(cotangent[0].transpose(1, 2, 0, 3), height, place)
    packed, rim_a = lax.optimization_barrier((packed, rim_a))
    rim_b = lax.ppermute(rim_a, "tile", swap)

    order = [0] + list(range(1, chips, 2)) + list(range(2, chips, 2))[::-1]
    ring = [
        (2 * z + c, 2 * order[(k + 1) % chips] + c) for k, z in enumerate(order) for c in range(2)
    ]

    flat = lambda w: w.reshape(9 * channels, channels)
    wf, w1, w2 = flat(fpn_weight), flat(mask_w1), flat(mask_w2)
    block = lax.ppermute(packed, "tile", ring)
    notes = lax.ppermute(notes, "tile", [(j, i) for i, j in ring])
    sizes = (side, height, width, dp, chips)
    held, plan = [packed], [1] + [4] * (chips - 2) if chips > 2 else [None]
    if chips > 2:
        plan[-1] = None
    state, weights, stash = [tile, other, rim_a, rim_b], [wf, w1, w2], []
    for step in range(chips):
        first, last = step == 0, step == chips - 1
        early = [notes] if step == chips - 2 else []
        if last:
            got = main_call(*sizes, first, last, [None], state, [], [block], [], stash)
            ends = got[3:]
            break
        got = list(main_call(*sizes, first, last, plan, state, weights, held, early, []))
        if first:
            kept, got = got[:5], got[5:]
        sums, stash, weights = got[:3], got[3:], []
        if step < chips - 2:
            block, kept[0], sums[0], notes = lax.optimization_barrier(
                (block, kept[0], sums[0], notes)
            )
            held = held + [block]
            block = lax.ppermute(block, "tile", ring)
        state = kept + sums
    keep, *sends, gp_own, gp_other = ends
    gp_got = lax.ppermute(gp_other, "tile", swap)

    def join(a, b, out):
        out[...] = (a[...] + b[...].astype(F32)).astype(BF)

    joined = local_kernel(
        join, sds((height * width, channels), BF), gp_own, gp_got, hbm_out=(0,)
    )
    grad_one, grad_two, grad_pyramid = reduce_weights(keep, sends, swap, dp, chips, joined)
    return grad_one, grad_two, grad_pyramid.reshape(1, height, width, channels)


def solution(mesh):
    placed = (
        P("dp", "tile", None, None),
        P(),
        P(),
        P(),
        P("dp", "tile", None),
        P("dp", "tile"),
        P("dp", "tile"),
        P("dp", "tile", None, None, None),
    )
    return jax.shard_map(
        body,
        mesh=mesh,
        in_specs=placed,
        out_specs=(P("dp", None), P("dp", None), P("dp", "tile", None, None)),
        check_vma=False,
    )
```

```python
import functools
import math

import jax
import jax.numpy as jnp
from jax import lax
from jax.experimental import pallas as pl
from jax.experimental.pallas import tpu as pltpu
from jax.sharding import PartitionSpec as P

BF = jnp.bfloat16
F32 = jnp.float32
VMEM_LIMIT = 24 * 1024 * 1024
PITCH = 16
SLOT = 208


def roundup(n, m):
    return (n + m - 1) // m * m


def run(kernel, outs, args, scratch=(), aliases=None, hbm=(), hbm_out=()):
    args = [
        pltpu.with_memory_space_constraint(x, pltpu.HBM if i in hbm else pltpu.VMEM)
        for i, x in enumerate(args)
    ]
    return pl.pallas_call(
        kernel,
        out_shape=tuple(
            s if i in hbm_out else pltpu.VMEM(s.shape, s.dtype) for i, s in enumerate(outs)
        ),
        in_specs=[
            pl.BlockSpec(memory_space=pltpu.HBM if i in hbm else pltpu.VMEM)
            for i in range(len(args))
        ],
        out_specs=tuple(pl.BlockSpec(memory_space=pltpu.VMEM) for _ in outs),
        scratch_shapes=list(scratch),
        input_output_aliases=aliases or {},
        compiler_params=pltpu.CompilerParams(vmem_limit_bytes=VMEM_LIMIT),
    )(*args)


def sds(shape, dtype):
    return jax.ShapeDtypeStruct(shape, dtype)


def pack_kernel(
    side, height, width, cot, owner, row, col, tile, packed, notes, edge, low, high, wide, places, sems
):
    regions = cot.shape[2]
    core = lax.rem(lax.axis_index("tile"), 2)
    line = pl.ds(pl.multiple_of(core * (height - 1) * width, width), width)
    copies = [pltpu.make_async_copy(tile.at[line, :], edge, sems.at[3])]
    copies += [
        pltpu.make_async_copy(source, places.at[n], sems.at[n])
        for n, source in enumerate((owner, row, col))
    ]
    for copy in copies:
        copy.start()
    for i in range(side):
        for j in range(side):
            at = (i * side + j) * regions
            cell = cot[i, j].astype(F32)
            low[at : at + regions, :] = cell[:, 0:128]
            high[at : at + regions, :] = cell[:, 128:256]
    for copy in copies:
        copy.wait()
    lanes = lax.broadcasted_iota(jnp.int32, (16, 256), 1)
    rows = lax.broadcasted_iota(jnp.int32, (16, 256), 0)
    cells = side * side
    for r in range(regions):
        wide[0:cells, 0:128] = low[pl.ds(r, cells, stride=regions), :]
        wide[0:cells, 128:256] = high[pl.ds(r, cells, stride=regions), :]
        spot = (places[0, 0, r] * height + places[1, 0, r] + 1).astype(F32)
        column = places[2, 0, r].astype(F32)
        note = jnp.where(lanes == 0, spot, jnp.where(lanes == 1, column, 0.0))
        wide[192:208, :] = jnp.where(rows < cells - 192, wide[192:208, :], note)
        packed[r] = wide[...].astype(BF)
        notes[r] = note.astype(BF)


def pack(cotangent, tile, height, width, place):
    side, regions = cotangent.shape[0], cotangent.shape[2]
    return local_kernel(
        functools.partial(pack_kernel, side, height, width),
        (
            sds((regions, SLOT, 256), BF),
            sds((regions, 16, 256), BF),
            sds((width, 256), BF),
        ),
        cotangent,
        *place,
        tile,
        scratch=[
            pltpu.VMEM((side * side * regions, 128), F32),
            pltpu.VMEM((side * side * regions, 128), F32),
            pltpu.VMEM((SLOT, 256), F32),
            pltpu.SMEM((3, 1, regions), jnp.int32),
            pltpu.SemaphoreType.DMA((4,)),
        ],
        hbm=(1, 2, 3, 4),
    )


def shifted(v, width):
    col = lax.broadcasted_iota(jnp.int32, (width, 256), 0)
    left = jnp.where(col == 0, 0.0, pltpu.roll(v, 1, 0)).astype(BF)
    right = jnp.where(col == width - 1, 0.0, pltpu.roll(v, width - 1, 0)).astype(BF)
    return left, v.astype(BF), right


def pyramid_part(height, width, own, other, wf, pyr, xp, fetched):
    core = lax.rem(lax.axis_index("tile"), 2)
    cells = height * width

    def fill(src, where):
        def step(t, carry):
            v = src[pl.ds(pl.multiple_of(t * width, width), width), :].astype(F32)
            to = pl.ds(pl.multiple_of(where + t * width, width), width)
            for b, piece in enumerate(shifted(v, width)):
                xp[to, b * 256 : b * 256 + 256] = piece
            return carry

        lax.fori_loop(0, height, step, 0)

    bottom = width + 2 * cells
    fill(own, width + core * cells)
    fill(other, width + (1 - core) * cells)
    xp[0:width, :] = jnp.zeros((width, 768), BF)
    xp[bottom : bottom + width, :] = jnp.zeros((width, 768), BF)
    fetched.wait()

    def conv(t, carry):
        at = t * 256
        total = jnp.zeros((256, 256), F32)
        for a in range(3):
            piece = xp[pl.ds(pl.multiple_of(at + a * width, 64), 256), :]
            total += jnp.dot(piece, wf[a * 768 : a * 768 + 768, :], preferred_element_type=F32)
        cell = at + lax.broadcasted_iota(jnp.int32, (256, 256), 0)
        open_row = (cell < width) | (cell >= 2 * cells - width)
        pyr[pl.ds(pl.multiple_of(at, 256), 256), :] = jnp.where(
            open_row, total, total.astype(BF).astype(F32)
        )
        return carry

    lax.fori_loop(0, 2 * cells // 256, conv, 0)
    pyr[2 * cells : 2 * cells + 16, :] = jnp.zeros((16, 256), F32)


def edges_part(height, width, rim_a, rim_b, wf, pyr):
    core = lax.rem(lax.axis_index("tile"), 2)
    last = 2 * height * width - width

    def close(rim, at, tap):
        total = pyr[at : at + width, :]
        for b, piece in enumerate(shifted(rim[...].astype(F32), width)):
            k = 3 * tap + b
            total += jnp.dot(piece, wf[k * 256 : k * 256 + 256, :], preferred_element_type=F32)
        pyr[at : at + width, :] = total.astype(BF).astype(F32)

    @pl.when(core == 0)
    def _():
        close(rim_a, 0, 0)
        close(rim_b, last, 2)

    @pl.when(core == 1)
    def _():
        close(rim_b, 0, 0)
        close(rim_a, last, 2)


def flip_part(w, wb):
    for k in range(9):
        block = w[(8 - k) * 256 : (9 - k) * 256, :].astype(F32)
        wb[k * 256 : k * 256 + 256, :] = block.T.astype(BF)


def gelu_pair(v):
    c = math.sqrt(2.0 / math.pi)
    sq = v * v
    t = jnp.tanh(c * (v + 0.044715 * (sq * v)))
    half = 0.5 * (1.0 + t)
    slope = half + 0.5 * v * (1.0 - t * t) * (c * (1.0 + 3 * 0.044715 * sq))
    return v * half, slope


def regions_part(side, height, width, plan, blocks, early, stash, tables, sums, scratch):
    pyr, wb1, wb2, w1, w2 = tables
    acc1, acc2, gp = sums
    xs, hs, gs, wide, vs, slope1, todo = scratch
    chip = lax.axis_index("tile") // 2
    lanes = lax.broadcasted_iota(jnp.int32, (16, 256), 1)
    rows16 = lax.broadcasted_iota(jnp.int32, (16, 256), 0)
    in_row = rows16 < side
    cells = side * PITCH
    inside = (lax.broadcasted_iota(jnp.int32, (cells, 256), 0) & (PITCH - 1)) < side
    used = pl.ds(16, cells)
    per = blocks[0].shape[0]
    tail = pl.ds(192, 16)

    count = jnp.int32(0)
    start, end = jnp.int32(0), jnp.int32(0)

    def enlist(s, r, note):
        note = jnp.where(rows16 == 15, note.astype(F32), 0.0)
        spot = jnp.sum(jnp.where(lanes == 0, note, 0.0)).astype(jnp.int32) - 1
        column = jnp.sum(jnp.where(lanes == 1, note, 0.0)).astype(jnp.int32)
        local = spot - chip * 2 * height
        here = (spot >= 0) & (local >= 0) & (local < 2 * height)
        todo[0, count] = jnp.int32(s * per + r)
        todo[1, count] = jnp.where(here, local * width + column // 8 * 8, 0)
        todo[2, count] = jnp.where(here, lax.rem(column, 8), 0)
        return count + here.astype(jnp.int32)

    for s, block in enumerate(blocks):
        for r in range(per):
            count = enlist(s, r, block[r, tail, :])
        most = plan[s]
        start, end = end, count if most is None else jnp.minimum(count, end + most)
    total = count
    for block in early:
        for r in range(per):
            count = enlist(len(blocks), r, block[r])

    for buf in (xs, hs, gs):
        buf[0:16, :] = jnp.zeros((16, 768), BF)
        buf[cells + 16 : cells + 32, :] = jnp.zeros((16, 768), BF)

    def put(buf, v):
        buf[used, 0:256] = pltpu.roll(v, 1, 0).astype(BF)
        buf[used, 256:512] = v.astype(BF)
        buf[used, 512:768] = pltpu.roll(v, cells - 1, 0).astype(BF)

    def conv(buf, w):
        total = jnp.zeros((cells, 256), F32)
        for a in range(3):
            total += jnp.dot(
                buf[a * 16 : a * 16 + cells, :],
                w[a * 768 : a * 768 + 768, :],
                preferred_element_type=F32,
            )
        return total

    def taps(acc, buf, grad):
        turned = grad.T.astype(BF)
        for a in range(3):
            acc[:, a * 768 : a * 768 + 768] += jnp.dot(
                turned, buf[a * 16 : a * 16 + cells, :], preferred_element_type=F32
            )

    def crop(n):
        base, lead = todo[1, n], todo[2, n]
        for i in range(side):
            got = pyr[pl.ds(pl.multiple_of(base + i * width, 8), 24), :]
            got = pltpu.roll(got, lax.rem(24 - lead, 24), 0)[0:16]
            vs[i * 16 : i * 16 + 16, :] = jnp.where(in_row, got, 0.0)
        put(xs, vs[...])

    def forward(n):
        crop(n)
        act1, slope = gelu_pair(conv(xs, w1))
        slope1[...] = slope
        act1 = jnp.where(inside, act1, 0.0)
        put(hs, act1)
        _, slope = gelu_pair(conv(hs, w2))
        return act1, slope

    def backward(n, slope2):
        which = todo[0, n]
        base, lead = todo[1, n], todo[2, n]
        for s, block in enumerate(blocks):

            @pl.when(which // per == s)
            def _(block=block):
                wide[...] = block[lax.rem(which, per)].astype(F32)

        for i in range(side):
            got = wide[i * side : i * side + 16, :]
            vs[i * 16 : i * 16 + 16, :] = jnp.where(in_row, got, 0.0)
        g2 = vs[...] * slope2
        put(gs, g2)
        taps(acc2, hs, g2)
        g1 = jnp.where(inside, conv(gs, wb2) * slope1[...], 0.0)
        put(gs, g1)
        taps(acc1, xs, g1)
        vs[...] = jnp.where(inside, conv(gs, wb1), 0.0).astype(BF).astype(F32)
        for i in range(side):
            at = pl.ds(pl.multiple_of(base + i * width, 8), 24)
            piece = jnp.concatenate([vs[i * 16 : i * 16 + 16, :], jnp.zeros((8, 256), F32)])
            gp[at, :] = gp[at, :] + pltpu.roll(piece, lead, 0)

    def whole(n, carry):
        _, slope2 = forward(n)
        backward(n, slope2)
        return carry

    def ahead(n, carry):
        r = lax.rem(todo[0, n], per)
        act1, slope2 = forward(n)
        stash[0][r] = act1.astype(BF)
        stash[1][r] = slope1[...]
        stash[2][r] = slope2
        return carry

    def behind(n, carry):
        r = lax.rem(todo[0, n], per)
        crop(n)
        put(hs, stash[0][r].astype(F32))
        slope1[...] = stash[1][r]
        backward(n, stash[2][r])
        return carry

    if early:
        lax.fori_loop(start, end, whole, 0)
        lax.fori_loop(total, count, ahead, 0)
    elif stash:
        lax.fori_loop(0, total, behind, 0)
    else:
        lax.fori_loop(start, end, whole, 0)


def chunks_of(rows):
    return ((0, rows),)


def finish_part(height, width, dp, chips, acc1, acc2, gp, keep, sends, gp_own, gp_other):
    core = lax.rem(lax.axis_index("tile"), 2)
    cells = height * width
    rows = 2304 // dp
    parts = chunks_of(rows)

    def write_keep(acc):
        for k in range(9):
            keep[k * 256 : k * 256 + 256, :] = acc[:, k * 256 : k * 256 + 256].T.astype(BF)

    def write_sends(acc):
        for k in range(9):
            value = acc[:, k * 256 : k * 256 + 256].T.astype(BF)
            for d in range(dp):
                for to, (lo, hi) in zip(sends, parts):
                    first = max(d * rows + lo, k * 256)
                    end = min(d * rows + hi, k * 256 + 256)
                    if first < end:
                        at = d * (hi - lo) + first - d * rows - lo
                        to[at : at + end - first, :] = value[first - k * 256 : end - k * 256, :]

    @pl.when(core == 0)
    def _():
        write_sends(acc2)
        write_keep(acc1)

    @pl.when(core == 1)
    def _():
        write_sends(acc1)
        write_keep(acc2)

    gp_own[...] = gp[pl.ds(pl.multiple_of(core * cells, cells), cells), :]
    gp_other[...] = gp[pl.ds(pl.multiple_of((1 - core) * cells, cells), cells), :].astype(BF)


def main_call(side, height, width, dp, chips, first, last, plan, state, weights, rims, blocks, early, stash):
    n = len(blocks)
    big = 2 * height * width + 16
    cells = side * PITCH
    kept = (sds((big, 256), F32),) + (sds((2304, 256), BF),) * 5
    sums = (sds((256, 2304), F32), sds((256, 2304), F32), sds((big, 256), F32))
    ends = (
        sds((2304, 256), BF),
        *(sds((dp * (hi - lo), 256), BF) for lo, hi in chunks_of(2304 // dp)),
        sds((height * width, 256), F32),
        sds((height * width, 256), BF),
    )
    per = early[0].shape[0] if early else 0
    stashed = (
        sds((per, cells, 256), BF),
        sds((per, cells, 256), F32),
        sds((per, cells, 256), F32),
    )
    outs = (kept if first else kept[:1] if rims else ()) + sums + (ends if last else ()) + (stashed if early else ())
    scratch = [
        pltpu.VMEM((cells + 32, 768), BF),
        pltpu.VMEM((cells + 32, 768), BF),
        pltpu.VMEM((cells + 32, 768), BF),
        pltpu.VMEM((SLOT, 256), F32),
        pltpu.VMEM((cells, 256), F32),
        pltpu.VMEM((cells, 256), F32),
        pltpu.SMEM((3, 256), jnp.int32),
    ]
    extra = []
    if first:
        extra = [
            pltpu.VMEM(((2 * height + 2) * width, 768), BF),
            pltpu.VMEM((height * width, 256), BF),
            pltpu.SemaphoreType.DMA((4,)),
        ]

    def kernel(*refs):
        refs = list(refs)

        def take(k):
            got = refs[:k]
            del refs[:k]
            return got

        state_refs = take(len(state))
        weight_refs = take(len(weights))
        rim_refs = take(len(rims))
        block_refs = take(n)
        early_refs = take(len(early))
        stash_refs = take(len(stash))
        out_refs = take(len(outs))
        if early:
            stash_refs = out_refs[-3:]
        scratch_refs = take(len(scratch))
        if first:
            pyr, wb1, wb2, w1, w2, wf = out_refs[:6]
            acc1, acc2, gp = out_refs[6:9]
            xp, own, sems = refs
            copies = [
                pltpu.make_async_copy(source, to, sems.at[k])
                for k, (source, to) in enumerate(zip((state_refs[0], *weight_refs), (own, wf, w1, w2)))
            ]
            for copy in copies:
                copy.start()
            for total in (acc1, acc2, gp):
                total[...] = jnp.zeros(total.shape, F32)
            copies[0].wait()
            pyramid_part(height, width, own, state_refs[1], wf, pyr, xp, copies[1])
            copies[2].wait()
            flip_part(w1, wb1)
            copies[3].wait()
            flip_part(w2, wb2)
        else:
            pyr, wb1, wb2, w1, w2, wf = state_refs[:6]
            shared = list(out_refs)
            if rims:
                pyr = shared.pop(0)
                edges_part(height, width, *rim_refs, wf, pyr)
            acc1, acc2, gp = shared[:3]
        if n:
            regions_part(
                *(side, height, width, plan, block_refs, early_refs, stash_refs),
                *((pyr, wb1, wb2, w1, w2), (acc1, acc2, gp), scratch_refs),
            )
        if last:
            keep, *sends, gp_own, gp_other = out_refs[3:]
            finish_part(height, width, dp, chips, acc1, acc2, gp, keep, sends, gp_own, gp_other)

    aliases = {} if first else {6: 0, 7: 1, 8: 2}
    if rims:
        aliases = {0: 0, 6: 1, 7: 2, 8: 3}
    return run(
        kernel,
        outs,
        [*state, *weights, *rims, *blocks, *early, *stash],
        scratch=scratch + extra,
        aliases=aliases,
        hbm=(0, *range(len(state), len(state) + len(weights))) if first else (),
    )


def local_kernel(fn, outs, *arrays, **more):
    if isinstance(outs, tuple):
        return run(fn, outs, arrays, **more)
    return run(fn, (outs,), arrays, **more)[0]


def add(a, b):
    return (a.astype(F32) + b.astype(F32)).astype(BF)


def reduce_weights(keep, sends, core_swap, dp, chips, beside):
    rows = keep.shape[0] // dp
    bits = dp.bit_length() - 1
    orders = (list(range(bits)), list(reversed(range(bits))))
    shifts = [
        [(2 * z + c, 2 * ((z + k) % chips) + c) for z in range(chips) for c in range(2)]
        for k in range(chips)
    ]
    arrived = [lax.ppermute(send, "tile", core_swap) for send in sends]

    def split(members, bit):
        return [m for m in members if not m & bit], [m for m in members if m & bit]

    class Chunk:
        pass

    def begin(lo, hi, got):
        c = Chunk()
        c.rows = hi - lo
        low = roundup(c.rows // 2, 16)
        c.spans = ((0, low), (low, c.rows))
        c.members = [list(range(dp)), list(range(dp))]

        def first(keep_ref, got_ref, *outs):
            me = lax.axis_index("dp")
            for half in range(2):
                start, size = c.spans[half][0], c.spans[half][1] - c.spans[half][0]
                groups = split(c.members[half], 1 << orders[half][0])
                for out, group in zip(outs[2 * half : 2 * half + 2], groups):
                    for n, m in enumerate(group):
                        a = pl.ds(pl.multiple_of((me ^ m) * rows + lo + start, 16), size)
                        b = pl.ds(pl.multiple_of((me ^ m) * c.rows + start, 16), size)
                        out[n] = add(keep_ref[a, :], got_ref[b, :])

        shapes = []
        for half in range(2):
            shapes += [sds((dp // 2, c.spans[half][1] - c.spans[half][0], 256), BF)] * 2
        c.parts = local_kernel(first, tuple(shapes), keep, got)
        return c

    def exchange(c, stage):
        c.received = []
        for half in range(2):
            bit = 1 << orders[half][stage]
            pairs = [(i, i ^ bit) for i in range(dp)]
            c.received.append(lax.ppermute(c.parts[2 * half + 1], "dp", pairs))
            c.members[half] = split(c.members[half], bit)[0]

    def halve(c, stage):
        shapes = []
        for half in range(2):
            size = c.spans[half][1] - c.spans[half][0]
            shapes += [sds((len(c.members[half]) // 2, size, 256), BF)] * 2
        members = [list(m) for m in c.members]

        def kernel(p, pr, q, qr, *outs):
            for half, (mine, theirs) in enumerate(((p, pr), (q, qr))):
                groups = split(members[half], 1 << orders[half][stage])
                for out, group in zip(outs[2 * half : 2 * half + 2], groups):
                    for n, m in enumerate(group):
                        k = members[half].index(m)
                        out[n] = add(mine[k], theirs[k])

        c.parts = local_kernel(
            kernel, tuple(shapes), c.parts[0], c.received[0], c.parts[2], c.received[1]
        )

    def deal(c):
        c.share = roundup(-(-c.rows // chips), 16)
        low = c.spans[0][1]

        def kernel(p, pr, q, qr, *refs):
            outs, total = refs[:chips], refs[chips]
            chip = lax.axis_index("tile") // 2
            total[0:low, :] = add(p[0], pr[0])
            total[low : c.rows, :] = add(q[0], qr[0])
            if c.share * chips > c.rows:
                total[c.rows :, :] = jnp.zeros((c.share * chips - c.rows, 256), BF)
            for k in range(chips):
                to = lax.rem(chip + k, chips)
                outs[k][...] = total[pl.ds(pl.multiple_of(to * c.share, 16), c.share), :]

        dealt = local_kernel(
            kernel,
            tuple(sds((c.share, 256), BF) for _ in range(chips)),
            *(c.parts[0], c.received[0], c.parts[2], c.received[1]),
            scratch=[pltpu.VMEM((c.share * chips, 256), BF)],
        )
        c.mine = dealt[0]
        c.others = [lax.ppermute(dealt[k], "tile", shifts[k]) for k in range(1, chips)]

    def gather(c):
        def kernel(*refs):
            total = refs[0][...].astype(F32)
            for ref in refs[1:-1]:
                total += ref[...].astype(F32)
            refs[-1][...] = total.astype(BF)

        c.mine = local_kernel(kernel, sds((c.share, 256), BF), c.mine, *c.others)
        c.others = [lax.ppermute(c.mine, "tile", shifts[k]) for k in range(1, chips)]

    def lay(c):
        def kernel(*refs):
            chip = lax.axis_index("tile") // 2
            for k in range(chips):
                source = lax.rem(chip - k + chips, chips)
                refs[-1][pl.ds(pl.multiple_of(source * c.share, 16), c.share), :] = refs[k][...]

        c.whole = local_kernel(kernel, sds((c.share * chips, 256), BF), c.mine, *c.others)
        c.theirs = lax.ppermute(c.whole, "tile", core_swap)

    spans = chunks_of(rows)
    chunks = [begin(lo, hi, got) for (lo, hi), got in zip(spans, arrived)]
    for c in chunks:
        exchange(c, 0)
    chunks[0].received[0], beside = lax.optimization_barrier((chunks[0].received[0], beside))
    for stage in range(1, bits):
        for c in chunks:
            halve(c, stage)
            exchange(c, stage)
    for step in (deal, gather, lay):
        for c in chunks:
            step(c)

    def out(*refs):
        core = lax.rem(lax.axis_index("tile"), 2)
        one, two = refs[-2:]

        def write(to, sources):
            for (lo, hi), source in zip(spans, sources):
                to[lo:hi, :] = source[0 : hi - lo, :].astype(F32)

        @pl.when(core == 0)
        def _():
            write(one, refs[0 : len(spans)])
            write(two, refs[len(spans) : -2])

        @pl.when(core == 1)
        def _():
            write(one, refs[len(spans) : -2])
            write(two, refs[0 : len(spans)])

    one, two = local_kernel(
        out,
        (sds((rows, 256), F32), sds((rows, 256), F32)),
        *(c.whole for c in chunks),
        *(c.theirs for c in chunks),
        hbm_out=(0, 1),
    )
    return one, two, beside


def body(features, fpn_weight, mask_w1, mask_w2, owner, row_off, col_off, cotangent):
    tiles = lax.axis_size("tile")
    dp = lax.axis_size("dp")
    chips = tiles // 2
    height, width, channels = features.shape[1:]
    side = cotangent.shape[2]
    swap = [(i, i ^ 1) for i in range(tiles)]

    tile = features.reshape(height * width, channels)
    regions = cotangent.shape[1]
    place = [x.reshape(1, regions) for x in (owner, row_off, col_off)]
    other = lax.ppermute(tile, "tile", swap)
    packed, notes, edge = pack(cotangent[0].transpose(1, 2, 0, 3), tile, height, width, place)
    rim_a = lax.ppermute(
        edge, "tile", [(i, i + 1 if i % 2 else i - 1) for i in range(1, tiles - 1)]
    )
    rim_b = lax.ppermute(rim_a, "tile", swap)

    order = [0] + list(range(1, chips, 2)) + list(range(2, chips, 2))[::-1]
    ring = [
        (2 * z + c, 2 * order[(k + 1) % chips] + c) for k, z in enumerate(order) for c in range(2)
    ]

    flat = lambda w: w.reshape(9 * channels, channels)
    wf, w1, w2 = flat(fpn_weight), flat(mask_w1), flat(mask_w2)
    block = lax.ppermute(packed, "tile", ring)
    notes = lax.ppermute(notes, "tile", [(j, i) for i, j in ring])
    sizes = (side, height, width, dp, chips)
    plan = [0] + [4] * (chips - 3) + [None]
    start = main_call(*sizes, True, False, [], [tile, other], [wf, w1, w2], [], [], [], [])
    kept, sums, held = list(start[:6]), list(start[6:]), [packed]
    for step in range(1, chips):
        state = kept + sums
        if step == chips - 1:
            got = main_call(*sizes, False, True, [None], state, [], [], [block], [], stash)
            ends = got[3:]
            break
        block, state[0], state[-1], notes, rim_a = lax.optimization_barrier(
            (block, state[0], state[-1], notes, rim_a)
        )
        held = held + [block]
        block = lax.ppermute(block, "tile", ring)
        early = [notes] if step == chips - 2 else []
        rims = [rim_a, rim_b] if step == 1 else []
        got = list(main_call(*sizes, False, False, plan, state, [], rims, held, early, []))
        if rims:
            kept[0] = got.pop(0)
        sums, stash = got[:3], got[3:]
    keep, *sends, gp_own, gp_other = ends
    gp_got = lax.ppermute(gp_other, "tile", swap)

    def join(a, b, out):
        out[...] = (a[...] + b[...].astype(F32)).astype(BF)

    joined = local_kernel(
        join, sds((height * width, channels), BF), gp_own, gp_got, hbm_out=(0,)
    )
    grad_one, grad_two, grad_pyramid = reduce_weights(keep, sends, swap, dp, chips, joined)
    return grad_one, grad_two, grad_pyramid.reshape(1, height, width, channels)


def solution(mesh):
    placed = (
        P("dp", "tile", None, None),
        P(),
        P(),
        P(),
        P("dp", "tile", None),
        P("dp", "tile"),
        P("dp", "tile"),
        P("dp", "tile", None, None, None),
    )
    return jax.shard_map(
        body,
        mesh=mesh,
        in_specs=placed,
        out_specs=(P("dp", None), P("dp", None), P("dp", "tile", None, None)),
        check_vma=False,
    )
```

```python
import functools
import math

import jax
import jax.numpy as jnp
from jax import lax
from jax.experimental import pallas as pl
from jax.experimental.pallas import tpu as pltpu
from jax.sharding import PartitionSpec as P

BF = jnp.bfloat16
F32 = jnp.float32
VMEM_LIMIT = 24 * 1024 * 1024
PITCH = 16


def roundup(n, m):
    return (n + m - 1) // m * m


def run(kernel, outs, args, scratch=(), aliases=None, hbm=(), hbm_out=()):
    args = [
        pltpu.with_memory_space_constraint(x, pltpu.HBM if i in hbm else pltpu.VMEM)
        for i, x in enumerate(args)
    ]
    return pl.pallas_call(
        kernel,
        out_shape=tuple(
            s if i in hbm_out else pltpu.VMEM(s.shape, s.dtype) for i, s in enumerate(outs)
        ),
        in_specs=[
            pl.BlockSpec(memory_space=pltpu.HBM if i in hbm else pltpu.VMEM)
            for i in range(len(args))
        ],
        out_specs=tuple(pl.BlockSpec(memory_space=pltpu.VMEM) for _ in outs),
        scratch_shapes=list(scratch),
        input_output_aliases=aliases or {},
        compiler_params=pltpu.CompilerParams(vmem_limit_bytes=VMEM_LIMIT),
    )(*args)


def sds(shape, dtype):
    return jax.ShapeDtypeStruct(shape, dtype)


def pack_kernel(
    side, height, width, cot, owner, row, col, tile, packed, notes, edge, low, high, wide, tails, places, sems
):
    regions = cot.shape[2]
    core = lax.rem(lax.axis_index("tile"), 2)
    line = pl.ds(pl.multiple_of(core * (height - 1) * width, width), width)
    copies = [pltpu.make_async_copy(tile.at[line, :], edge, sems.at[3])]
    copies += [
        pltpu.make_async_copy(source, places.at[n], sems.at[n])
        for n, source in enumerate((owner, row, col))
    ]
    for copy in copies:
        copy.start()
    for i in range(side):
        for j in range(side):
            at = (i * side + j) * regions
            cell = cot[i, j].astype(F32)
            low[at : at + regions, :] = cell[:, 0:128]
            high[at : at + regions, :] = cell[:, 128:256]
    for copy in copies:
        copy.wait()
    lanes = lax.broadcasted_iota(jnp.int32, (16, 256), 1)
    rows = lax.broadcasted_iota(jnp.int32, (16, 256), 0)
    cells = side * side
    main = cells // 16 * 16
    rest = cells - main
    note = jnp.zeros((16, 256), F32)
    for r in range(regions):
        wide[0:cells, 0:128] = low[pl.ds(r, cells, stride=regions), :]
        wide[0:cells, 128:256] = high[pl.ds(r, cells, stride=regions), :]
        spot = (places[0, 0, r] * height + places[1, 0, r] + 1).astype(F32)
        column = places[2, 0, r].astype(F32)
        value = jnp.where(lanes == 0, spot, jnp.where(lanes == 1, column, 0.0))
        note = jnp.where(rows == r, value, note)
        packed[r * main : r * main + main, :] = wide[0:main, :].astype(BF)
        tails[r * rest : r * rest + rest, :] = wide[main:cells, :]
    at = regions * main
    packed[at : at + tails.shape[0], :] = tails[...].astype(BF)
    at += tails.shape[0]
    packed[at : at + 16, :] = note.astype(BF)
    notes[...] = note.astype(BF)


def packed_rows(side, regions):
    cells = side * side
    return regions * (cells // 16 * 16), roundup(regions * (cells % 16), 16)


def pack(cotangent, tile, height, width, place):
    side, regions = cotangent.shape[0], cotangent.shape[2]
    return local_kernel(
        functools.partial(pack_kernel, side, height, width),
        (
            sds((sum(packed_rows(side, regions)) + 16, 256), BF),
            sds((16, 256), BF),
            sds((width, 256), BF),
        ),
        cotangent,
        *place,
        tile,
        scratch=[
            pltpu.VMEM((side * side * regions, 128), F32),
            pltpu.VMEM((side * side * regions, 128), F32),
            pltpu.VMEM((side * side, 256), F32),
            pltpu.VMEM((packed_rows(side, regions)[1], 256), F32),
            pltpu.SMEM((3, 1, regions), jnp.int32),
            pltpu.SemaphoreType.DMA((4,)),
        ],
        hbm=(1, 2, 3, 4),
    )


def shifted(v, width):
    col = lax.broadcasted_iota(jnp.int32, (width, 256), 0)
    left = jnp.where(col == 0, 0.0, pltpu.roll(v, 1, 0)).astype(BF)
    right = jnp.where(col == width - 1, 0.0, pltpu.roll(v, width - 1, 0)).astype(BF)
    return left, v.astype(BF), right


def pyramid_part(height, width, own, other, wf, pyr, xp, fetched):
    core = lax.rem(lax.axis_index("tile"), 2)
    cells = height * width

    def fill(src, where):
        def step(t, carry):
            v = src[pl.ds(pl.multiple_of(t * width, width), width), :].astype(F32)
            to = pl.ds(pl.multiple_of(where + t * width, width), width)
            for b, piece in enumerate(shifted(v, width)):
                xp[to, b * 256 : b * 256 + 256] = piece
            return carry

        lax.fori_loop(0, height, step, 0)

    bottom = width + 2 * cells
    fill(own, width + core * cells)
    fill(other, width + (1 - core) * cells)
    xp[0:width, :] = jnp.zeros((width, 768), BF)
    xp[bottom : bottom + width, :] = jnp.zeros((width, 768), BF)
    fetched.wait()

    def conv(t, carry):
        at = t * 256
        total = jnp.zeros((256, 256), F32)
        for a in range(3):
            piece = xp[pl.ds(pl.multiple_of(at + a * width, 64), 256), :]
            total += jnp.dot(piece, wf[a * 768 : a * 768 + 768, :], preferred_element_type=F32)
        cell = at + lax.broadcasted_iota(jnp.int32, (256, 256), 0)
        open_row = (cell < width) | (cell >= 2 * cells - width)
        pyr[pl.ds(pl.multiple_of(at, 256), 256), :] = jnp.where(
            open_row, total, total.astype(BF).astype(F32)
        )
        return carry

    lax.fori_loop(0, 2 * cells // 256, conv, 0)
    pyr[2 * cells : 2 * cells + 16, :] = jnp.zeros((16, 256), F32)


def edges_part(height, width, rim_a, rim_b, wf, pyr):
    core = lax.rem(lax.axis_index("tile"), 2)
    last = 2 * height * width - width

    def close(rim, at, tap):
        total = pyr[at : at + width, :]
        for b, piece in enumerate(shifted(rim[...].astype(F32), width)):
            k = 3 * tap + b
            total += jnp.dot(piece, wf[k * 256 : k * 256 + 256, :], preferred_element_type=F32)
        pyr[at : at + width, :] = total.astype(BF).astype(F32)

    @pl.when(core == 0)
    def _():
        close(rim_a, 0, 0)
        close(rim_b, last, 2)

    @pl.when(core == 1)
    def _():
        close(rim_b, 0, 0)
        close(rim_a, last, 2)


def flip_part(w, wb):
    for k in range(9):
        block = w[(8 - k) * 256 : (9 - k) * 256, :].astype(F32)
        wb[k * 256 : k * 256 + 256, :] = block.T.astype(BF)


def gelu_pair(v):
    c = math.sqrt(2.0 / math.pi)
    sq = v * v
    t = jnp.tanh(c * (v + 0.044715 * (sq * v)))
    half = 0.5 * (1.0 + t)
    slope = half + 0.5 * v * (1.0 - t * t) * (c * (1.0 + 3 * 0.044715 * sq))
    return v * half, slope


def regions_part(side, height, width, per, plan, blocks, early, stash, tables, sums, scratch):
    pyr, wb1, wb2, w1, w2 = tables
    acc1, acc2, gp = sums
    xs, hs, gs, wide, vs, slope1, todo = scratch
    chip = lax.axis_index("tile") // 2
    lanes = lax.broadcasted_iota(jnp.int32, (16, 256), 1)
    rows16 = lax.broadcasted_iota(jnp.int32, (16, 256), 0)
    in_row = rows16 < side
    cells = side * PITCH
    inside = (lax.broadcasted_iota(jnp.int32, (cells, 256), 0) & (PITCH - 1)) < side
    used = pl.ds(16, cells)
    main, tails = packed_rows(side, per)
    one = main // per
    rest = side * side - one

    count = jnp.int32(0)
    start, end = jnp.int32(0), jnp.int32(0)

    def enlist(s, r, note, wanted=None):
        note = jnp.where(rows16 == r, note.astype(F32), 0.0)
        spot = jnp.sum(jnp.where(lanes == 0, note, 0.0)).astype(jnp.int32) - 1
        column = jnp.sum(jnp.where(lanes == 1, note, 0.0)).astype(jnp.int32)
        local = spot - chip * 2 * height
        here = (spot >= 0) & (local >= 0) & (local < 2 * height)
        if wanted is not None:
            outer = (local == 0) | (local == 2 * height - side)
            here = here & (outer == wanted)
        todo[0, count] = jnp.int32(s * per + r)
        todo[1, count] = jnp.where(here, local * width + column // 8 * 8, 0)
        todo[2, count] = jnp.where(here, lax.rem(column, 8), 0)
        return count + here.astype(jnp.int32)

    for s, block in enumerate(blocks):
        note = block[main + tails : main + tails + 16, :]
        for r in range(per):
            count = enlist(s, r, note, False if s == 0 and plan[0] is not None else None)
        most = plan[s]
        start, end = end, count if most is None else jnp.minimum(count, end + most)
        if s == 0 and plan[0] is not None:
            for r in range(per):
                count = enlist(s, r, note, True)
    total = count
    for note in early:
        for r in range(per):
            count = enlist(len(blocks), r, note[...])

    for buf in (xs, hs, gs):
        buf[0:16, :] = jnp.zeros((16, 768), BF)
        buf[cells + 16 : cells + 32, :] = jnp.zeros((16, 768), BF)

    def put(buf, v):
        buf[used, 0:256] = pltpu.roll(v, 1, 0).astype(BF)
        buf[used, 256:512] = v.astype(BF)
        buf[used, 512:768] = pltpu.roll(v, cells - 1, 0).astype(BF)

    def conv(buf, w):
        total = jnp.zeros((cells, 256), F32)
        for a in range(3):
            total += jnp.dot(
                buf[a * 16 : a * 16 + cells, :],
                w[a * 768 : a * 768 + 768, :],
                preferred_element_type=F32,
            )
        return total

    def taps(acc, buf, grad):
        turned = grad.T.astype(BF)
        for a in range(3):
            acc[:, a * 768 : a * 768 + 768] += jnp.dot(
                turned, buf[a * 16 : a * 16 + cells, :], preferred_element_type=F32
            )

    def crop(n):
        base, lead = todo[1, n], todo[2, n]
        for i in range(side):
            got = pyr[pl.ds(pl.multiple_of(base + i * width, 8), 24), :]
            got = pltpu.roll(got, lax.rem(24 - lead, 24), 0)[0:16]
            vs[i * 16 : i * 16 + 16, :] = jnp.where(in_row, got, 0.0)
        put(xs, vs[...])

    def forward(n):
        crop(n)
        act1, slope = gelu_pair(conv(xs, w1))
        slope1[...] = slope
        act1 = jnp.where(inside, act1, 0.0)
        put(hs, act1)
        _, slope = gelu_pair(conv(hs, w2))
        return act1, slope

    def backward(n, slope2):
        which = todo[0, n]
        base, lead = todo[1, n], todo[2, n]
        for s, block in enumerate(blocks):

            @pl.when(which // per == s)
            def _(block=block):
                r = lax.rem(which, per)
                cell = pl.ds(pl.multiple_of(r * one, 16), one)
                wide[0:one, :] = block[cell, :].astype(F32)
                left = block[main : main + tails, :].astype(F32)
                wide[one : one + tails, :] = pltpu.roll(left, lax.rem(tails - r * rest, tails), 0)

        for i in range(side):
            got = wide[i * side : i * side + 16, :]
            vs[i * 16 : i * 16 + 16, :] = jnp.where(in_row, got, 0.0)
        g2 = vs[...] * slope2
        put(gs, g2)
        taps(acc2, hs, g2)
        g1 = jnp.where(inside, conv(gs, wb2) * slope1[...], 0.0)
        put(gs, g1)
        taps(acc1, xs, g1)
        vs[...] = jnp.where(inside, conv(gs, wb1), 0.0).astype(BF).astype(F32)
        for i in range(side):
            at = pl.ds(pl.multiple_of(base + i * width, 8), 24)
            piece = jnp.concatenate([vs[i * 16 : i * 16 + 16, :], jnp.zeros((8, 256), F32)])
            gp[at, :] = gp[at, :] + pltpu.roll(piece, lead, 0)

    def whole(n, carry):
        _, slope2 = forward(n)
        backward(n, slope2)
        return carry

    def ahead(n, carry):
        r = lax.rem(todo[0, n], per)
        act1, slope2 = forward(n)
        stash[0][r] = act1.astype(BF)
        stash[1][r] = slope1[...]
        stash[2][r] = slope2
        return carry

    def behind(n, carry):
        r = lax.rem(todo[0, n], per)
        crop(n)
        put(hs, stash[0][r].astype(F32))
        slope1[...] = stash[1][r]
        backward(n, stash[2][r])
        return carry

    if early:
        lax.fori_loop(start, end, whole, 0)
        lax.fori_loop(total, count, ahead, 0)
    elif stash:
        lax.fori_loop(0, total, behind, 0)
    else:
        lax.fori_loop(start, end, whole, 0)


def chunks_of(rows):
    return ((0, rows),)


def finish_part(height, width, dp, chips, acc1, acc2, gp, keep, sends, gp_own, gp_other):
    core = lax.rem(lax.axis_index("tile"), 2)
    cells = height * width
    rows = 2304 // dp
    parts = chunks_of(rows)

    def write_keep(acc):
        for k in range(9):
            keep[k * 256 : k * 256 + 256, :] = acc[:, k * 256 : k * 256 + 256].T.astype(BF)

    def write_sends(acc):
        for k in range(9):
            value = acc[:, k * 256 : k * 256 + 256].T.astype(BF)
            for d in range(dp):
                for to, (lo, hi) in zip(sends, parts):
                    first = max(d * rows + lo, k * 256)
                    end = min(d * rows + hi, k * 256 + 256)
                    if first < end:
                        at = d * (hi - lo) + first - d * rows - lo
                        to[at : at + end - first, :] = value[first - k * 256 : end - k * 256, :]

    @pl.when(core == 0)
    def _():
        write_sends(acc2)
        write_keep(acc1)

    @pl.when(core == 1)
    def _():
        write_sends(acc1)
        write_keep(acc2)

    gp_own[...] = gp[pl.ds(pl.multiple_of(core * cells, cells), cells), :]
    gp_other[...] = gp[pl.ds(pl.multiple_of((1 - core) * cells, cells), cells), :].astype(BF)


def main_call(side, height, width, per, dp, chips, first, last, plan, state, weights, rims, blocks, early, stash):
    n = len(blocks)
    big = 2 * height * width + 16
    cells = side * PITCH
    kept = (sds((big, 256), F32),) + (sds((2304, 256), BF),) * 5
    sums = (sds((256, 2304), F32), sds((256, 2304), F32), sds((big, 256), F32))
    ends = (
        sds((2304, 256), BF),
        *(sds((dp * (hi - lo), 256), BF) for lo, hi in chunks_of(2304 // dp)),
        sds((height * width, 256), F32),
        sds((height * width, 256), BF),
    )
    stashed = (
        sds((per, cells, 256), BF),
        sds((per, cells, 256), F32),
        sds((per, cells, 256), F32),
    )
    outs = (kept if first else kept[:1] if rims else ()) + sums + (ends if last else ()) + (stashed if early else ())
    scratch = [
        pltpu.VMEM((cells + 32, 768), BF),
        pltpu.VMEM((cells + 32, 768), BF),
        pltpu.VMEM((cells + 32, 768), BF),
        pltpu.VMEM((side * side // 16 * 16 + packed_rows(side, per)[1], 256), F32),
        pltpu.VMEM((cells, 256), F32),
        pltpu.VMEM((cells, 256), F32),
        pltpu.SMEM((3, 256), jnp.int32),
    ]
    extra = []
    if first:
        extra = [
            pltpu.VMEM(((2 * height + 2) * width, 768), BF),
            pltpu.VMEM((height * width, 256), BF),
            pltpu.SemaphoreType.DMA((4,)),
        ]

    def kernel(*refs):
        refs = list(refs)

        def take(k):
            got = refs[:k]
            del refs[:k]
            return got

        state_refs = take(len(state))
        weight_refs = take(len(weights))
        rim_refs = take(len(rims))
        block_refs = take(n)
        early_refs = take(len(early))
        stash_refs = take(len(stash))
        out_refs = take(len(outs))
        if early:
            stash_refs = out_refs[-3:]
        scratch_refs = take(len(scratch))
        if first:
            pyr, wb1, wb2, w1, w2, wf = out_refs[:6]
            acc1, acc2, gp = out_refs[6:9]
            xp, own, sems = refs
            copies = [
                pltpu.make_async_copy(source, to, sems.at[k])
                for k, (source, to) in enumerate(zip((state_refs[0], *weight_refs), (own, wf, w1, w2)))
            ]
            for copy in copies:
                copy.start()
            for total in (acc1, acc2, gp):
                total[...] = jnp.zeros(total.shape, F32)
            copies[0].wait()
            pyramid_part(height, width, own, state_refs[1], wf, pyr, xp, copies[1])
            copies[2].wait()
            flip_part(w1, wb1)
            copies[3].wait()
            flip_part(w2, wb2)
        else:
            pyr, wb1, wb2, w1, w2, wf = state_refs[:6]
            shared = list(out_refs)
            if rims:
                pyr = shared.pop(0)
                edges_part(height, width, *rim_refs, wf, pyr)
            acc1, acc2, gp = shared[:3]
        if n:
            regions_part(
                *(side, height, width, per, plan, block_refs, early_refs, stash_refs),
                *((pyr, wb1, wb2, w1, w2), (acc1, acc2, gp), scratch_refs),
            )
        if last:
            keep, *sends, gp_own, gp_other = out_refs[3:]
            finish_part(height, width, dp, chips, acc1, acc2, gp, keep, sends, gp_own, gp_other)

    aliases = {} if first else {6: 0, 7: 1, 8: 2}
    if rims:
        aliases = {0: 0, 6: 1, 7: 2, 8: 3}
    return run(
        kernel,
        outs,
        [*state, *weights, *rims, *blocks, *early, *stash],
        scratch=scratch + extra,
        aliases=aliases,
        hbm=(0, *range(len(state), len(state) + len(weights))) if first else (),
    )


def local_kernel(fn, outs, *arrays, **more):
    if isinstance(outs, tuple):
        return run(fn, outs, arrays, **more)
    return run(fn, (outs,), arrays, **more)[0]


def add(a, b):
    return (a.astype(F32) + b.astype(F32)).astype(BF)


def reduce_weights(keep, sends, core_swap, dp, chips, beside, gp_other):
    rows = keep.shape[0] // dp
    bits = dp.bit_length() - 1
    orders = (list(range(bits)), list(reversed(range(bits))))
    shifts = [
        [(2 * z + c, 2 * ((z + k) % chips) + c) for z in range(chips) for c in range(2)]
        for k in range(chips)
    ]
    arrived = [lax.ppermute(send, "tile", core_swap) for send in sends]

    def split(members, bit):
        return [m for m in members if not m & bit], [m for m in members if m & bit]

    class Chunk:
        pass

    def begin(lo, hi, got):
        c = Chunk()
        c.rows = hi - lo
        low = roundup(c.rows // 2, 16)
        c.spans = ((0, low), (low, c.rows))
        c.members = [list(range(dp)), list(range(dp))]

        def first(keep_ref, got_ref, *outs):
            me = lax.axis_index("dp")
            for half in range(2):
                start, size = c.spans[half][0], c.spans[half][1] - c.spans[half][0]
                groups = split(c.members[half], 1 << orders[half][0])
                for out, group in zip(outs[2 * half : 2 * half + 2], groups):
                    for n, m in enumerate(group):
                        a = pl.ds(pl.multiple_of((me ^ m) * rows + lo + start, 16), size)
                        b = pl.ds(pl.multiple_of((me ^ m) * c.rows + start, 16), size)
                        out[n] = add(keep_ref[a, :], got_ref[b, :])

        shapes = []
        for half in range(2):
            shapes += [sds((dp // 2, c.spans[half][1] - c.spans[half][0], 256), BF)] * 2
        c.parts = local_kernel(first, tuple(shapes), keep, got)
        return c

    def exchange(c, stage):
        c.received = []
        for half in range(2):
            bit = 1 << orders[half][stage]
            pairs = [(i, i ^ bit) for i in range(dp)]
            c.received.append(lax.ppermute(c.parts[2 * half + 1], "dp", pairs))
            c.members[half] = split(c.members[half], bit)[0]

    def halve(c, stage):
        shapes = []
        for half in range(2):
            size = c.spans[half][1] - c.spans[half][0]
            shapes += [sds((len(c.members[half]) // 2, size, 256), BF)] * 2
        members = [list(m) for m in c.members]

        def kernel(p, pr, q, qr, *outs):
            for half, (mine, theirs) in enumerate(((p, pr), (q, qr))):
                groups = split(members[half], 1 << orders[half][stage])
                for out, group in zip(outs[2 * half : 2 * half + 2], groups):
                    for n, m in enumerate(group):
                        k = members[half].index(m)
                        out[n] = add(mine[k], theirs[k])

        c.parts = local_kernel(
            kernel, tuple(shapes), c.parts[0], c.received[0], c.parts[2], c.received[1]
        )

    def deal(c):
        c.share = roundup(-(-c.rows // chips), 16)
        low = c.spans[0][1]

        def kernel(p, pr, q, qr, *refs):
            outs, total = refs[:chips], refs[chips]
            chip = lax.axis_index("tile") // 2
            total[0:low, :] = add(p[0], pr[0])
            total[low : c.rows, :] = add(q[0], qr[0])
            if c.share * chips > c.rows:
                total[c.rows :, :] = jnp.zeros((c.share * chips - c.rows, 256), BF)
            for k in range(chips):
                to = lax.rem(chip + k, chips)
                outs[k][...] = total[pl.ds(pl.multiple_of(to * c.share, 16), c.share), :]

        dealt = local_kernel(
            kernel,
            tuple(sds((c.share, 256), BF) for _ in range(chips)),
            *(c.parts[0], c.received[0], c.parts[2], c.received[1]),
            scratch=[pltpu.VMEM((c.share * chips, 256), BF)],
        )
        c.mine = dealt[0]
        c.others = [lax.ppermute(dealt[k], "tile", shifts[k]) for k in range(1, chips)]

    def gather(c):
        def kernel(*refs):
            total = refs[0][...].astype(F32)
            for ref in refs[1:-1]:
                total += ref[...].astype(F32)
            refs[-1][...] = total.astype(BF)

        c.mine = local_kernel(kernel, sds((c.share, 256), BF), c.mine, *c.others)
        c.others = [lax.ppermute(c.mine, "tile", shifts[k]) for k in range(1, chips)]

    def lay(c):
        def kernel(*refs):
            chip = lax.axis_index("tile") // 2
            for k in range(chips):
                source = lax.rem(chip - k + chips, chips)
                refs[-1][pl.ds(pl.multiple_of(source * c.share, 16), c.share), :] = refs[k][...]

        c.whole = local_kernel(kernel, sds((c.share * chips, 256), BF), c.mine, *c.others)
        c.theirs = lax.ppermute(c.whole, "tile", core_swap)

    spans = chunks_of(rows)
    chunks = [begin(lo, hi, got) for (lo, hi), got in zip(spans, arrived)]
    chunks[0].parts = list(chunks[0].parts)
    chunks[0].parts[1], gp_other = lax.optimization_barrier((chunks[0].parts[1], gp_other))
    for c in chunks:
        exchange(c, 0)
    beside = beside(gp_other)
    chunks[0].received[0], beside = lax.optimization_barrier((chunks[0].received[0], beside))
    for stage in range(1, bits):
        for c in chunks:
            halve(c, stage)
            exchange(c, stage)
    for step in (deal, gather, lay):
        for c in chunks:
            step(c)

    def out(*refs):
        core = lax.rem(lax.axis_index("tile"), 2)
        one, two = refs[-2:]

        def write(to, sources):
            for (lo, hi), source in zip(spans, sources):
                to[lo:hi, :] = source[0 : hi - lo, :].astype(F32)

        @pl.when(core == 0)
        def _():
            write(one, refs[0 : len(spans)])
            write(two, refs[len(spans) : -2])

        @pl.when(core == 1)
        def _():
            write(one, refs[len(spans) : -2])
            write(two, refs[0 : len(spans)])

    one, two = local_kernel(
        out,
        (sds((rows, 256), F32), sds((rows, 256), F32)),
        *(c.whole for c in chunks),
        *(c.theirs for c in chunks),
        hbm_out=(0, 1),
    )
    return one, two, beside


def body(features, fpn_weight, mask_w1, mask_w2, owner, row_off, col_off, cotangent):
    tiles = lax.axis_size("tile")
    dp = lax.axis_size("dp")
    chips = tiles // 2
    height, width, channels = features.shape[1:]
    side = cotangent.shape[2]
    swap = [(i, i ^ 1) for i in range(tiles)]

    tile = features.reshape(height * width, channels)
    regions = cotangent.shape[1]
    place = [x.reshape(1, regions) for x in (owner, row_off, col_off)]
    other = lax.ppermute(tile, "tile", swap)
    packed, notes, edge = pack(cotangent[0].transpose(1, 2, 0, 3), tile, height, width, place)
    rim_a = lax.ppermute(
        edge, "tile", [(i, i + 1 if i % 2 else i - 1) for i in range(1, tiles - 1)]
    )
    rim_b = lax.ppermute(rim_a, "tile", swap)

    order = [0] + list(range(1, chips, 2)) + list(range(2, chips, 2))[::-1]
    ring = [
        (2 * z + c, 2 * order[(k + 1) % chips] + c) for k, z in enumerate(order) for c in range(2)
    ]

    flat = lambda w: w.reshape(9 * channels, channels)
    wf, w1, w2 = flat(fpn_weight), flat(mask_w1), flat(mask_w2)
    block = lax.ppermute(packed, "tile", ring)
    notes = lax.ppermute(notes, "tile", [(j, i) for i, j in ring])
    sizes = (side, height, width, regions, dp, chips)
    plan = [1] + [3] * (chips - 3) + [None]
    start = main_call(
        *(*sizes, True, False, plan, [tile, other], [wf, w1, w2], [], [packed], [], [])
    )
    kept, sums, held = list(start[:6]), list(start[6:]), [packed]
    for step in range(1, chips):
        state = kept + sums
        if step == chips - 1:
            got = main_call(*sizes, False, True, [None], state, [], [], [block], [], stash)
            ends = got[3:]
            break
        block, state[0], state[-1], notes, rim_a = lax.optimization_barrier(
            (block, state[0], state[-1], notes, rim_a)
        )
        held = held + [block]
        block = lax.ppermute(block, "tile", ring)
        early = [notes] if step == chips - 2 else []
        rims = [rim_a, rim_b] if step == 1 else []
        got = list(main_call(*sizes, False, False, plan, state, [], rims, held, early, []))
        if rims:
            kept[0] = got.pop(0)
        sums, stash = got[:3], got[3:]
    keep, *sends, gp_own, gp_other = ends

    def join(a, b, out):
        out[...] = (a[...] + b[...].astype(F32)).astype(BF)

    def joined(gp_other):
        gp_got = lax.ppermute(gp_other, "tile", swap)
        return local_kernel(
            join, sds((height * width, channels), BF), gp_own, gp_got, hbm_out=(0,)
        )

    grad_one, grad_two, grad_pyramid = reduce_weights(
        keep, sends, swap, dp, chips, joined, gp_other
    )
    return grad_one, grad_two, grad_pyramid.reshape(1, height, width, channels)


def solution(mesh):
    placed = (
        P("dp", "tile", None, None),
        P(),
        P(),
        P(),
        P("dp", "tile", None),
        P("dp", "tile"),
        P("dp", "tile"),
        P("dp", "tile", None, None, None),
    )
    return jax.shard_map(
        body,
        mesh=mesh,
        in_specs=placed,
        out_specs=(P("dp", None), P("dp", None), P("dp", "tile", None, None)),
        check_vma=False,
    )
```

```python
import functools
import math

import jax
import jax.numpy as jnp
from jax import lax
from jax.experimental import pallas as pl
from jax.experimental.pallas import tpu as pltpu
from jax.sharding import PartitionSpec as P

BF = jnp.bfloat16
F32 = jnp.float32
VMEM_LIMIT = 24 * 1024 * 1024
PITCH = 16


def roundup(n, m):
    return (n + m - 1) // m * m


def run(kernel, outs, args, scratch=(), aliases=None, hbm=(), hbm_out=()):
    args = [
        pltpu.with_memory_space_constraint(x, pltpu.HBM if i in hbm else pltpu.VMEM)
        for i, x in enumerate(args)
    ]
    return pl.pallas_call(
        kernel,
        out_shape=tuple(
            s if i in hbm_out else pltpu.VMEM(s.shape, s.dtype) for i, s in enumerate(outs)
        ),
        in_specs=[
            pl.BlockSpec(memory_space=pltpu.HBM if i in hbm else pltpu.VMEM)
            for i in range(len(args))
        ],
        out_specs=tuple(pl.BlockSpec(memory_space=pltpu.VMEM) for _ in outs),
        scratch_shapes=list(scratch),
        input_output_aliases=aliases or {},
        compiler_params=pltpu.CompilerParams(vmem_limit_bytes=VMEM_LIMIT),
    )(*args)


def sds(shape, dtype):
    return jax.ShapeDtypeStruct(shape, dtype)


def pack_kernel(
    side, height, width, cot, owner, row, col, tile, packed, notes, edge, low, high, wide, tails, places, sems
):
    regions = cot.shape[2]
    core = lax.rem(lax.axis_index("tile"), 2)
    line = pl.ds(pl.multiple_of(core * (height - 1) * width, width), width)
    copies = [pltpu.make_async_copy(tile.at[line, :], edge, sems.at[3])]
    copies += [
        pltpu.make_async_copy(source, places.at[n], sems.at[n])
        for n, source in enumerate((owner, row, col))
    ]
    for copy in copies:
        copy.start()
    for i in range(side):
        for j in range(side):
            at = (i * side + j) * regions
            cell = cot[i, j].astype(F32)
            low[at : at + regions, :] = cell[:, 0:128]
            high[at : at + regions, :] = cell[:, 128:256]
    for copy in copies:
        copy.wait()
    lanes = lax.broadcasted_iota(jnp.int32, (16, 256), 1)
    rows = lax.broadcasted_iota(jnp.int32, (16, 256), 0)
    cells = side * side
    main = cells // 16 * 16
    rest = cells - main
    note = jnp.zeros((16, 256), F32)
    for r in range(regions):
        wide[0:cells, 0:128] = low[pl.ds(r, cells, stride=regions), :]
        wide[0:cells, 128:256] = high[pl.ds(r, cells, stride=regions), :]
        spot = (places[0, 0, r] * height + places[1, 0, r] + 1).astype(F32)
        column = places[2, 0, r].astype(F32)
        value = jnp.where(lanes == 0, spot, jnp.where(lanes == 1, column, 0.0))
        note = jnp.where(rows == r, value, note)
        packed[r * main : r * main + main, :] = wide[0:main, :].astype(BF)
        tails[r * rest : r * rest + rest, :] = wide[main:cells, :]
    at = regions * main
    packed[at : at + tails.shape[0], :] = tails[...].astype(BF)
    at += tails.shape[0]
    packed[at : at + 16, :] = note.astype(BF)
    notes[...] = note.astype(BF)


def packed_rows(side, regions):
    cells = side * side
    return regions * (cells // 16 * 16), roundup(regions * (cells % 16), 16)


def pack(cotangent, tile, height, width, place):
    side, regions = cotangent.shape[0], cotangent.shape[2]
    return local_kernel(
        functools.partial(pack_kernel, side, height, width),
        (
            sds((sum(packed_rows(side, regions)) + 16, 256), BF),
            sds((16, 256), BF),
            sds((width, 256), BF),
        ),
        cotangent,
        *place,
        tile,
        scratch=[
            pltpu.VMEM((side * side * regions, 128), F32),
            pltpu.VMEM((side * side * regions, 128), F32),
            pltpu.VMEM((side * side, 256), F32),
            pltpu.VMEM((packed_rows(side, regions)[1], 256), F32),
            pltpu.SMEM((3, 1, regions), jnp.int32),
            pltpu.SemaphoreType.DMA((4,)),
        ],
        hbm=(1, 2, 3, 4),
    )


def shifted(v, width):
    col = lax.broadcasted_iota(jnp.int32, (width, 256), 0)
    left = jnp.where(col == 0, 0.0, pltpu.roll(v, 1, 0)).astype(BF)
    right = jnp.where(col == width - 1, 0.0, pltpu.roll(v, width - 1, 0)).astype(BF)
    return left, v.astype(BF), right


def pyramid_part(height, width, own, other, wf, pyr, xp, fetched):
    core = lax.rem(lax.axis_index("tile"), 2)
    cells = height * width

    def fill(src, where):
        def step(t, carry):
            v = src[pl.ds(pl.multiple_of(t * width, width), width), :].astype(F32)
            to = pl.ds(pl.multiple_of(where + t * width, width), width)
            for b, piece in enumerate(shifted(v, width)):
                xp[to, b * 256 : b * 256 + 256] = piece
            return carry

        lax.fori_loop(0, height, step, 0)

    bottom = width + 2 * cells
    fill(own, width + core * cells)
    fill(other, width + (1 - core) * cells)
    xp[0:width, :] = jnp.zeros((width, 768), BF)
    xp[bottom : bottom + width, :] = jnp.zeros((width, 768), BF)
    fetched.wait()

    def conv(t, carry):
        at = t * 512
        total = jnp.zeros((512, 256), F32)
        for a in range(3):
            piece = xp[pl.ds(pl.multiple_of(at + a * width, 64), 512), :]
            total += jnp.dot(piece, wf[a * 768 : a * 768 + 768, :], preferred_element_type=F32)
        cell = at + lax.broadcasted_iota(jnp.int32, (512, 256), 0)
        open_row = (cell < width) | (cell >= 2 * cells - width)
        pyr[pl.ds(pl.multiple_of(at, 512), 512), :] = jnp.where(
            open_row, total, total.astype(BF).astype(F32)
        )
        return carry

    lax.fori_loop(0, 2 * cells // 512, conv, 0)
    pyr[2 * cells : 2 * cells + 16, :] = jnp.zeros((16, 256), F32)


def edges_part(height, width, rim_a, rim_b, wf, pyr):
    core = lax.rem(lax.axis_index("tile"), 2)
    last = 2 * height * width - width

    def close(rim, at, tap):
        total = pyr[at : at + width, :]
        for b, piece in enumerate(shifted(rim[...].astype(F32), width)):
            k = 3 * tap + b
            total += jnp.dot(piece, wf[k * 256 : k * 256 + 256, :], preferred_element_type=F32)
        pyr[at : at + width, :] = total.astype(BF).astype(F32)

    @pl.when(core == 0)
    def _():
        close(rim_a, 0, 0)
        close(rim_b, last, 2)

    @pl.when(core == 1)
    def _():
        close(rim_b, 0, 0)
        close(rim_a, last, 2)


def flip_part(w, wb):
    for k in range(9):
        block = w[(8 - k) * 256 : (9 - k) * 256, :].astype(F32)
        wb[k * 256 : k * 256 + 256, :] = block.T.astype(BF)


def gelu_pair(v):
    c = math.sqrt(2.0 / math.pi)
    sq = v * v
    t = jnp.tanh(c * (v + 0.044715 * (sq * v)))
    half = 0.5 * (1.0 + t)
    slope = half + 0.5 * v * (1.0 - t * t) * (c * (1.0 + 3 * 0.044715 * sq))
    return v * half, slope


def regions_part(side, height, width, per, plan, blocks, early, stash, tables, sums, scratch):
    pyr, wb1, wb2, w1, w2 = tables
    acc1, acc2, gp = sums
    xs, hs, gs, wide, vs, slope1, todo = scratch
    chip = lax.axis_index("tile") // 2
    lanes = lax.broadcasted_iota(jnp.int32, (16, 256), 1)
    rows16 = lax.broadcasted_iota(jnp.int32, (16, 256), 0)
    in_row = rows16 < side
    cells = side * PITCH
    inside = (lax.broadcasted_iota(jnp.int32, (cells, 256), 0) & (PITCH - 1)) < side
    used = pl.ds(16, cells)
    main, tails = packed_rows(side, per)
    one = main // per
    rest = side * side - one

    count = jnp.int32(0)
    start, end = jnp.int32(0), jnp.int32(0)

    def enlist(count, s, r, note, wanted=None):
        note = jnp.where(rows16 == r, note.astype(F32), 0.0)
        spot = jnp.sum(jnp.where(lanes == 0, note, 0.0)).astype(jnp.int32) - 1
        column = jnp.sum(jnp.where(lanes == 1, note, 0.0)).astype(jnp.int32)
        local = spot - chip * 2 * height
        here = (spot >= 0) & (local >= 0) & (local < 2 * height)
        if wanted is not None:
            outer = (local == 0) | (local == 2 * height - side)
            here = here & (outer == wanted)
        todo[0, count] = jnp.int32(s * per + r)
        todo[1, count] = jnp.where(here, local * width + column // 8 * 8, 0)
        todo[2, count] = jnp.where(here, lax.rem(column, 8), 0)
        return count + here.astype(jnp.int32)

    def scan(s, wanted):
        note = blocks[s][main + tails : main + tails + 16, :]
        found = count
        for r in range(per):
            found = enlist(found, s, r, note, wanted)
        return found

    for s, most in enumerate(plan[: len(blocks)]):
        if s == 2:
            count = scan(0, True)
            count = scan(1, True)
        count = scan(s, False if s < 2 and len(plan) > 1 else None)
        start, end = end, count if most is None else jnp.minimum(count, end + most)
    total = count
    for note in early:
        for r in range(per):
            count = enlist(count, len(blocks), r, note[...])

    for buf in (xs, hs, gs):
        buf[0:16, :] = jnp.zeros((16, 768), BF)
        buf[cells + 16 : cells + 32, :] = jnp.zeros((16, 768), BF)

    def put(buf, v):
        buf[used, 0:256] = pltpu.roll(v, 1, 0).astype(BF)
        buf[used, 256:512] = v.astype(BF)
        buf[used, 512:768] = pltpu.roll(v, cells - 1, 0).astype(BF)

    def conv(buf, w):
        total = jnp.zeros((cells, 256), F32)
        for a in range(3):
            total += jnp.dot(
                buf[a * 16 : a * 16 + cells, :],
                w[a * 768 : a * 768 + 768, :],
                preferred_element_type=F32,
            )
        return total

    def taps(acc, buf, grad):
        turned = grad.T.astype(BF)
        for a in range(3):
            acc[:, a * 768 : a * 768 + 768] += jnp.dot(
                turned, buf[a * 16 : a * 16 + cells, :], preferred_element_type=F32
            )

    def crop(n):
        base, lead = todo[1, n], todo[2, n]
        for i in range(side):
            got = pyr[pl.ds(pl.multiple_of(base + i * width, 8), 24), :]
            got = pltpu.roll(got, lax.rem(24 - lead, 24), 0)[0:16]
            vs[i * 16 : i * 16 + 16, :] = jnp.where(in_row, got, 0.0)
        put(xs, vs[...])

    def forward(n):
        crop(n)
        act1, slope = gelu_pair(conv(xs, w1))
        slope1[...] = slope
        act1 = jnp.where(inside, act1, 0.0)
        put(hs, act1)
        _, slope = gelu_pair(conv(hs, w2))
        return act1, slope

    def backward(n, slope2):
        which = todo[0, n]
        base, lead = todo[1, n], todo[2, n]
        for s, block in enumerate(blocks):

            @pl.when(which // per == s)
            def _(block=block):
                r = lax.rem(which, per)
                cell = pl.ds(pl.multiple_of(r * one, 16), one)
                wide[0:one, :] = block[cell, :].astype(F32)
                left = block[main : main + tails, :].astype(F32)
                wide[one : one + tails, :] = pltpu.roll(left, lax.rem(tails - r * rest, tails), 0)

        for i in range(side):
            got = wide[i * side : i * side + 16, :]
            vs[i * 16 : i * 16 + 16, :] = jnp.where(in_row, got, 0.0)
        g2 = vs[...] * slope2
        put(gs, g2)
        taps(acc2, hs, g2)
        g1 = jnp.where(inside, conv(gs, wb2) * slope1[...], 0.0)
        put(gs, g1)
        taps(acc1, xs, g1)
        vs[...] = jnp.where(inside, conv(gs, wb1), 0.0).astype(BF).astype(F32)
        for i in range(side):
            at = pl.ds(pl.multiple_of(base + i * width, 8), 24)
            piece = jnp.concatenate([vs[i * 16 : i * 16 + 16, :], jnp.zeros((8, 256), F32)])
            gp[at, :] = gp[at, :] + pltpu.roll(piece, lead, 0)

    def whole(n, carry):
        _, slope2 = forward(n)
        backward(n, slope2)
        return carry

    def ahead(n, carry):
        r = lax.rem(todo[0, n], per)
        act1, slope2 = forward(n)
        stash[0][r] = act1.astype(BF)
        stash[1][r] = slope1[...]
        stash[2][r] = slope2
        return carry

    def behind(n, carry):
        r = lax.rem(todo[0, n], per)
        crop(n)
        put(hs, stash[0][r].astype(F32))
        slope1[...] = stash[1][r]
        backward(n, stash[2][r])
        return carry

    if early:
        lax.fori_loop(start, end, whole, 0)
        lax.fori_loop(total, count, ahead, 0)
    elif stash:
        lax.fori_loop(0, total, behind, 0)
    else:
        lax.fori_loop(start, end, whole, 0)


def chunks_of(rows):
    return ((0, rows),)


def finish_part(height, width, dp, chips, acc1, acc2, gp, keep, sends, gp_own, gp_other):
    core = lax.rem(lax.axis_index("tile"), 2)
    cells = height * width
    rows = 2304 // dp
    parts = chunks_of(rows)

    def write_keep(acc):
        for k in range(9):
            keep[k * 256 : k * 256 + 256, :] = acc[:, k * 256 : k * 256 + 256].T.astype(BF)

    def write_sends(acc):
        for k in range(9):
            value = acc[:, k * 256 : k * 256 + 256].T.astype(BF)
            for d in range(dp):
                for to, (lo, hi) in zip(sends, parts):
                    first = max(d * rows + lo, k * 256)
                    end = min(d * rows + hi, k * 256 + 256)
                    if first < end:
                        at = d * (hi - lo) + first - d * rows - lo
                        to[at : at + end - first, :] = value[first - k * 256 : end - k * 256, :]

    @pl.when(core == 0)
    def _():
        write_sends(acc2)
        write_keep(acc1)

    @pl.when(core == 1)
    def _():
        write_sends(acc1)
        write_keep(acc2)

    gp_own[...] = gp[pl.ds(pl.multiple_of(core * cells, cells), cells), :]
    gp_other[...] = gp[pl.ds(pl.multiple_of((1 - core) * cells, cells), cells), :].astype(BF)


def main_call(side, height, width, per, dp, chips, first, last, plan, state, weights, rims, blocks, early, stash):
    n = len(blocks)
    big = 2 * height * width + 16
    cells = side * PITCH
    kept = (sds((big, 256), F32),) + (sds((2304, 256), BF),) * 5
    sums = (sds((256, 2304), F32), sds((256, 2304), F32), sds((big, 256), F32))
    ends = (
        sds((2304, 256), BF),
        *(sds((dp * (hi - lo), 256), BF) for lo, hi in chunks_of(2304 // dp)),
        sds((height * width, 256), F32),
        sds((height * width, 256), BF),
    )
    stashed = (
        sds((per, cells, 256), BF),
        sds((per, cells, 256), F32),
        sds((per, cells, 256), F32),
    )
    outs = (kept if first else kept[:1] if rims else ()) + sums + (ends if last else ()) + (stashed if early else ())
    scratch = [
        pltpu.VMEM((cells + 32, 768), BF),
        pltpu.VMEM((cells + 32, 768), BF),
        pltpu.VMEM((cells + 32, 768), BF),
        pltpu.VMEM((side * side // 16 * 16 + packed_rows(side, per)[1], 256), F32),
        pltpu.VMEM((cells, 256), F32),
        pltpu.VMEM((cells, 256), F32),
        pltpu.SMEM((3, 256), jnp.int32),
    ]
    extra = []
    if first:
        extra = [
            pltpu.VMEM(((2 * height + 2) * width, 768), BF),
            pltpu.VMEM((height * width, 256), BF),
            pltpu.SemaphoreType.DMA((4,)),
        ]

    def kernel(*refs):
        refs = list(refs)

        def take(k):
            got = refs[:k]
            del refs[:k]
            return got

        state_refs = take(len(state))
        weight_refs = take(len(weights))
        rim_refs = take(len(rims))
        block_refs = take(n)
        early_refs = take(len(early))
        stash_refs = take(len(stash))
        out_refs = take(len(outs))
        if early:
            stash_refs = out_refs[-3:]
        scratch_refs = take(len(scratch))
        if first:
            pyr, wb1, wb2, w1, w2, wf = out_refs[:6]
            acc1, acc2, gp = out_refs[6:9]
            xp, own, sems = refs
            copies = [
                pltpu.make_async_copy(source, to, sems.at[k])
                for k, (source, to) in enumerate(zip((state_refs[0], *weight_refs), (own, wf, w1, w2)))
            ]
            for copy in copies:
                copy.start()
            for total in (acc1, acc2, gp):
                total[...] = jnp.zeros(total.shape, F32)
            copies[0].wait()
            pyramid_part(height, width, own, state_refs[1], wf, pyr, xp, copies[1])
            copies[2].wait()
            flip_part(w1, wb1)
            copies[3].wait()
            flip_part(w2, wb2)
        else:
            pyr, wb1, wb2, w1, w2, wf = state_refs[:6]
            shared = list(out_refs)
            if rims:
                pyr = shared.pop(0)
                edges_part(height, width, *rim_refs, wf, pyr)
            acc1, acc2, gp = shared[:3]
        if n:
            regions_part(
                *(side, height, width, per, plan, block_refs, early_refs, stash_refs),
                *((pyr, wb1, wb2, w1, w2), (acc1, acc2, gp), scratch_refs),
            )
        if last:
            keep, *sends, gp_own, gp_other = out_refs[3:]
            finish_part(height, width, dp, chips, acc1, acc2, gp, keep, sends, gp_own, gp_other)

    aliases = {} if first else {6: 0, 7: 1, 8: 2}
    if rims:
        aliases = {0: 0, 6: 1, 7: 2, 8: 3}
    return run(
        kernel,
        outs,
        [*state, *weights, *rims, *blocks, *early, *stash],
        scratch=scratch + extra,
        aliases=aliases,
        hbm=(0, *range(len(state), len(state) + len(weights))) if first else (),
    )


def local_kernel(fn, outs, *arrays, **more):
    if isinstance(outs, tuple):
        return run(fn, outs, arrays, **more)
    return run(fn, (outs,), arrays, **more)[0]


def add(a, b):
    return (a.astype(F32) + b.astype(F32)).astype(BF)


def reduce_weights(keep, sends, core_swap, dp, chips, beside, gp_other):
    rows = keep.shape[0] // dp
    bits = dp.bit_length() - 1
    orders = (list(range(bits)), list(reversed(range(bits))))
    shifts = [
        [(2 * z + c, 2 * ((z + k) % chips) + c) for z in range(chips) for c in range(2)]
        for k in range(chips)
    ]
    arrived = [lax.ppermute(send, "tile", core_swap) for send in sends]

    def split(members, bit):
        return [m for m in members if not m & bit], [m for m in members if m & bit]

    class Chunk:
        pass

    def begin(lo, hi, got):
        c = Chunk()
        c.rows = hi - lo
        low = roundup(c.rows // 2, 16)
        c.spans = ((0, low), (low, c.rows))
        c.members = [list(range(dp)), list(range(dp))]

        def first(keep_ref, got_ref, *outs):
            me = lax.axis_index("dp")
            for half in range(2):
                start, size = c.spans[half][0], c.spans[half][1] - c.spans[half][0]
                groups = split(c.members[half], 1 << orders[half][0])
                for out, group in zip(outs[2 * half : 2 * half + 2], groups):
                    for n, m in enumerate(group):
                        a = pl.ds(pl.multiple_of((me ^ m) * rows + lo + start, 16), size)
                        b = pl.ds(pl.multiple_of((me ^ m) * c.rows + start, 16), size)
                        out[n] = add(keep_ref[a, :], got_ref[b, :])

        shapes = []
        for half in range(2):
            shapes += [sds((dp // 2, c.spans[half][1] - c.spans[half][0], 256), BF)] * 2
        c.parts = local_kernel(first, tuple(shapes), keep, got)
        return c

    def exchange(c, stage):
        c.received = []
        for half in range(2):
            bit = 1 << orders[half][stage]
            pairs = [(i, i ^ bit) for i in range(dp)]
            c.received.append(lax.ppermute(c.parts[2 * half + 1], "dp", pairs))
            c.members[half] = split(c.members[half], bit)[0]

    def halve(c, stage):
        shapes = []
        for half in range(2):
            size = c.spans[half][1] - c.spans[half][0]
            shapes += [sds((len(c.members[half]) // 2, size, 256), BF)] * 2
        members = [list(m) for m in c.members]

        def kernel(p, pr, q, qr, *outs):
            for half, (mine, theirs) in enumerate(((p, pr), (q, qr))):
                groups = split(members[half], 1 << orders[half][stage])
                for out, group in zip(outs[2 * half : 2 * half + 2], groups):
                    for n, m in enumerate(group):
                        k = members[half].index(m)
                        out[n] = add(mine[k], theirs[k])

        c.parts = local_kernel(
            kernel, tuple(shapes), c.parts[0], c.received[0], c.parts[2], c.received[1]
        )

    def deal(c):
        c.share = roundup(-(-c.rows // chips), 16)
        low = c.spans[0][1]

        def kernel(p, pr, q, qr, *refs):
            outs, total = refs[:chips], refs[chips]
            chip = lax.axis_index("tile") // 2
            total[0:low, :] = add(p[0], pr[0])
            total[low : c.rows, :] = add(q[0], qr[0])
            if c.share * chips > c.rows:
                total[c.rows :, :] = jnp.zeros((c.share * chips - c.rows, 256), BF)
            for k in range(chips):
                to = lax.rem(chip + k, chips)
                outs[k][...] = total[pl.ds(pl.multiple_of(to * c.share, 16), c.share), :]

        dealt = local_kernel(
            kernel,
            tuple(sds((c.share, 256), BF) for _ in range(chips)),
            *(c.parts[0], c.received[0], c.parts[2], c.received[1]),
            scratch=[pltpu.VMEM((c.share * chips, 256), BF)],
        )
        c.mine = dealt[0]
        c.others = [lax.ppermute(dealt[k], "tile", shifts[k]) for k in range(1, chips)]

    def gather(c):
        def kernel(*refs):
            total = refs[0][...].astype(F32)
            for ref in refs[1:-1]:
                total += ref[...].astype(F32)
            refs[-1][...] = total.astype(BF)

        c.mine = local_kernel(kernel, sds((c.share, 256), BF), c.mine, *c.others)
        c.others = [lax.ppermute(c.mine, "tile", shifts[k]) for k in range(1, chips)]

    def lay(c):
        def kernel(*refs):
            chip = lax.axis_index("tile") // 2
            for k in range(chips):
                source = lax.rem(chip - k + chips, chips)
                refs[-1][pl.ds(pl.multiple_of(source * c.share, 16), c.share), :] = refs[k][...]

        c.whole = local_kernel(kernel, sds((c.share * chips, 256), BF), c.mine, *c.others)
        c.theirs = lax.ppermute(c.whole, "tile", core_swap)

    spans = chunks_of(rows)
    chunks = [begin(lo, hi, got) for (lo, hi), got in zip(spans, arrived)]
    chunks[0].parts = list(chunks[0].parts)
    chunks[0].parts[1], gp_other = lax.optimization_barrier((chunks[0].parts[1], gp_other))
    for c in chunks:
        exchange(c, 0)
    beside = beside(gp_other)
    chunks[0].received[0], beside = lax.optimization_barrier((chunks[0].received[0], beside))
    for stage in range(1, bits):
        for c in chunks:
            halve(c, stage)
            exchange(c, stage)
    for step in (deal, gather, lay):
        for c in chunks:
            step(c)

    def out(*refs):
        core = lax.rem(lax.axis_index("tile"), 2)
        one, two = refs[-2:]

        def write(to, sources):
            for (lo, hi), source in zip(spans, sources):
                to[lo:hi, :] = source[0 : hi - lo, :].astype(F32)

        @pl.when(core == 0)
        def _():
            write(one, refs[0 : len(spans)])
            write(two, refs[len(spans) : -2])

        @pl.when(core == 1)
        def _():
            write(one, refs[len(spans) : -2])
            write(two, refs[0 : len(spans)])

    one, two = local_kernel(
        out,
        (sds((rows, 256), F32), sds((rows, 256), F32)),
        *(c.whole for c in chunks),
        *(c.theirs for c in chunks),
        hbm_out=(0, 1),
    )
    return one, two, beside


def body(features, fpn_weight, mask_w1, mask_w2, owner, row_off, col_off, cotangent):
    tiles = lax.axis_size("tile")
    dp = lax.axis_size("dp")
    chips = tiles // 2
    height, width, channels = features.shape[1:]
    side = cotangent.shape[2]
    swap = [(i, i ^ 1) for i in range(tiles)]

    tile = features.reshape(height * width, channels)
    regions = cotangent.shape[1]
    place = [x.reshape(1, regions) for x in (owner, row_off, col_off)]
    other = lax.ppermute(tile, "tile", swap)
    packed, notes, edge = pack(cotangent[0].transpose(1, 2, 0, 3), tile, height, width, place)

    order = [0] + list(range(1, chips, 2)) + list(range(2, chips, 2))[::-1]
    ring = [
        (2 * z + c, 2 * order[(k + 1) % chips] + c) for k, z in enumerate(order) for c in range(2)
    ]

    flat = lambda w: w.reshape(9 * channels, channels)
    wf, w1, w2 = flat(fpn_weight), flat(mask_w1), flat(mask_w2)
    block = lax.ppermute(packed, "tile", ring)
    sizes = (side, height, width, regions, dp, chips)
    plan = [1] + [3] * (chips - 3) + [None]
    start = main_call(
        *(*sizes, True, False, plan, [tile, other], [wf, w1, w2], [], [packed], [], [])
    )
    kept, sums, held = list(start[:6]), list(start[6:]), [packed]
    edge, notes, kept[0] = lax.optimization_barrier((edge, notes, kept[0]))
    rim_a = lax.ppermute(
        edge, "tile", [(i, i + 1 if i % 2 else i - 1) for i in range(1, tiles - 1)]
    )
    notes = lax.ppermute(notes, "tile", [(j, i) for i, j in ring])
    for step in range(1, chips):
        state = kept + sums
        if step == chips - 1:
            got = main_call(*sizes, False, True, [None], state, [], [], [block], [], stash)
            ends = got[3:]
            break
        block, state[0], state[-1] = lax.optimization_barrier((block, state[0], state[-1]))
        if step == 1:
            block, rim_a = lax.optimization_barrier((block, rim_a))
        if step == 2:
            block, notes, rim_b = lax.optimization_barrier((block, notes, rim_b))
        held = held + [block]
        block = lax.ppermute(block, "tile", ring)
        if step == 1:
            rim_b = lax.ppermute(rim_a, "tile", swap)
        early = [notes] if step == chips - 2 else []
        rims = [rim_a, rim_b] if step == 2 else []
        got = list(main_call(*sizes, False, False, plan, state, [], rims, held, early, []))
        if rims:
            kept[0] = got.pop(0)
        sums, stash = got[:3], got[3:]
    keep, *sends, gp_own, gp_other = ends

    def join(a, b, out):
        out[...] = (a[...] + b[...].astype(F32)).astype(BF)

    def joined(gp_other):
        gp_got = lax.ppermute(gp_other, "tile", swap)
        return local_kernel(
            join, sds((height * width, channels), BF), gp_own, gp_got, hbm_out=(0,)
        )

    grad_one, grad_two, grad_pyramid = reduce_weights(
        keep, sends, swap, dp, chips, joined, gp_other
    )
    return grad_one, grad_two, grad_pyramid.reshape(1, height, width, channels)


def solution(mesh):
    placed = (
        P("dp", "tile", None, None),
        P(),
        P(),
        P(),
        P("dp", "tile", None),
        P("dp", "tile"),
        P("dp", "tile"),
        P("dp", "tile", None, None, None),
    )
    return jax.shard_map(
        body,
        mesh=mesh,
        in_specs=placed,
        out_specs=(P("dp", None), P("dp", None), P("dp", "tile", None, None)),
        check_vma=False,
    )
```

```python
import functools
import math

import jax
import jax.numpy as jnp
from jax import lax
from jax.experimental import pallas as pl
from jax.experimental.pallas import tpu as pltpu
from jax.sharding import PartitionSpec as P

BF = jnp.bfloat16
F32 = jnp.float32
VMEM_LIMIT = 24 * 1024 * 1024
PITCH = 16


def roundup(n, m):
    return (n + m - 1) // m * m


def run(kernel, outs, args, scratch=(), aliases=None, hbm=(), hbm_out=()):
    args = [
        pltpu.with_memory_space_constraint(x, pltpu.HBM if i in hbm else pltpu.VMEM)
        for i, x in enumerate(args)
    ]
    return pl.pallas_call(
        kernel,
        out_shape=tuple(
            s if i in hbm_out else pltpu.VMEM(s.shape, s.dtype) for i, s in enumerate(outs)
        ),
        in_specs=[
            pl.BlockSpec(memory_space=pltpu.HBM if i in hbm else pltpu.VMEM)
            for i in range(len(args))
        ],
        out_specs=tuple(pl.BlockSpec(memory_space=pltpu.VMEM) for _ in outs),
        scratch_shapes=list(scratch),
        input_output_aliases=aliases or {},
        compiler_params=pltpu.CompilerParams(vmem_limit_bytes=VMEM_LIMIT),
    )(*args)


def sds(shape, dtype):
    return jax.ShapeDtypeStruct(shape, dtype)


def pack_kernel(
    side, height, width, cot, owner, row, col, tile, packed, notes, edge, low, high, wide, tails, places, sems
):
    regions = cot.shape[2]
    core = lax.rem(lax.axis_index("tile"), 2)
    line = pl.ds(pl.multiple_of(core * (height - 1) * width, width), width)
    copies = [pltpu.make_async_copy(tile.at[line, :], edge, sems.at[3])]
    copies += [
        pltpu.make_async_copy(source, places.at[n], sems.at[n])
        for n, source in enumerate((owner, row, col))
    ]
    for copy in copies:
        copy.start()
    for i in range(side):
        for j in range(side):
            at = (i * side + j) * regions
            cell = cot[i, j].astype(F32)
            low[at : at + regions, :] = cell[:, 0:128]
            high[at : at + regions, :] = cell[:, 128:256]
    for copy in copies:
        copy.wait()
    lanes = lax.broadcasted_iota(jnp.int32, (16, 256), 1)
    rows = lax.broadcasted_iota(jnp.int32, (16, 256), 0)
    cells = side * side
    main = cells // 16 * 16
    rest = cells - main
    note = jnp.zeros((16, 256), F32)
    for r in range(regions):
        wide[0:cells, 0:128] = low[pl.ds(r, cells, stride=regions), :]
        wide[0:cells, 128:256] = high[pl.ds(r, cells, stride=regions), :]
        spot = (places[0, 0, r] * height + places[1, 0, r] + 1).astype(F32)
        column = places[2, 0, r].astype(F32)
        value = jnp.where(lanes == 0, spot, jnp.where(lanes == 1, column, 0.0))
        note = jnp.where(rows == r, value, note)
        packed[r * main : r * main + main, :] = wide[0:main, :].astype(BF)
        tails[r * rest : r * rest + rest, :] = wide[main:cells, :]
    at = regions * main
    packed[at : at + tails.shape[0], :] = tails[...].astype(BF)
    at += tails.shape[0]
    packed[at : at + 16, :] = note.astype(BF)
    notes[...] = note.astype(BF)


def packed_rows(side, regions):
    cells = side * side
    return regions * (cells // 16 * 16), roundup(regions * (cells % 16), 16)


def pack(cotangent, tile, height, width, place):
    side, regions = cotangent.shape[0], cotangent.shape[2]
    return local_kernel(
        functools.partial(pack_kernel, side, height, width),
        (
            sds((sum(packed_rows(side, regions)) + 16, 256), BF),
            sds((16, 256), BF),
            sds((width, 256), BF),
        ),
        cotangent,
        *place,
        tile,
        scratch=[
            pltpu.VMEM((side * side * regions, 128), F32),
            pltpu.VMEM((side * side * regions, 128), F32),
            pltpu.VMEM((side * side, 256), F32),
            pltpu.VMEM((packed_rows(side, regions)[1], 256), F32),
            pltpu.SMEM((3, 1, regions), jnp.int32),
            pltpu.SemaphoreType.DMA((4,)),
        ],
        hbm=(1, 2, 3, 4),
    )


def shifted(v, width):
    col = lax.broadcasted_iota(jnp.int32, (width, 256), 0)
    left = jnp.where(col == 0, 0.0, pltpu.roll(v, 1, 0)).astype(BF)
    right = jnp.where(col == width - 1, 0.0, pltpu.roll(v, width - 1, 0)).astype(BF)
    return left, v.astype(BF), right


def pyramid_part(height, width, own, other, wf, pyr, xp, fetched):
    core = lax.rem(lax.axis_index("tile"), 2)
    cells = height * width

    def fill(src, where):
        def step(t, carry):
            v = src[pl.ds(pl.multiple_of(t * width, width), width), :].astype(F32)
            to = pl.ds(pl.multiple_of(where + t * width, width), width)
            for b, piece in enumerate(shifted(v, width)):
                xp[to, b * 256 : b * 256 + 256] = piece
            return carry

        lax.fori_loop(0, height, step, 0)

    bottom = width + 2 * cells
    fill(own, width + core * cells)
    fill(other, width + (1 - core) * cells)
    xp[0:width, :] = jnp.zeros((width, 768), BF)
    xp[bottom : bottom + width, :] = jnp.zeros((width, 768), BF)
    fetched.wait()

    def conv(t, carry):
        at = t * 512
        total = jnp.zeros((512, 256), F32)
        for a in range(3):
            piece = xp[pl.ds(pl.multiple_of(at + a * width, 64), 512), :]
            total += jnp.dot(piece, wf[a * 768 : a * 768 + 768, :], preferred_element_type=F32)
        cell = at + lax.broadcasted_iota(jnp.int32, (512, 256), 0)
        open_row = (cell < width) | (cell >= 2 * cells - width)
        pyr[pl.ds(pl.multiple_of(at, 512), 512), :] = jnp.where(
            open_row, total, total.astype(BF).astype(F32)
        )
        return carry

    lax.fori_loop(0, 2 * cells // 512, conv, 0)
    pyr[2 * cells : 2 * cells + 16, :] = jnp.zeros((16, 256), F32)


def edges_part(height, width, rim_a, rim_b, wf, pyr):
    core = lax.rem(lax.axis_index("tile"), 2)
    last = 2 * height * width - width

    def close(rim, at, tap):
        total = pyr[at : at + width, :]
        for b, piece in enumerate(shifted(rim[...].astype(F32), width)):
            k = 3 * tap + b
            total += jnp.dot(piece, wf[k * 256 : k * 256 + 256, :], preferred_element_type=F32)
        pyr[at : at + width, :] = total.astype(BF).astype(F32)

    @pl.when(core == 0)
    def _():
        close(rim_a, 0, 0)
        close(rim_b, last, 2)

    @pl.when(core == 1)
    def _():
        close(rim_b, 0, 0)
        close(rim_a, last, 2)


def flip_part(w, wb):
    for k in range(9):
        block = w[(8 - k) * 256 : (9 - k) * 256, :].astype(F32)
        wb[k * 256 : k * 256 + 256, :] = block.T.astype(BF)


def gelu_pair(v):
    c = math.sqrt(2.0 / math.pi)
    sq = v * v
    t = jnp.tanh(c * (v + 0.044715 * (sq * v)))
    half = 0.5 * (1.0 + t)
    slope = half + 0.5 * v * (1.0 - t * t) * (c * (1.0 + 3 * 0.044715 * sq))
    return v * half, slope


def regions_part(side, height, width, per, plan, blocks, early, stash, tables, sums, scratch):
    pyr, wb1, wb2, w1, w2 = tables
    acc1, acc2, gp = sums
    xs, hs, gs, wide, vs, slope1, todo = scratch
    chip = lax.axis_index("tile") // 2
    lanes = lax.broadcasted_iota(jnp.int32, (16, 256), 1)
    rows16 = lax.broadcasted_iota(jnp.int32, (16, 256), 0)
    in_row = rows16 < side
    cells = side * PITCH
    inside = (lax.broadcasted_iota(jnp.int32, (cells, 256), 0) & (PITCH - 1)) < side
    used = pl.ds(16, cells)
    main, tails = packed_rows(side, per)
    one = main // per
    rest = side * side - one

    count = jnp.int32(0)
    start, end = jnp.int32(0), jnp.int32(0)

    def enlist(count, s, r, note, wanted=None):
        note = jnp.where(rows16 == r, note.astype(F32), 0.0)
        spot = jnp.sum(jnp.where(lanes == 0, note, 0.0)).astype(jnp.int32) - 1
        column = jnp.sum(jnp.where(lanes == 1, note, 0.0)).astype(jnp.int32)
        local = spot - chip * 2 * height
        here = (spot >= 0) & (local >= 0) & (local < 2 * height)
        if wanted is not None:
            outer = (local == 0) | (local == 2 * height - side)
            here = here & (outer == wanted)
        todo[0, count] = jnp.int32(s * per + r)
        todo[1, count] = jnp.where(here, local * width + column // 8 * 8, 0)
        todo[2, count] = jnp.where(here, lax.rem(column, 8), 0)
        return count + here.astype(jnp.int32)

    def scan(s, wanted):
        note = blocks[s][main + tails : main + tails + 16, :]
        found = count
        for r in range(per):
            found = enlist(found, s, r, note, wanted)
        return found

    for s, most in enumerate(plan[: len(blocks)]):
        if s == 1:
            count = scan(0, True)
        count = scan(s, False if s == 0 and len(plan) > 1 else None)
        start, end = end, count if most is None else jnp.minimum(count, end + most)
    total = count
    for note in early:
        for r in range(per):
            count = enlist(count, len(blocks), r, note[...])

    for buf in (xs, hs, gs):
        buf[0:16, :] = jnp.zeros((16, 768), BF)
        buf[cells + 16 : cells + 32, :] = jnp.zeros((16, 768), BF)

    def put(buf, v):
        buf[used, 0:256] = pltpu.roll(v, 1, 0).astype(BF)
        buf[used, 256:512] = v.astype(BF)
        buf[used, 512:768] = pltpu.roll(v, cells - 1, 0).astype(BF)

    def conv(buf, w):
        total = jnp.zeros((cells, 256), F32)
        for a in range(3):
            total += jnp.dot(
                buf[a * 16 : a * 16 + cells, :],
                w[a * 768 : a * 768 + 768, :],
                preferred_element_type=F32,
            )
        return total

    def taps(acc, buf, grad):
        turned = grad.T.astype(BF)
        for a in range(3):
            acc[:, a * 768 : a * 768 + 768] += jnp.dot(
                turned, buf[a * 16 : a * 16 + cells, :], preferred_element_type=F32
            )

    def crop(n):
        base, lead = todo[1, n], todo[2, n]
        for i in range(side):
            got = pyr[pl.ds(pl.multiple_of(base + i * width, 8), 24), :]
            got = pltpu.roll(got, lax.rem(24 - lead, 24), 0)[0:16]
            vs[i * 16 : i * 16 + 16, :] = jnp.where(in_row, got, 0.0)
        put(xs, vs[...])

    def forward(n):
        crop(n)
        act1, slope = gelu_pair(conv(xs, w1))
        slope1[...] = slope
        act1 = jnp.where(inside, act1, 0.0)
        put(hs, act1)
        _, slope = gelu_pair(conv(hs, w2))
        return act1, slope

    def backward(n, slope2):
        which = todo[0, n]
        base, lead = todo[1, n], todo[2, n]
        for s, block in enumerate(blocks):

            @pl.when(which // per == s)
            def _(block=block):
                r = lax.rem(which, per)
                cell = pl.ds(pl.multiple_of(r * one, 16), one)
                wide[0:one, :] = block[cell, :].astype(F32)
                left = block[main : main + tails, :].astype(F32)
                wide[one : one + tails, :] = pltpu.roll(left, lax.rem(tails - r * rest, tails), 0)

        for i in range(side):
            got = wide[i * side : i * side + 16, :]
            vs[i * 16 : i * 16 + 16, :] = jnp.where(in_row, got, 0.0)
        g2 = vs[...] * slope2
        put(gs, g2)
        taps(acc2, hs, g2)
        g1 = jnp.where(inside, conv(gs, wb2) * slope1[...], 0.0)
        put(gs, g1)
        taps(acc1, xs, g1)
        vs[...] = jnp.where(inside, conv(gs, wb1), 0.0).astype(BF).astype(F32)
        for i in range(side):
            at = pl.ds(pl.multiple_of(base + i * width, 8), 24)
            piece = jnp.concatenate([vs[i * 16 : i * 16 + 16, :], jnp.zeros((8, 256), F32)])
            gp[at, :] = gp[at, :] + pltpu.roll(piece, lead, 0)

    def whole(n, carry):
        _, slope2 = forward(n)
        backward(n, slope2)
        return carry

    def ahead(n, carry):
        r = lax.rem(todo[0, n], per)
        act1, slope2 = forward(n)
        stash[0][r] = act1.astype(BF)
        stash[1][r] = slope1[...]
        stash[2][r] = slope2
        return carry

    def behind(n, carry):
        r = lax.rem(todo[0, n], per)
        crop(n)
        put(hs, stash[0][r].astype(F32))
        slope1[...] = stash[1][r]
        backward(n, stash[2][r])
        return carry

    if early:
        lax.fori_loop(start, end, whole, 0)
        lax.fori_loop(total, count, ahead, 0)
    elif stash:
        lax.fori_loop(0, total, behind, 0)
    else:
        lax.fori_loop(start, end, whole, 0)


def chunks_of(rows):
    return ((0, rows),)


def finish_part(height, width, dp, chips, acc1, acc2, gp, keep, sends, gp_own, gp_other):
    core = lax.rem(lax.axis_index("tile"), 2)
    cells = height * width
    rows = 2304 // dp
    parts = chunks_of(rows)

    def write_keep(acc):
        for k in range(9):
            keep[k * 256 : k * 256 + 256, :] = acc[:, k * 256 : k * 256 + 256].T.astype(BF)

    def write_sends(acc):
        for k in range(9):
            value = acc[:, k * 256 : k * 256 + 256].T.astype(BF)
            for d in range(dp):
                for to, (lo, hi) in zip(sends, parts):
                    first = max(d * rows + lo, k * 256)
                    end = min(d * rows + hi, k * 256 + 256)
                    if first < end:
                        at = d * (hi - lo) + first - d * rows - lo
                        to[at : at + end - first, :] = value[first - k * 256 : end - k * 256, :]

    @pl.when(core == 0)
    def _():
        write_sends(acc2)
        write_keep(acc1)

    @pl.when(core == 1)
    def _():
        write_sends(acc1)
        write_keep(acc2)

    gp_own[...] = gp[pl.ds(pl.multiple_of(core * cells, cells), cells), :]
    gp_other[...] = gp[pl.ds(pl.multiple_of((1 - core) * cells, cells), cells), :].astype(BF)


def main_call(side, height, width, per, dp, chips, first, last, plan, state, weights, rims, blocks, early, stash):
    n = len(blocks)
    big = 2 * height * width + 16
    cells = side * PITCH
    kept = (sds((big, 256), F32),) + (sds((2304, 256), BF),) * 5
    sums = (sds((256, 2304), F32), sds((256, 2304), F32), sds((big, 256), F32))
    ends = (
        sds((2304, 256), BF),
        *(sds((dp * (hi - lo), 256), BF) for lo, hi in chunks_of(2304 // dp)),
        sds((height * width, 256), F32),
        sds((height * width, 256), BF),
    )
    stashed = (
        sds((per, cells, 256), BF),
        sds((per, cells, 256), F32),
        sds((per, cells, 256), F32),
    )
    outs = (kept if first else kept[:1] if rims else ()) + sums + (ends if last else ()) + (stashed if early else ())
    scratch = [
        pltpu.VMEM((cells + 32, 768), BF),
        pltpu.VMEM((cells + 32, 768), BF),
        pltpu.VMEM((cells + 32, 768), BF),
        pltpu.VMEM((side * side // 16 * 16 + packed_rows(side, per)[1], 256), F32),
        pltpu.VMEM((cells, 256), F32),
        pltpu.VMEM((cells, 256), F32),
        pltpu.SMEM((3, 256), jnp.int32),
    ]
    extra = []
    if first:
        extra = [
            pltpu.VMEM(((2 * height + 2) * width, 768), BF),
            pltpu.VMEM((height * width, 256), BF),
            pltpu.SemaphoreType.DMA((4,)),
        ]

    def kernel(*refs):
        refs = list(refs)

        def take(k):
            got = refs[:k]
            del refs[:k]
            return got

        state_refs = take(len(state))
        weight_refs = take(len(weights))
        rim_refs = take(len(rims))
        block_refs = take(n)
        early_refs = take(len(early))
        stash_refs = take(len(stash))
        out_refs = take(len(outs))
        if early:
            stash_refs = out_refs[-3:]
        scratch_refs = take(len(scratch))
        if first:
            pyr, wb1, wb2, w1, w2, wf = out_refs[:6]
            acc1, acc2, gp = out_refs[6:9]
            xp, own, sems = refs
            copies = [
                pltpu.make_async_copy(source, to, sems.at[k])
                for k, (source, to) in enumerate(zip((state_refs[0], *weight_refs), (own, wf, w1, w2)))
            ]
            for copy in copies:
                copy.start()
            for total in (acc1, acc2, gp):
                total[...] = jnp.zeros(total.shape, F32)
            copies[0].wait()
            pyramid_part(height, width, own, state_refs[1], wf, pyr, xp, copies[1])
            copies[2].wait()
            flip_part(w1, wb1)
            copies[3].wait()
            flip_part(w2, wb2)
        else:
            pyr, wb1, wb2, w1, w2, wf = state_refs[:6]
            shared = list(out_refs)
            if rims:
                pyr = shared.pop(0)
                edges_part(height, width, *rim_refs, wf, pyr)
            acc1, acc2, gp = shared[:3]
        if n:
            regions_part(
                *(side, height, width, per, plan, block_refs, early_refs, stash_refs),
                *((pyr, wb1, wb2, w1, w2), (acc1, acc2, gp), scratch_refs),
            )
        if last:
            keep, *sends, gp_own, gp_other = out_refs[3:]
            finish_part(height, width, dp, chips, acc1, acc2, gp, keep, sends, gp_own, gp_other)

    aliases = {} if first else {6: 0, 7: 1, 8: 2}
    if rims:
        aliases = {0: 0, 6: 1, 7: 2, 8: 3}
    return run(
        kernel,
        outs,
        [*state, *weights, *rims, *blocks, *early, *stash],
        scratch=scratch + extra,
        aliases=aliases,
        hbm=(0, *range(len(state), len(state) + len(weights))) if first else (),
    )


def local_kernel(fn, outs, *arrays, **more):
    if isinstance(outs, tuple):
        return run(fn, outs, arrays, **more)
    return run(fn, (outs,), arrays, **more)[0]


def add(a, b):
    return (a.astype(F32) + b.astype(F32)).astype(BF)


def reduce_weights(keep, sends, core_swap, dp, chips, beside, gp_other):
    rows = keep.shape[0] // dp
    bits = dp.bit_length() - 1
    orders = (list(range(bits)), list(reversed(range(bits))))
    shifts = [
        [(2 * z + c, 2 * ((z + k) % chips) + c) for z in range(chips) for c in range(2)]
        for k in range(chips)
    ]
    arrived = [lax.ppermute(send, "tile", core_swap) for send in sends]

    def split(members, bit):
        return [m for m in members if not m & bit], [m for m in members if m & bit]

    class Chunk:
        pass

    def begin(lo, hi, got):
        c = Chunk()
        c.rows = hi - lo
        low = roundup(c.rows // 2, 16)
        c.spans = ((0, low), (low, c.rows))
        c.members = [list(range(dp)), list(range(dp))]

        def first(keep_ref, got_ref, *outs):
            me = lax.axis_index("dp")
            for half in range(2):
                start, size = c.spans[half][0], c.spans[half][1] - c.spans[half][0]
                groups = split(c.members[half], 1 << orders[half][0])
                for out, group in zip(outs[2 * half : 2 * half + 2], groups):
                    for n, m in enumerate(group):
                        a = pl.ds(pl.multiple_of((me ^ m) * rows + lo + start, 16), size)
                        b = pl.ds(pl.multiple_of((me ^ m) * c.rows + start, 16), size)
                        out[n] = add(keep_ref[a, :], got_ref[b, :])

        shapes = []
        for half in range(2):
            shapes += [sds((dp // 2, c.spans[half][1] - c.spans[half][0], 256), BF)] * 2
        c.parts = local_kernel(first, tuple(shapes), keep, got)
        return c

    def exchange(c, stage):
        c.received = []
        for half in range(2):
            bit = 1 << orders[half][stage]
            pairs = [(i, i ^ bit) for i in range(dp)]
            c.received.append(lax.ppermute(c.parts[2 * half + 1], "dp", pairs))
            c.members[half] = split(c.members[half], bit)[0]

    def halve(c, stage):
        shapes = []
        for half in range(2):
            size = c.spans[half][1] - c.spans[half][0]
            shapes += [sds((len(c.members[half]) // 2, size, 256), BF)] * 2
        members = [list(m) for m in c.members]

        def kernel(p, pr, q, qr, *outs):
            for half, (mine, theirs) in enumerate(((p, pr), (q, qr))):
                groups = split(members[half], 1 << orders[half][stage])
                for out, group in zip(outs[2 * half : 2 * half + 2], groups):
                    for n, m in enumerate(group):
                        k = members[half].index(m)
                        out[n] = add(mine[k], theirs[k])

        c.parts = local_kernel(
            kernel, tuple(shapes), c.parts[0], c.received[0], c.parts[2], c.received[1]
        )

    def deal(c):
        c.share = roundup(-(-c.rows // chips), 16)
        low = c.spans[0][1]

        def kernel(p, pr, q, qr, *refs):
            outs, total = refs[:chips], refs[chips]
            chip = lax.axis_index("tile") // 2
            total[0:low, :] = add(p[0], pr[0])
            total[low : c.rows, :] = add(q[0], qr[0])
            if c.share * chips > c.rows:
                total[c.rows :, :] = jnp.zeros((c.share * chips - c.rows, 256), BF)
            for k in range(chips):
                to = lax.rem(chip + k, chips)
                outs[k][...] = total[pl.ds(pl.multiple_of(to * c.share, 16), c.share), :]

        dealt = local_kernel(
            kernel,
            tuple(sds((c.share, 256), BF) for _ in range(chips)),
            *(c.parts[0], c.received[0], c.parts[2], c.received[1]),
            scratch=[pltpu.VMEM((c.share * chips, 256), BF)],
        )
        c.mine = dealt[0]
        c.others = [lax.ppermute(dealt[k], "tile", shifts[k]) for k in range(1, chips)]

    def gather(c):
        def kernel(*refs):
            total = refs[0][...].astype(F32)
            for ref in refs[1:-1]:
                total += ref[...].astype(F32)
            refs[-1][...] = total.astype(BF)

        c.mine = local_kernel(kernel, sds((c.share, 256), BF), c.mine, *c.others)
        c.others = [lax.ppermute(c.mine, "tile", shifts[k]) for k in range(1, chips)]

    def lay(c):
        def kernel(*refs):
            chip = lax.axis_index("tile") // 2
            for k in range(chips):
                source = lax.rem(chip - k + chips, chips)
                refs[-1][pl.ds(pl.multiple_of(source * c.share, 16), c.share), :] = refs[k][...]

        c.whole = local_kernel(kernel, sds((c.share * chips, 256), BF), c.mine, *c.others)
        c.theirs = lax.ppermute(c.whole, "tile", core_swap)

    spans = chunks_of(rows)
    chunks = [begin(lo, hi, got) for (lo, hi), got in zip(spans, arrived)]
    chunks[0].parts = list(chunks[0].parts)
    chunks[0].parts[1], gp_other = lax.optimization_barrier((chunks[0].parts[1], gp_other))
    for c in chunks:
        exchange(c, 0)
    beside = beside(gp_other)
    chunks[0].received[0], beside = lax.optimization_barrier((chunks[0].received[0], beside))
    for stage in range(1, bits):
        for c in chunks:
            halve(c, stage)
            exchange(c, stage)
    for step in (deal, gather, lay):
        for c in chunks:
            step(c)

    def out(*refs):
        core = lax.rem(lax.axis_index("tile"), 2)
        one, two = refs[-2:]

        def write(to, sources):
            for (lo, hi), source in zip(spans, sources):
                to[lo:hi, :] = source[0 : hi - lo, :].astype(F32)

        @pl.when(core == 0)
        def _():
            write(one, refs[0 : len(spans)])
            write(two, refs[len(spans) : -2])

        @pl.when(core == 1)
        def _():
            write(one, refs[len(spans) : -2])
            write(two, refs[0 : len(spans)])

    one, two = local_kernel(
        out,
        (sds((rows, 256), F32), sds((rows, 256), F32)),
        *(c.whole for c in chunks),
        *(c.theirs for c in chunks),
        hbm_out=(0, 1),
    )
    return one, two, beside


def body(features, fpn_weight, mask_w1, mask_w2, owner, row_off, col_off, cotangent):
    tiles = lax.axis_size("tile")
    dp = lax.axis_size("dp")
    chips = tiles // 2
    height, width, channels = features.shape[1:]
    side = cotangent.shape[2]
    swap = [(i, i ^ 1) for i in range(tiles)]

    tile = features.reshape(height * width, channels)
    regions = cotangent.shape[1]
    place = [x.reshape(1, regions) for x in (owner, row_off, col_off)]
    other = lax.ppermute(tile, "tile", swap)
    packed, notes, edge = pack(cotangent[0].transpose(1, 2, 0, 3), tile, height, width, place)

    order = [0] + list(range(1, chips, 2)) + list(range(2, chips, 2))[::-1]
    ring = [
        (2 * z + c, 2 * order[(k + 1) % chips] + c) for k, z in enumerate(order) for c in range(2)
    ]

    flat = lambda w: w.reshape(9 * channels, channels)
    wf, w1, w2 = flat(fpn_weight), flat(mask_w1), flat(mask_w2)
    block = lax.ppermute(packed, "tile", ring)
    sizes = (side, height, width, regions, dp, chips)
    plan = [1] + [3] * (chips - 3) + [None]
    start = main_call(
        *(*sizes, True, False, plan, [tile, other], [wf, w1, w2], [], [packed], [], [])
    )
    kept, sums, held = list(start[:6]), list(start[6:]), [packed]
    edge, notes, kept[0] = lax.optimization_barrier((edge, notes, kept[0]))
    rim_a = lax.ppermute(
        edge, "tile", [(i, i + 1 if i % 2 else i - 1) for i in range(1, tiles - 1)]
    )
    notes = lax.ppermute(notes, "tile", [(j, i) for i, j in ring])
    for step in range(1, chips):
        state = kept + sums
        if step == chips - 1:
            got = main_call(*sizes, False, True, [None], state, [], [], [block], [], stash)
            ends = got[3:]
            break
        block, state[0], state[-1] = lax.optimization_barrier((block, state[0], state[-1]))
        if step == 1:
            block, rim_a = lax.optimization_barrier((block, rim_a))
        if step == chips - 2:
            block, notes = lax.optimization_barrier((block, notes))
        held = held + [block]
        block = lax.ppermute(block, "tile", ring)
        if step == 1:
            rim_b = lax.ppermute(rim_a, "tile", swap)
        early = [notes] if step == chips - 2 else []
        rims = [rim_a, rim_b] if step == 1 else []
        got = list(main_call(*sizes, False, False, plan, state, [], rims, held, early, []))
        if rims:
            kept[0] = got.pop(0)
        sums, stash = got[:3], got[3:]
    keep, *sends, gp_own, gp_other = ends

    def join(a, b, out):
        out[...] = (a[...] + b[...].astype(F32)).astype(BF)

    def joined(gp_other):
        gp_got = lax.ppermute(gp_other, "tile", swap)
        return local_kernel(
            join, sds((height * width, channels), BF), gp_own, gp_got, hbm_out=(0,)
        )

    grad_one, grad_two, grad_pyramid = reduce_weights(
        keep, sends, swap, dp, chips, joined, gp_other
    )
    return grad_one, grad_two, grad_pyramid.reshape(1, height, width, channels)


def solution(mesh):
    placed = (
        P("dp", "tile", None, None),
        P(),
        P(),
        P(),
        P("dp", "tile", None),
        P("dp", "tile"),
        P("dp", "tile"),
        P("dp", "tile", None, None, None),
    )
    return jax.shard_map(
        body,
        mesh=mesh,
        in_specs=placed,
        out_specs=(P("dp", None), P("dp", None), P("dp", "tile", None, None)),
        check_vma=False,
    )
```

```python
import functools
import math

import jax
import jax.numpy as jnp
from jax import lax
from jax.experimental import pallas as pl
from jax.experimental.pallas import tpu as pltpu
from jax.sharding import PartitionSpec as P

BF = jnp.bfloat16
F32 = jnp.float32
VMEM_LIMIT = 24 * 1024 * 1024
PITCH = 16


def roundup(n, m):
    return (n + m - 1) // m * m


def run(kernel, outs, args, scratch=(), aliases=None, hbm=(), hbm_out=()):
    args = [
        pltpu.with_memory_space_constraint(x, pltpu.HBM if i in hbm else pltpu.VMEM)
        for i, x in enumerate(args)
    ]
    return pl.pallas_call(
        kernel,
        out_shape=tuple(
            s if i in hbm_out else pltpu.VMEM(s.shape, s.dtype) for i, s in enumerate(outs)
        ),
        in_specs=[
            pl.BlockSpec(memory_space=pltpu.HBM if i in hbm else pltpu.VMEM)
            for i in range(len(args))
        ],
        out_specs=tuple(pl.BlockSpec(memory_space=pltpu.VMEM) for _ in outs),
        scratch_shapes=list(scratch),
        input_output_aliases=aliases or {},
        compiler_params=pltpu.CompilerParams(vmem_limit_bytes=VMEM_LIMIT),
    )(*args)


def sds(shape, dtype):
    return jax.ShapeDtypeStruct(shape, dtype)


def pack_kernel(
    side, height, width, cot, owner, row, col, tile, packed, notes, edge, low, high, wide, tails, places, sems
):
    regions = cot.shape[2]
    core = lax.rem(lax.axis_index("tile"), 2)
    line = pl.ds(pl.multiple_of(core * (height - 1) * width, width), width)
    copies = [pltpu.make_async_copy(tile.at[line, :], edge, sems.at[3])]
    copies += [
        pltpu.make_async_copy(source, places.at[n], sems.at[n])
        for n, source in enumerate((owner, row, col))
    ]
    for copy in copies:
        copy.start()
    for i in range(side):
        for j in range(side):
            at = (i * side + j) * regions
            cell = cot[i, j].astype(F32)
            low[at : at + regions, :] = cell[:, 0:128]
            high[at : at + regions, :] = cell[:, 128:256]
    for copy in copies:
        copy.wait()
    lanes = lax.broadcasted_iota(jnp.int32, (16, 256), 1)
    rows = lax.broadcasted_iota(jnp.int32, (16, 256), 0)
    cells = side * side
    main = cells // 16 * 16
    rest = cells - main
    note = jnp.zeros((16, 256), F32)
    for r in range(regions):
        wide[0:cells, 0:128] = low[pl.ds(r, cells, stride=regions), :]
        wide[0:cells, 128:256] = high[pl.ds(r, cells, stride=regions), :]
        spot = (places[0, 0, r] * height + places[1, 0, r] + 1).astype(F32)
        column = places[2, 0, r].astype(F32)
        value = jnp.where(lanes == 0, spot, jnp.where(lanes == 1, column, 0.0))
        note = jnp.where(rows == r, value, note)
        packed[r * main : r * main + main, :] = wide[0:main, :].astype(BF)
        tails[r * rest : r * rest + rest, :] = wide[main:cells, :]
    at = regions * main
    packed[at : at + tails.shape[0], :] = tails[...].astype(BF)
    at += tails.shape[0]
    packed[at : at + 16, :] = note.astype(BF)
    notes[...] = note.astype(BF)


def packed_rows(side, regions):
    cells = side * side
    return regions * (cells // 16 * 16), roundup(regions * (cells % 16), 16)


def pack(cotangent, tile, height, width, place):
    side, regions = cotangent.shape[0], cotangent.shape[2]
    return local_kernel(
        functools.partial(pack_kernel, side, height, width),
        (
            sds((sum(packed_rows(side, regions)) + 16, 256), BF),
            sds((16, 256), BF),
            sds((width, 256), BF),
        ),
        cotangent,
        *place,
        tile,
        scratch=[
            pltpu.VMEM((side * side * regions, 128), F32),
            pltpu.VMEM((side * side * regions, 128), F32),
            pltpu.VMEM((side * side, 256), F32),
            pltpu.VMEM((packed_rows(side, regions)[1], 256), F32),
            pltpu.SMEM((3, 1, regions), jnp.int32),
            pltpu.SemaphoreType.DMA((4,)),
        ],
        hbm=(1, 2, 3, 4),
    )


def shifted(v, width):
    col = lax.broadcasted_iota(jnp.int32, (width, 256), 0)
    left = jnp.where(col == 0, 0.0, pltpu.roll(v, 1, 0)).astype(BF)
    right = jnp.where(col == width - 1, 0.0, pltpu.roll(v, width - 1, 0)).astype(BF)
    return left, v.astype(BF), right


def pyramid_part(height, width, own, other, wf, pyr, xp, fetched):
    core = lax.rem(lax.axis_index("tile"), 2)
    cells = height * width

    def fill(src, where):
        def step(t, carry):
            v = src[pl.ds(pl.multiple_of(t * width, width), width), :].astype(F32)
            to = pl.ds(pl.multiple_of(where + t * width, width), width)
            for b, piece in enumerate(shifted(v, width)):
                xp[to, b * 256 : b * 256 + 256] = piece
            return carry

        lax.fori_loop(0, height, step, 0)

    bottom = width + 2 * cells
    fill(own, width + core * cells)
    fill(other, width + (1 - core) * cells)
    xp[0:width, :] = jnp.zeros((width, 768), BF)
    xp[bottom : bottom + width, :] = jnp.zeros((width, 768), BF)
    fetched.wait()

    def conv(t, carry):
        at = t * 512
        total = jnp.zeros((512, 256), F32)
        for a in range(3):
            piece = xp[pl.ds(pl.multiple_of(at + a * width, 64), 512), :]
            total += jnp.dot(piece, wf[a * 768 : a * 768 + 768, :], preferred_element_type=F32)
        cell = at + lax.broadcasted_iota(jnp.int32, (512, 256), 0)
        open_row = (cell < width) | (cell >= 2 * cells - width)
        pyr[pl.ds(pl.multiple_of(at, 512), 512), :] = jnp.where(
            open_row, total, total.astype(BF).astype(F32)
        )
        return carry

    lax.fori_loop(0, 2 * cells // 512, conv, 0)
    pyr[2 * cells : 2 * cells + 16, :] = jnp.zeros((16, 256), F32)


def edges_part(height, width, rim_a, rim_b, wf, pyr):
    core = lax.rem(lax.axis_index("tile"), 2)
    last = 2 * height * width - width

    def close(rim, at, tap):
        total = pyr[at : at + width, :]
        for b, piece in enumerate(shifted(rim[...].astype(F32), width)):
            k = 3 * tap + b
            total += jnp.dot(piece, wf[k * 256 : k * 256 + 256, :], preferred_element_type=F32)
        pyr[at : at + width, :] = total.astype(BF).astype(F32)

    @pl.when(core == 0)
    def _():
        close(rim_a, 0, 0)
        close(rim_b, last, 2)

    @pl.when(core == 1)
    def _():
        close(rim_b, 0, 0)
        close(rim_a, last, 2)


def flip_part(w, wb):
    for k in range(9):
        block = w[(8 - k) * 256 : (9 - k) * 256, :].astype(F32)
        wb[k * 256 : k * 256 + 256, :] = block.T.astype(BF)


def gelu_pair(v):
    c = math.sqrt(2.0 / math.pi)
    sq = v * v
    t = jnp.tanh(c * (v + 0.044715 * (sq * v)))
    half = 0.5 * (1.0 + t)
    slope = half + 0.5 * v * (1.0 - t * t) * (c * (1.0 + 3 * 0.044715 * sq))
    return v * half, slope


def regions_part(side, height, width, per, plan, blocks, early, stash, tables, sums, scratch):
    pyr, wb1, wb2, w1, w2 = tables
    acc1, acc2, gp = sums
    xs, hs, gs, wide, vs, slope1, todo = scratch
    chip = lax.axis_index("tile") // 2
    lanes = lax.broadcasted_iota(jnp.int32, (16, 256), 1)
    rows16 = lax.broadcasted_iota(jnp.int32, (16, 256), 0)
    in_row = rows16 < side
    cells = side * PITCH
    inside = (lax.broadcasted_iota(jnp.int32, (cells, 256), 0) & (PITCH - 1)) < side
    used = pl.ds(16, cells)
    main, tails = packed_rows(side, per)
    one = main // per
    rest = side * side - one

    count = jnp.int32(0)
    start, end = jnp.int32(0), jnp.int32(0)

    def enlist(count, s, r, note, wanted=None):
        note = jnp.where(rows16 == r, note.astype(F32), 0.0)
        spot = jnp.sum(jnp.where(lanes == 0, note, 0.0)).astype(jnp.int32) - 1
        column = jnp.sum(jnp.where(lanes == 1, note, 0.0)).astype(jnp.int32)
        local = spot - chip * 2 * height
        here = (spot >= 0) & (local >= 0) & (local < 2 * height)
        if wanted is not None:
            outer = (local == 0) | (local == 2 * height - side)
            here = here & (outer == wanted)
        todo[0, count] = jnp.int32(s * per + r)
        todo[1, count] = jnp.where(here, local * width + column // 8 * 8, 0)
        todo[2, count] = jnp.where(here, lax.rem(column, 8), 0)
        return count + here.astype(jnp.int32)

    def scan(s, wanted):
        note = blocks[s][main + tails : main + tails + 16, :]
        found = count
        for r in range(per):
            found = enlist(found, s, r, note, wanted)
        return found

    for s, most in enumerate(plan[: len(blocks)]):
        if s == 1:
            count = scan(0, True)
        count = scan(s, False if s == 0 and len(plan) > 1 else None)
        start, end = end, count if most is None else jnp.minimum(count, end + most)
    total = count
    for note in early:
        for r in range(per):
            count = enlist(count, len(blocks), r, note[...])

    for buf in (xs, hs, gs):
        buf[0:16, :] = jnp.zeros((16, 768), BF)
        buf[cells + 16 : cells + 32, :] = jnp.zeros((16, 768), BF)

    def put(buf, v):
        buf[used, 0:256] = pltpu.roll(v, 1, 0).astype(BF)
        buf[used, 256:512] = v.astype(BF)
        buf[used, 512:768] = pltpu.roll(v, cells - 1, 0).astype(BF)

    def conv(buf, w):
        total = jnp.zeros((cells, 256), F32)
        for a in range(3):
            total += jnp.dot(
                buf[a * 16 : a * 16 + cells, :],
                w[a * 768 : a * 768 + 768, :],
                preferred_element_type=F32,
            )
        return total

    def taps(acc, buf, grad):
        turned = grad.T.astype(BF)
        for a in range(3):
            acc[:, a * 768 : a * 768 + 768] += jnp.dot(
                turned, buf[a * 16 : a * 16 + cells, :], preferred_element_type=F32
            )

    def crop(n):
        base, lead = todo[1, n], todo[2, n]
        for i in range(side):
            got = pyr[pl.ds(pl.multiple_of(base + i * width, 8), 24), :]
            got = pltpu.roll(got, lax.rem(24 - lead, 24), 0)[0:16]
            vs[i * 16 : i * 16 + 16, :] = jnp.where(in_row, got, 0.0)
        put(xs, vs[...])

    def forward(n):
        crop(n)
        act1, slope = gelu_pair(conv(xs, w1))
        slope1[...] = slope
        act1 = jnp.where(inside, act1, 0.0)
        put(hs, act1)
        _, slope = gelu_pair(conv(hs, w2))
        return act1, slope

    def backward(n, slope2):
        which = todo[0, n]
        base, lead = todo[1, n], todo[2, n]
        for s, block in enumerate(blocks):

            @pl.when(which // per == s)
            def _(block=block):
                r = lax.rem(which, per)
                cell = pl.ds(pl.multiple_of(r * one, 16), one)
                wide[0:one, :] = block[cell, :].astype(F32)
                left = block[main : main + tails, :].astype(F32)
                wide[one : one + tails, :] = pltpu.roll(left, lax.rem(tails - r * rest, tails), 0)

        for i in range(side):
            got = wide[i * side : i * side + 16, :]
            vs[i * 16 : i * 16 + 16, :] = jnp.where(in_row, got, 0.0)
        g2 = vs[...] * slope2
        put(gs, g2)
        taps(acc2, hs, g2)
        g1 = jnp.where(inside, conv(gs, wb2) * slope1[...], 0.0)
        put(gs, g1)
        taps(acc1, xs, g1)
        vs[...] = jnp.where(inside, conv(gs, wb1), 0.0).astype(BF).astype(F32)
        for i in range(side):
            at = pl.ds(pl.multiple_of(base + i * width, 8), 24)
            piece = jnp.concatenate([vs[i * 16 : i * 16 + 16, :], jnp.zeros((8, 256), F32)])
            gp[at, :] = gp[at, :] + pltpu.roll(piece, lead, 0)

    def whole(n, carry):
        _, slope2 = forward(n)
        backward(n, slope2)
        return carry

    def ahead(n, carry):
        r = lax.rem(todo[0, n], per)
        act1, slope2 = forward(n)
        stash[0][r] = act1.astype(BF)
        stash[1][r] = slope1[...]
        stash[2][r] = slope2
        return carry

    def behind(n, carry):
        r = lax.rem(todo[0, n], per)
        crop(n)
        put(hs, stash[0][r].astype(F32))
        slope1[...] = stash[1][r]
        backward(n, stash[2][r])
        return carry

    if early:
        lax.fori_loop(start, end, whole, 0)
        lax.fori_loop(total, count, ahead, 0)
    elif stash:
        lax.fori_loop(0, total, behind, 0)
    else:
        lax.fori_loop(start, end, whole, 0)


def chunks_of(rows):
    return ((0, rows),)


def finish_part(height, width, dp, chips, acc1, acc2, gp, keep, sends, gp_own, gp_other):
    core = lax.rem(lax.axis_index("tile"), 2)
    cells = height * width
    rows = 2304 // dp
    parts = chunks_of(rows)

    def write_keep(acc):
        for k in range(9):
            keep[k * 256 : k * 256 + 256, :] = acc[:, k * 256 : k * 256 + 256].T.astype(BF)

    def write_sends(acc):
        for k in range(9):
            value = acc[:, k * 256 : k * 256 + 256].T.astype(BF)
            for d in range(dp):
                for to, (lo, hi) in zip(sends, parts):
                    first = max(d * rows + lo, k * 256)
                    end = min(d * rows + hi, k * 256 + 256)
                    if first < end:
                        at = d * (hi - lo) + first - d * rows - lo
                        to[at : at + end - first, :] = value[first - k * 256 : end - k * 256, :]

    @pl.when(core == 0)
    def _():
        write_sends(acc2)
        write_keep(acc1)

    @pl.when(core == 1)
    def _():
        write_sends(acc1)
        write_keep(acc2)

    gp_own[...] = gp[pl.ds(pl.multiple_of(core * cells, cells), cells), :]
    gp_other[...] = gp[pl.ds(pl.multiple_of((1 - core) * cells, cells), cells), :].astype(BF)


def main_call(side, height, width, per, dp, chips, first, last, plan, state, weights, rims, blocks, early, stash):
    n = len(blocks)
    big = 2 * height * width + 16
    cells = side * PITCH
    kept = (sds((big, 256), F32),) + (sds((2304, 256), BF),) * 5
    sums = (sds((256, 2304), F32), sds((256, 2304), F32), sds((big, 256), F32))
    ends = (
        sds((2304, 256), BF),
        *(sds((dp * (hi - lo), 256), BF) for lo, hi in chunks_of(2304 // dp)),
        sds((height * width, 256), F32),
        sds((height * width, 256), BF),
    )
    stashed = (
        sds((per, cells, 256), BF),
        sds((per, cells, 256), F32),
        sds((per, cells, 256), F32),
    )
    outs = (kept if first else kept[:1] if rims else ()) + sums + (ends if last else ()) + (stashed if early else ())
    scratch = [
        pltpu.VMEM((cells + 32, 768), BF),
        pltpu.VMEM((cells + 32, 768), BF),
        pltpu.VMEM((cells + 32, 768), BF),
        pltpu.VMEM((side * side // 16 * 16 + packed_rows(side, per)[1], 256), F32),
        pltpu.VMEM((cells, 256), F32),
        pltpu.VMEM((cells, 256), F32),
        pltpu.SMEM((3, 256), jnp.int32),
    ]
    extra = []
    if first:
        extra = [
            pltpu.VMEM(((2 * height + 2) * width, 768), BF),
            pltpu.VMEM((height * width, 256), BF),
            pltpu.SemaphoreType.DMA((4,)),
        ]

    def kernel(*refs):
        refs = list(refs)

        def take(k):
            got = refs[:k]
            del refs[:k]
            return got

        state_refs = take(len(state))
        weight_refs = take(len(weights))
        rim_refs = take(len(rims))
        block_refs = take(n)
        early_refs = take(len(early))
        stash_refs = take(len(stash))
        out_refs = take(len(outs))
        if early:
            stash_refs = out_refs[-3:]
        scratch_refs = take(len(scratch))
        if first:
            pyr, wb1, wb2, w1, w2, wf = out_refs[:6]
            acc1, acc2, gp = out_refs[6:9]
            xp, own, sems = refs
            copies = [
                pltpu.make_async_copy(source, to, sems.at[k])
                for k, (source, to) in enumerate(zip((state_refs[0], *weight_refs), (own, wf, w1, w2)))
            ]
            for copy in copies:
                copy.start()
            for total in (acc1, acc2, gp):
                total[...] = jnp.zeros(total.shape, F32)
            copies[0].wait()
            pyramid_part(height, width, own, state_refs[1], wf, pyr, xp, copies[1])
            copies[2].wait()
            flip_part(w1, wb1)
            copies[3].wait()
            flip_part(w2, wb2)
        else:
            pyr, wb1, wb2, w1, w2, wf = state_refs[:6]
            shared = list(out_refs)
            if rims:
                pyr = shared.pop(0)
                edges_part(height, width, *rim_refs, wf, pyr)
            acc1, acc2, gp = shared[:3]
        if n:
            regions_part(
                *(side, height, width, per, plan, block_refs, early_refs, stash_refs),
                *((pyr, wb1, wb2, w1, w2), (acc1, acc2, gp), scratch_refs),
            )
        if last:
            keep, *sends, gp_own, gp_other = out_refs[3:]
            finish_part(height, width, dp, chips, acc1, acc2, gp, keep, sends, gp_own, gp_other)

    aliases = {} if first else {6: 0, 7: 1, 8: 2}
    if rims:
        aliases = {0: 0, 6: 1, 7: 2, 8: 3}
    return run(
        kernel,
        outs,
        [*state, *weights, *rims, *blocks, *early, *stash],
        scratch=scratch + extra,
        aliases=aliases,
        hbm=(0, *range(len(state), len(state) + len(weights))) if first else (),
    )


def local_kernel(fn, outs, *arrays, **more):
    if isinstance(outs, tuple):
        return run(fn, outs, arrays, **more)
    return run(fn, (outs,), arrays, **more)[0]


def add(a, b):
    return (a.astype(F32) + b.astype(F32)).astype(BF)


def reduce_weights(keep, sends, core_swap, dp, chips, beside, gp_other):
    rows = keep.shape[0] // dp
    bits = dp.bit_length() - 1
    orders = (list(range(bits)), list(reversed(range(bits))))
    shifts = [
        [(2 * z + c, 2 * ((z + k) % chips) + c) for z in range(chips) for c in range(2)]
        for k in range(chips)
    ]
    arrived = [lax.ppermute(send, "tile", core_swap) for send in sends]

    def split(members, bit):
        return [m for m in members if not m & bit], [m for m in members if m & bit]

    class Chunk:
        pass

    def begin(lo, hi, got):
        c = Chunk()
        c.rows = hi - lo
        low = roundup(c.rows // 2, 16)
        c.spans = ((0, low), (low, c.rows))
        c.members = [list(range(dp)), list(range(dp))]

        def first(keep_ref, got_ref, *outs):
            me = lax.axis_index("dp")
            for half in range(2):
                start, size = c.spans[half][0], c.spans[half][1] - c.spans[half][0]
                groups = split(c.members[half], 1 << orders[half][0])
                for out, group in zip(outs[2 * half : 2 * half + 2], groups):
                    for n, m in enumerate(group):
                        a = pl.ds(pl.multiple_of((me ^ m) * rows + lo + start, 16), size)
                        b = pl.ds(pl.multiple_of((me ^ m) * c.rows + start, 16), size)
                        out[n] = add(keep_ref[a, :], got_ref[b, :])

        shapes = []
        for half in range(2):
            shapes += [sds((dp // 2, c.spans[half][1] - c.spans[half][0], 256), BF)] * 2
        c.parts = local_kernel(first, tuple(shapes), keep, got)
        return c

    def exchange(c, stage):
        c.received = []
        for half in range(2):
            bit = 1 << orders[half][stage]
            pairs = [(i, i ^ bit) for i in range(dp)]
            c.received.append(lax.ppermute(c.parts[2 * half + 1], "dp", pairs))
            c.members[half] = split(c.members[half], bit)[0]

    def halve(c, stage):
        shapes = []
        for half in range(2):
            size = c.spans[half][1] - c.spans[half][0]
            shapes += [sds((len(c.members[half]) // 2, size, 256), BF)] * 2
        members = [list(m) for m in c.members]

        def kernel(p, pr, q, qr, *outs):
            for half, (mine, theirs) in enumerate(((p, pr), (q, qr))):
                groups = split(members[half], 1 << orders[half][stage])
                for out, group in zip(outs[2 * half : 2 * half + 2], groups):
                    for n, m in enumerate(group):
                        k = members[half].index(m)
                        out[n] = add(mine[k], theirs[k])

        c.parts = local_kernel(
            kernel, tuple(shapes), c.parts[0], c.received[0], c.parts[2], c.received[1]
        )

    def deal(c):
        c.share = roundup(-(-c.rows // chips), 16)
        low = c.spans[0][1]

        def kernel(p, pr, q, qr, *refs):
            outs, total = refs[:chips], refs[chips]
            chip = lax.axis_index("tile") // 2
            total[0:low, :] = add(p[0], pr[0])
            total[low : c.rows, :] = add(q[0], qr[0])
            if c.share * chips > c.rows:
                total[c.rows :, :] = jnp.zeros((c.share * chips - c.rows, 256), BF)
            for k in range(chips):
                to = lax.rem(chip + k, chips)
                outs[k][...] = total[pl.ds(pl.multiple_of(to * c.share, 16), c.share), :]

        dealt = local_kernel(
            kernel,
            tuple(sds((c.share, 256), BF) for _ in range(chips)),
            *(c.parts[0], c.received[0], c.parts[2], c.received[1]),
            scratch=[pltpu.VMEM((c.share * chips, 256), BF)],
        )
        c.mine = dealt[0]
        c.others = [lax.ppermute(dealt[k], "tile", shifts[k]) for k in range(1, chips)]

    def gather(c):
        def kernel(*refs):
            total = refs[0][...].astype(F32)
            for ref in refs[1:-1]:
                total += ref[...].astype(F32)
            refs[-1][...] = total.astype(BF)

        c.mine = local_kernel(kernel, sds((c.share, 256), BF), c.mine, *c.others)
        c.others = [lax.ppermute(c.mine, "tile", shifts[k]) for k in range(1, chips)]

    def lay(c):
        def kernel(*refs):
            chip = lax.axis_index("tile") // 2
            for k in range(chips):
                source = lax.rem(chip - k + chips, chips)
                refs[-1][pl.ds(pl.multiple_of(source * c.share, 16), c.share), :] = refs[k][...]

        c.whole = local_kernel(kernel, sds((c.share * chips, 256), BF), c.mine, *c.others)
        c.theirs = lax.ppermute(c.whole, "tile", core_swap)

    spans = chunks_of(rows)
    chunks = [begin(lo, hi, got) for (lo, hi), got in zip(spans, arrived)]
    chunks[0].parts = list(chunks[0].parts)
    chunks[0].parts[1], gp_other = lax.optimization_barrier((chunks[0].parts[1], gp_other))
    for c in chunks:
        exchange(c, 0)
    beside = beside(gp_other)
    chunks[0].received[0], beside = lax.optimization_barrier((chunks[0].received[0], beside))
    for stage in range(1, bits):
        for c in chunks:
            halve(c, stage)
            exchange(c, stage)
    for step in (deal, gather, lay):
        for c in chunks:
            step(c)

    def out(*refs):
        core = lax.rem(lax.axis_index("tile"), 2)
        one, two = refs[-2:]

        def write(to, sources):
            for (lo, hi), source in zip(spans, sources):
                to[lo:hi, :] = source[0 : hi - lo, :].astype(F32)

        @pl.when(core == 0)
        def _():
            write(one, refs[0 : len(spans)])
            write(two, refs[len(spans) : -2])

        @pl.when(core == 1)
        def _():
            write(one, refs[len(spans) : -2])
            write(two, refs[0 : len(spans)])

    one, two = local_kernel(
        out,
        (sds((rows, 256), F32), sds((rows, 256), F32)),
        *(c.whole for c in chunks),
        *(c.theirs for c in chunks),
        hbm_out=(0, 1),
    )
    return one, two, beside


def body(features, fpn_weight, mask_w1, mask_w2, owner, row_off, col_off, cotangent):
    tiles = lax.axis_size("tile")
    dp = lax.axis_size("dp")
    chips = tiles // 2
    height, width, channels = features.shape[1:]
    side = cotangent.shape[2]
    swap = [(i, i ^ 1) for i in range(tiles)]

    tile = features.reshape(height * width, channels)
    regions = cotangent.shape[1]
    place = [x.reshape(1, regions) for x in (owner, row_off, col_off)]
    other = lax.ppermute(tile, "tile", swap)
    packed, notes, edge = pack(cotangent[0].transpose(1, 2, 0, 3), tile, height, width, place)

    order = [0] + list(range(1, chips, 2)) + list(range(2, chips, 2))[::-1]
    ring = [
        (2 * z + c, 2 * order[(k + 1) % chips] + c) for k, z in enumerate(order) for c in range(2)
    ]

    flat = lambda w: w.reshape(9 * channels, channels)
    wf, w1, w2 = flat(fpn_weight), flat(mask_w1), flat(mask_w2)
    block = lax.ppermute(packed, "tile", ring)
    sizes = (side, height, width, regions, dp, chips)
    rim_a = lax.ppermute(
        edge, "tile", [(i, i + 1 if i % 2 else i - 1) for i in range(1, tiles - 1)]
    )
    plan = [1] + [3] * (chips - 3) + [None]
    start = main_call(
        *(*sizes, True, False, plan, [tile, other], [wf, w1, w2], [], [packed], [], [])
    )
    kept, sums, held = list(start[:6]), list(start[6:]), [packed]
    notes, kept[0] = lax.optimization_barrier((notes, kept[0]))
    notes = lax.ppermute(notes, "tile", [(j, i) for i, j in ring])
    for step in range(1, chips):
        state = kept + sums
        if step == chips - 1:
            got = main_call(*sizes, False, True, [None], state, [], [], [block], [], stash)
            ends = got[3:]
            break
        block, state[0], state[-1] = lax.optimization_barrier((block, state[0], state[-1]))
        if step == 1:
            block, rim_a = lax.optimization_barrier((block, rim_a))
        if step == chips - 2:
            block, notes = lax.optimization_barrier((block, notes))
        held = held + [block]
        block = lax.ppermute(block, "tile", ring)
        if step == 1:
            rim_b = lax.ppermute(rim_a, "tile", swap)
        early = [notes] if step == chips - 2 else []
        rims = [rim_a, rim_b] if step == 1 else []
        got = list(main_call(*sizes, False, False, plan, state, [], rims, held, early, []))
        if rims:
            kept[0] = got.pop(0)
        sums, stash = got[:3], got[3:]
    keep, *sends, gp_own, gp_other = ends

    def join(a, b, out):
        out[...] = (a[...] + b[...].astype(F32)).astype(BF)

    def joined(gp_other):
        gp_got = lax.ppermute(gp_other, "tile", swap)
        return local_kernel(
            join, sds((height * width, channels), BF), gp_own, gp_got, hbm_out=(0,)
        )

    grad_one, grad_two, grad_pyramid = reduce_weights(
        keep, sends, swap, dp, chips, joined, gp_other
    )
    return grad_one, grad_two, grad_pyramid.reshape(1, height, width, channels)


def solution(mesh):
    placed = (
        P("dp", "tile", None, None),
        P(),
        P(),
        P(),
        P("dp", "tile", None),
        P("dp", "tile"),
        P("dp", "tile"),
        P("dp", "tile", None, None, None),
    )
    return jax.shard_map(
        body,
        mesh=mesh,
        in_specs=placed,
        out_specs=(P("dp", None), P("dp", None), P("dp", "tile", None, None)),
        check_vma=False,
    )
```

```python
import functools
import math

import jax
import jax.numpy as jnp
from jax import lax
from jax.experimental import pallas as pl
from jax.experimental.pallas import tpu as pltpu
from jax.sharding import PartitionSpec as P

BF = jnp.bfloat16
F32 = jnp.float32
VMEM_LIMIT = 24 * 1024 * 1024
PITCH = 16


def roundup(n, m):
    return (n + m - 1) // m * m


def run(kernel, outs, args, scratch=(), aliases=None, hbm=(), hbm_out=()):
    args = [
        pltpu.with_memory_space_constraint(x, pltpu.HBM if i in hbm else pltpu.VMEM)
        for i, x in enumerate(args)
    ]
    return pl.pallas_call(
        kernel,
        out_shape=tuple(
            s if i in hbm_out else pltpu.VMEM(s.shape, s.dtype) for i, s in enumerate(outs)
        ),
        in_specs=[
            pl.BlockSpec(memory_space=pltpu.HBM if i in hbm else pltpu.VMEM)
            for i in range(len(args))
        ],
        out_specs=tuple(pl.BlockSpec(memory_space=pltpu.VMEM) for _ in outs),
        scratch_shapes=list(scratch),
        input_output_aliases=aliases or {},
        compiler_params=pltpu.CompilerParams(vmem_limit_bytes=VMEM_LIMIT),
    )(*args)


def sds(shape, dtype):
    return jax.ShapeDtypeStruct(shape, dtype)


def pack_kernel(
    side, height, width, cot, owner, row, col, tile, packed, notes, edge, got, low, high, wide, tails, places, sems
):
    regions = cot.shape[2]
    core = lax.rem(lax.axis_index("tile"), 2)
    line = pl.ds(pl.multiple_of(core * (height - 1) * width, width), width)
    copies = [pltpu.make_async_copy(tile.at[line, :], edge, sems.at[3])]
    copies += [
        pltpu.make_async_copy(source, places.at[n], sems.at[n])
        for n, source in enumerate((owner, row, col))
    ]
    middle = side // 2
    halves = [
        pltpu.make_async_copy(cot.at[lo:hi], got.at[lo:hi], sems.at[4 + n])
        for n, (lo, hi) in enumerate(((0, middle), (middle, side)))
    ]
    for copy in halves + copies:
        copy.start()
    for i in range(side):
        if i in (0, middle):
            halves[i // middle].wait()
        for j in range(side):
            at = (i * side + j) * regions
            cell = got[i, j].astype(F32)
            low[at : at + regions, :] = cell[:, 0:128]
            high[at : at + regions, :] = cell[:, 128:256]
    for copy in copies:
        copy.wait()
    lanes = lax.broadcasted_iota(jnp.int32, (16, 256), 1)
    rows = lax.broadcasted_iota(jnp.int32, (16, 256), 0)
    cells = side * side
    main = cells // 16 * 16
    rest = cells - main
    note = jnp.zeros((16, 256), F32)
    for r in range(regions):
        wide[0:cells, 0:128] = low[pl.ds(r, cells, stride=regions), :]
        wide[0:cells, 128:256] = high[pl.ds(r, cells, stride=regions), :]
        spot = (places[0, 0, r] * height + places[1, 0, r] + 1).astype(F32)
        column = places[2, 0, r].astype(F32)
        value = jnp.where(lanes == 0, spot, jnp.where(lanes == 1, column, 0.0))
        note = jnp.where(rows == r, value, note)
        packed[r * main : r * main + main, :] = wide[0:main, :].astype(BF)
        tails[r * rest : r * rest + rest, :] = wide[main:cells, :]
    at = regions * main
    packed[at : at + tails.shape[0], :] = tails[...].astype(BF)
    at += tails.shape[0]
    packed[at : at + 16, :] = note.astype(BF)
    notes[...] = note.astype(BF)


def packed_rows(side, regions):
    cells = side * side
    return regions * (cells // 16 * 16), roundup(regions * (cells % 16), 16)


def pack(cotangent, tile, height, width, place):
    side, regions = cotangent.shape[0], cotangent.shape[2]
    return local_kernel(
        functools.partial(pack_kernel, side, height, width),
        (
            sds((sum(packed_rows(side, regions)) + 16, 256), BF),
            sds((16, 256), BF),
            sds((width, 256), BF),
        ),
        cotangent,
        *place,
        tile,
        scratch=[
            pltpu.VMEM((side, side, regions, 256), BF),
            pltpu.VMEM((side * side * regions, 128), F32),
            pltpu.VMEM((side * side * regions, 128), F32),
            pltpu.VMEM((side * side, 256), F32),
            pltpu.VMEM((packed_rows(side, regions)[1], 256), F32),
            pltpu.SMEM((3, 1, regions), jnp.int32),
            pltpu.SemaphoreType.DMA((6,)),
        ],
        hbm=(0, 1, 2, 3, 4),
    )


def shifted(v, width):
    col = lax.broadcasted_iota(jnp.int32, (width, 256), 0)
    left = jnp.where(col == 0, 0.0, pltpu.roll(v, 1, 0)).astype(BF)
    right = jnp.where(col == width - 1, 0.0, pltpu.roll(v, width - 1, 0)).astype(BF)
    return left, v.astype(BF), right


def pyramid_part(height, width, own, other, wf, pyr, xp, fetched):
    core = lax.rem(lax.axis_index("tile"), 2)
    cells = height * width

    def fill(src, where):
        def step(t, carry):
            v = src[pl.ds(pl.multiple_of(t * width, width), width), :].astype(F32)
            to = pl.ds(pl.multiple_of(where + t * width, width), width)
            for b, piece in enumerate(shifted(v, width)):
                xp[to, b * 256 : b * 256 + 256] = piece
            return carry

        lax.fori_loop(0, height, step, 0)

    bottom = width + 2 * cells
    fill(own, width + core * cells)
    fill(other, width + (1 - core) * cells)
    xp[0:width, :] = jnp.zeros((width, 768), BF)
    xp[bottom : bottom + width, :] = jnp.zeros((width, 768), BF)
    fetched.wait()

    def conv(t, carry):
        at = t * 512
        total = jnp.zeros((512, 256), F32)
        for a in range(3):
            piece = xp[pl.ds(pl.multiple_of(at + a * width, 64), 512), :]
            total += jnp.dot(piece, wf[a * 768 : a * 768 + 768, :], preferred_element_type=F32)
        cell = at + lax.broadcasted_iota(jnp.int32, (512, 256), 0)
        open_row = (cell < width) | (cell >= 2 * cells - width)
        pyr[pl.ds(pl.multiple_of(at, 512), 512), :] = jnp.where(
            open_row, total, total.astype(BF).astype(F32)
        )
        return carry

    lax.fori_loop(0, 2 * cells // 512, conv, 0)
    pyr[2 * cells : 2 * cells + 16, :] = jnp.zeros((16, 256), F32)


def edges_part(height, width, rim_a, rim_b, wf, pyr):
    core = lax.rem(lax.axis_index("tile"), 2)
    last = 2 * height * width - width

    def close(rim, at, tap):
        total = pyr[at : at + width, :]
        for b, piece in enumerate(shifted(rim[...].astype(F32), width)):
            k = 3 * tap + b
            total += jnp.dot(piece, wf[k * 256 : k * 256 + 256, :], preferred_element_type=F32)
        pyr[at : at + width, :] = total.astype(BF).astype(F32)

    @pl.when(core == 0)
    def _():
        close(rim_a, 0, 0)
        close(rim_b, last, 2)

    @pl.when(core == 1)
    def _():
        close(rim_b, 0, 0)
        close(rim_a, last, 2)


def flip_part(w, wb):
    for k in range(9):
        block = w[(8 - k) * 256 : (9 - k) * 256, :].astype(F32)
        wb[k * 256 : k * 256 + 256, :] = block.T.astype(BF)


def gelu_pair(v):
    c = math.sqrt(2.0 / math.pi)
    sq = v * v
    t = jnp.tanh(c * (v + 0.044715 * (sq * v)))
    half = 0.5 * (1.0 + t)
    slope = half + 0.5 * v * (1.0 - t * t) * (c * (1.0 + 3 * 0.044715 * sq))
    return v * half, slope


def regions_part(side, height, width, per, plan, blocks, early, stash, tables, sums, scratch):
    pyr, wb1, wb2, w1, w2 = tables
    acc1, acc2, gp = sums
    xs, hs, gs, wide, vs, slope1, todo = scratch
    chip = lax.axis_index("tile") // 2
    lanes = lax.broadcasted_iota(jnp.int32, (16, 256), 1)
    rows16 = lax.broadcasted_iota(jnp.int32, (16, 256), 0)
    in_row = rows16 < side
    cells = side * PITCH
    inside = (lax.broadcasted_iota(jnp.int32, (cells, 256), 0) & (PITCH - 1)) < side
    used = pl.ds(16, cells)
    main, tails = packed_rows(side, per)
    one = main // per
    rest = side * side - one

    count = jnp.int32(0)
    start, end = jnp.int32(0), jnp.int32(0)

    def enlist(count, s, r, note, wanted=None):
        note = jnp.where(rows16 == r, note.astype(F32), 0.0)
        spot = jnp.sum(jnp.where(lanes == 0, note, 0.0)).astype(jnp.int32) - 1
        column = jnp.sum(jnp.where(lanes == 1, note, 0.0)).astype(jnp.int32)
        local = spot - chip * 2 * height
        here = (spot >= 0) & (local >= 0) & (local < 2 * height)
        if wanted is not None:
            outer = (local == 0) | (local == 2 * height - side)
            here = here & (outer == wanted)
        todo[0, count] = jnp.int32(s * per + r)
        todo[1, count] = jnp.where(here, local * width + column // 8 * 8, 0)
        todo[2, count] = jnp.where(here, lax.rem(column, 8), 0)
        return count + here.astype(jnp.int32)

    def scan(s, wanted):
        note = blocks[s][main + tails : main + tails + 16, :]
        found = count
        for r in range(per):
            found = enlist(found, s, r, note, wanted)
        return found

    for s, most in enumerate(plan[: len(blocks)]):
        if s == 1:
            count = scan(0, True)
        count = scan(s, False if s == 0 and len(plan) > 1 else None)
        start, end = end, count if most is None else jnp.minimum(count, end + most)
    total = count
    for note in early:
        for r in range(per):
            count = enlist(count, len(blocks), r, note[...])

    for buf in (xs, hs, gs):
        buf[0:16, :] = jnp.zeros((16, 768), BF)
        buf[cells + 16 : cells + 32, :] = jnp.zeros((16, 768), BF)

    def put(buf, v):
        buf[used, 0:256] = pltpu.roll(v, 1, 0).astype(BF)
        buf[used, 256:512] = v.astype(BF)
        buf[used, 512:768] = pltpu.roll(v, cells - 1, 0).astype(BF)

    def conv(buf, w):
        total = jnp.zeros((cells, 256), F32)
        for a in range(3):
            total += jnp.dot(
                buf[a * 16 : a * 16 + cells, :],
                w[a * 768 : a * 768 + 768, :],
                preferred_element_type=F32,
            )
        return total

    def taps(acc, buf, grad):
        turned = grad.T.astype(BF)
        for a in range(3):
            acc[:, a * 768 : a * 768 + 768] += jnp.dot(
                turned, buf[a * 16 : a * 16 + cells, :], preferred_element_type=F32
            )

    def crop(n):
        base, lead = todo[1, n], todo[2, n]
        for i in range(side):
            got = pyr[pl.ds(pl.multiple_of(base + i * width, 8), 24), :]
            got = pltpu.roll(got, lax.rem(24 - lead, 24), 0)[0:16]
            vs[i * 16 : i * 16 + 16, :] = jnp.where(in_row, got, 0.0)
        put(xs, vs[...])

    def forward(n):
        crop(n)
        act1, slope = gelu_pair(conv(xs, w1))
        slope1[...] = slope
        act1 = jnp.where(inside, act1, 0.0)
        put(hs, act1)
        _, slope = gelu_pair(conv(hs, w2))
        return act1, slope

    def backward(n, slope2):
        which = todo[0, n]
        base, lead = todo[1, n], todo[2, n]
        for s, block in enumerate(blocks):

            @pl.when(which // per == s)
            def _(block=block):
                r = lax.rem(which, per)
                cell = pl.ds(pl.multiple_of(r * one, 16), one)
                wide[0:one, :] = block[cell, :].astype(F32)
                left = block[main : main + tails, :].astype(F32)
                wide[one : one + tails, :] = pltpu.roll(left, lax.rem(tails - r * rest, tails), 0)

        for i in range(side):
            got = wide[i * side : i * side + 16, :]
            vs[i * 16 : i * 16 + 16, :] = jnp.where(in_row, got, 0.0)
        g2 = vs[...] * slope2
        put(gs, g2)
        taps(acc2, hs, g2)
        g1 = jnp.where(inside, conv(gs, wb2) * slope1[...], 0.0)
        put(gs, g1)
        taps(acc1, xs, g1)
        vs[...] = jnp.where(inside, conv(gs, wb1), 0.0).astype(BF).astype(F32)
        for i in range(side):
            at = pl.ds(pl.multiple_of(base + i * width, 8), 24)
            piece = jnp.concatenate([vs[i * 16 : i * 16 + 16, :], jnp.zeros((8, 256), F32)])
            gp[at, :] = gp[at, :] + pltpu.roll(piece, lead, 0)

    def whole(n, carry):
        _, slope2 = forward(n)
        backward(n, slope2)
        return carry

    def ahead(n, carry):
        r = lax.rem(todo[0, n], per)
        act1, slope2 = forward(n)
        stash[0][r] = act1.astype(BF)
        stash[1][r] = slope1[...]
        stash[2][r] = slope2
        return carry

    def behind(n, carry):
        r = lax.rem(todo[0, n], per)
        crop(n)
        put(hs, stash[0][r].astype(F32))
        slope1[...] = stash[1][r]
        backward(n, stash[2][r])
        return carry

    if early:
        lax.fori_loop(start, end, whole, 0)
        lax.fori_loop(total, count, ahead, 0)
    elif stash:
        lax.fori_loop(0, total, behind, 0)
    else:
        lax.fori_loop(start, end, whole, 0)


def chunks_of(rows):
    return ((0, rows),)


def finish_part(height, width, dp, chips, acc1, acc2, gp, keep, sends, gp_own, gp_other):
    core = lax.rem(lax.axis_index("tile"), 2)
    cells = height * width
    rows = 2304 // dp
    parts = chunks_of(rows)

    def write_keep(acc):
        for k in range(9):
            keep[k * 256 : k * 256 + 256, :] = acc[:, k * 256 : k * 256 + 256].T.astype(BF)

    def write_sends(acc):
        for k in range(9):
            value = acc[:, k * 256 : k * 256 + 256].T.astype(BF)
            for d in range(dp):
                for to, (lo, hi) in zip(sends, parts):
                    first = max(d * rows + lo, k * 256)
                    end = min(d * rows + hi, k * 256 + 256)
                    if first < end:
                        at = d * (hi - lo) + first - d * rows - lo
                        to[at : at + end - first, :] = value[first - k * 256 : end - k * 256, :]

    @pl.when(core == 0)
    def _():
        write_sends(acc2)
        write_keep(acc1)

    @pl.when(core == 1)
    def _():
        write_sends(acc1)
        write_keep(acc2)

    gp_own[...] = gp[pl.ds(pl.multiple_of(core * cells, cells), cells), :]
    gp_other[...] = gp[pl.ds(pl.multiple_of((1 - core) * cells, cells), cells), :].astype(BF)


def main_call(side, height, width, per, dp, chips, first, last, plan, state, weights, rims, blocks, early, stash):
    n = len(blocks)
    big = 2 * height * width + 16
    cells = side * PITCH
    kept = (sds((big, 256), F32),) + (sds((2304, 256), BF),) * 5
    sums = (sds((256, 2304), F32), sds((256, 2304), F32), sds((big, 256), F32))
    ends = (
        sds((2304, 256), BF),
        *(sds((dp * (hi - lo), 256), BF) for lo, hi in chunks_of(2304 // dp)),
        sds((height * width, 256), F32),
        sds((height * width, 256), BF),
    )
    stashed = (
        sds((per, cells, 256), BF),
        sds((per, cells, 256), F32),
        sds((per, cells, 256), F32),
    )
    outs = (kept if first else kept[:1] if rims else ()) + sums + (ends if last else ()) + (stashed if early else ())
    scratch = [
        pltpu.VMEM((cells + 32, 768), BF),
        pltpu.VMEM((cells + 32, 768), BF),
        pltpu.VMEM((cells + 32, 768), BF),
        pltpu.VMEM((side * side // 16 * 16 + packed_rows(side, per)[1], 256), F32),
        pltpu.VMEM((cells, 256), F32),
        pltpu.VMEM((cells, 256), F32),
        pltpu.SMEM((3, 256), jnp.int32),
    ]
    extra = []
    if first:
        extra = [
            pltpu.VMEM(((2 * height + 2) * width, 768), BF),
            pltpu.VMEM((height * width, 256), BF),
            pltpu.SemaphoreType.DMA((4,)),
        ]

    def kernel(*refs):
        refs = list(refs)

        def take(k):
            got = refs[:k]
            del refs[:k]
            return got

        state_refs = take(len(state))
        weight_refs = take(len(weights))
        rim_refs = take(len(rims))
        block_refs = take(n)
        early_refs = take(len(early))
        stash_refs = take(len(stash))
        out_refs = take(len(outs))
        if early:
            stash_refs = out_refs[-3:]
        scratch_refs = take(len(scratch))
        if first:
            pyr, wb1, wb2, w1, w2, wf = out_refs[:6]
            acc1, acc2, gp = out_refs[6:9]
            xp, own, sems = refs
            copies = [
                pltpu.make_async_copy(source, to, sems.at[k])
                for k, (source, to) in enumerate(zip((state_refs[0], *weight_refs), (own, wf, w1, w2)))
            ]
            for copy in copies:
                copy.start()
            for total in (acc1, acc2, gp):
                total[...] = jnp.zeros(total.shape, F32)
            copies[0].wait()
            pyramid_part(height, width, own, state_refs[1], wf, pyr, xp, copies[1])
            copies[2].wait()
            flip_part(w1, wb1)
            copies[3].wait()
            flip_part(w2, wb2)
        else:
            pyr, wb1, wb2, w1, w2, wf = state_refs[:6]
            shared = list(out_refs)
            if rims:
                pyr = shared.pop(0)
                edges_part(height, width, *rim_refs, wf, pyr)
            acc1, acc2, gp = shared[:3]
        if n:
            regions_part(
                *(side, height, width, per, plan, block_refs, early_refs, stash_refs),
                *((pyr, wb1, wb2, w1, w2), (acc1, acc2, gp), scratch_refs),
            )
        if last:
            keep, *sends, gp_own, gp_other = out_refs[3:]
            finish_part(height, width, dp, chips, acc1, acc2, gp, keep, sends, gp_own, gp_other)

    aliases = {} if first else {6: 0, 7: 1, 8: 2}
    if rims:
        aliases = {0: 0, 6: 1, 7: 2, 8: 3}
    return run(
        kernel,
        outs,
        [*state, *weights, *rims, *blocks, *early, *stash],
        scratch=scratch + extra,
        aliases=aliases,
        hbm=(0, *range(len(state), len(state) + len(weights))) if first else (),
    )


def local_kernel(fn, outs, *arrays, **more):
    if isinstance(outs, tuple):
        return run(fn, outs, arrays, **more)
    return run(fn, (outs,), arrays, **more)[0]


def add(a, b):
    return (a.astype(F32) + b.astype(F32)).astype(BF)


def reduce_weights(keep, sends, core_swap, dp, chips, beside, gp_other):
    rows = keep.shape[0] // dp
    bits = dp.bit_length() - 1
    orders = (list(range(bits)), list(reversed(range(bits))))
    shifts = [
        [(2 * z + c, 2 * ((z + k) % chips) + c) for z in range(chips) for c in range(2)]
        for k in range(chips)
    ]
    arrived = [lax.ppermute(send, "tile", core_swap) for send in sends]

    def split(members, bit):
        return [m for m in members if not m & bit], [m for m in members if m & bit]

    class Chunk:
        pass

    def begin(lo, hi, got):
        c = Chunk()
        c.rows = hi - lo
        low = roundup(c.rows // 2, 16)
        c.spans = ((0, low), (low, c.rows))
        c.members = [list(range(dp)), list(range(dp))]

        def first(keep_ref, got_ref, *outs):
            me = lax.axis_index("dp")
            for half in range(2):
                start, size = c.spans[half][0], c.spans[half][1] - c.spans[half][0]
                groups = split(c.members[half], 1 << orders[half][0])
                for out, group in zip(outs[2 * half : 2 * half + 2], groups):
                    for n, m in enumerate(group):
                        a = pl.ds(pl.multiple_of((me ^ m) * rows + lo + start, 16), size)
                        b = pl.ds(pl.multiple_of((me ^ m) * c.rows + start, 16), size)
                        out[n] = add(keep_ref[a, :], got_ref[b, :])

        shapes = []
        for half in range(2):
            shapes += [sds((dp // 2, c.spans[half][1] - c.spans[half][0], 256), BF)] * 2
        c.parts = local_kernel(first, tuple(shapes), keep, got)
        return c

    def exchange(c, stage):
        c.received = []
        for half in range(2):
            bit = 1 << orders[half][stage]
            pairs = [(i, i ^ bit) for i in range(dp)]
            c.received.append(lax.ppermute(c.parts[2 * half + 1], "dp", pairs))
            c.members[half] = split(c.members[half], bit)[0]

    def halve(c, stage):
        shapes = []
        for half in range(2):
            size = c.spans[half][1] - c.spans[half][0]
            shapes += [sds((len(c.members[half]) // 2, size, 256), BF)] * 2
        members = [list(m) for m in c.members]

        def kernel(p, pr, q, qr, *outs):
            for half, (mine, theirs) in enumerate(((p, pr), (q, qr))):
                groups = split(members[half], 1 << orders[half][stage])
                for out, group in zip(outs[2 * half : 2 * half + 2], groups):
                    for n, m in enumerate(group):
                        k = members[half].index(m)
                        out[n] = add(mine[k], theirs[k])

        c.parts = local_kernel(
            kernel, tuple(shapes), c.parts[0], c.received[0], c.parts[2], c.received[1]
        )

    def deal(c):
        c.share = roundup(-(-c.rows // chips), 16)
        low = c.spans[0][1]

        def kernel(p, pr, q, qr, *refs):
            outs, total = refs[:chips], refs[chips]
            chip = lax.axis_index("tile") // 2
            total[0:low, :] = add(p[0], pr[0])
            total[low : c.rows, :] = add(q[0], qr[0])
            if c.share * chips > c.rows:
                total[c.rows :, :] = jnp.zeros((c.share * chips - c.rows, 256), BF)
            for k in range(chips):
                to = lax.rem(chip + k, chips)
                outs[k][...] = total[pl.ds(pl.multiple_of(to * c.share, 16), c.share), :]

        dealt = local_kernel(
            kernel,
            tuple(sds((c.share, 256), BF) for _ in range(chips)),
            *(c.parts[0], c.received[0], c.parts[2], c.received[1]),
            scratch=[pltpu.VMEM((c.share * chips, 256), BF)],
        )
        c.mine = dealt[0]
        c.others = [lax.ppermute(dealt[k], "tile", shifts[k]) for k in range(1, chips)]

    def gather(c):
        def kernel(*refs):
            total = refs[0][...].astype(F32)
            for ref in refs[1:-1]:
                total += ref[...].astype(F32)
            refs[-1][...] = total.astype(BF)

        c.mine = local_kernel(kernel, sds((c.share, 256), BF), c.mine, *c.others)
        c.others = [lax.ppermute(c.mine, "tile", shifts[k]) for k in range(1, chips)]

    def lay(c):
        def kernel(*refs):
            chip = lax.axis_index("tile") // 2
            for k in range(chips):
                source = lax.rem(chip - k + chips, chips)
                refs[-1][pl.ds(pl.multiple_of(source * c.share, 16), c.share), :] = refs[k][...]

        c.whole = local_kernel(kernel, sds((c.share * chips, 256), BF), c.mine, *c.others)
        c.theirs = lax.ppermute(c.whole, "tile", core_swap)

    spans = chunks_of(rows)
    chunks = [begin(lo, hi, got) for (lo, hi), got in zip(spans, arrived)]
    chunks[0].parts = list(chunks[0].parts)
    chunks[0].parts[1], gp_other = lax.optimization_barrier((chunks[0].parts[1], gp_other))
    for c in chunks:
        exchange(c, 0)
    beside = beside(gp_other)
    chunks[0].received[0], beside = lax.optimization_barrier((chunks[0].received[0], beside))
    for stage in range(1, bits):
        for c in chunks:
            halve(c, stage)
            exchange(c, stage)
    for step in (deal, gather, lay):
        for c in chunks:
            step(c)

    def out(*refs):
        core = lax.rem(lax.axis_index("tile"), 2)
        one, two = refs[-2:]

        def write(to, sources):
            for (lo, hi), source in zip(spans, sources):
                to[lo:hi, :] = source[0 : hi - lo, :].astype(F32)

        @pl.when(core == 0)
        def _():
            write(one, refs[0 : len(spans)])
            write(two, refs[len(spans) : -2])

        @pl.when(core == 1)
        def _():
            write(one, refs[len(spans) : -2])
            write(two, refs[0 : len(spans)])

    one, two = local_kernel(
        out,
        (sds((rows, 256), F32), sds((rows, 256), F32)),
        *(c.whole for c in chunks),
        *(c.theirs for c in chunks),
        hbm_out=(0, 1),
    )
    return one, two, beside


def body(features, fpn_weight, mask_w1, mask_w2, owner, row_off, col_off, cotangent):
    tiles = lax.axis_size("tile")
    dp = lax.axis_size("dp")
    chips = tiles // 2
    height, width, channels = features.shape[1:]
    side = cotangent.shape[2]
    swap = [(i, i ^ 1) for i in range(tiles)]

    tile = features.reshape(height * width, channels)
    regions = cotangent.shape[1]
    place = [x.reshape(1, regions) for x in (owner, row_off, col_off)]
    other = lax.ppermute(tile, "tile", swap)
    packed, notes, edge = pack(cotangent[0].transpose(1, 2, 0, 3), tile, height, width, place)

    order = [0] + list(range(1, chips, 2)) + list(range(2, chips, 2))[::-1]
    ring = [
        (2 * z + c, 2 * order[(k + 1) % chips] + c) for k, z in enumerate(order) for c in range(2)
    ]

    flat = lambda w: w.reshape(9 * channels, channels)
    wf, w1, w2 = flat(fpn_weight), flat(mask_w1), flat(mask_w2)
    block = lax.ppermute(packed, "tile", ring)
    sizes = (side, height, width, regions, dp, chips)
    rim_a = lax.ppermute(
        edge, "tile", [(i, i + 1 if i % 2 else i - 1) for i in range(1, tiles - 1)]
    )
    plan = [1] + [3] * (chips - 3) + [None]
    start = main_call(
        *(*sizes, True, False, plan, [tile, other], [wf, w1, w2], [], [packed], [], [])
    )
    kept, sums, held = list(start[:6]), list(start[6:]), [packed]
    notes, kept[0] = lax.optimization_barrier((notes, kept[0]))
    notes = lax.ppermute(notes, "tile", [(j, i) for i, j in ring])
    for step in range(1, chips):
        state = kept + sums
        if step == chips - 1:
            got = main_call(*sizes, False, True, [None], state, [], [], [block], [], stash)
            ends = got[3:]
            break
        block, state[0], state[-1] = lax.optimization_barrier((block, state[0], state[-1]))
        if step == 1:
            block, rim_a = lax.optimization_barrier((block, rim_a))
        if step == chips - 2:
            block, notes = lax.optimization_barrier((block, notes))
        held = held + [block]
        block = lax.ppermute(block, "tile", ring)
        if step == 1:
            rim_b = lax.ppermute(rim_a, "tile", swap)
        early = [notes] if step == chips - 2 else []
        rims = [rim_a, rim_b] if step == 1 else []
        got = list(main_call(*sizes, False, False, plan, state, [], rims, held, early, []))
        if rims:
            kept[0] = got.pop(0)
        sums, stash = got[:3], got[3:]
    keep, *sends, gp_own, gp_other = ends

    def join(a, b, out):
        out[...] = (a[...] + b[...].astype(F32)).astype(BF)

    def joined(gp_other):
        gp_got = lax.ppermute(gp_other, "tile", swap)
        return local_kernel(
            join, sds((height * width, channels), BF), gp_own, gp_got, hbm_out=(0,)
        )

    grad_one, grad_two, grad_pyramid = reduce_weights(
        keep, sends, swap, dp, chips, joined, gp_other
    )
    return grad_one, grad_two, grad_pyramid.reshape(1, height, width, channels)


def solution(mesh):
    placed = (
        P("dp", "tile", None, None),
        P(),
        P(),
        P(),
        P("dp", "tile", None),
        P("dp", "tile"),
        P("dp", "tile"),
        P("dp", "tile", None, None, None),
    )
    return jax.shard_map(
        body,
        mesh=mesh,
        in_specs=placed,
        out_specs=(P("dp", None), P("dp", None), P("dp", "tile", None, None)),
        check_vma=False,
    )
```
